128 devices in a mesh: cube: 4 (over y_lo, core), row: 8 (over z, y_hi), col: 4 (over x).
Axes of the slice: x: 4, y: 4 (y_hi: 2, y_lo: 2; y = y_hi * 2 + y_lo), z: 4, core: 2. Of those that a mesh axis runs over, the one named last changes fastest.
Arguments:
- child_front: float32 [4, 32768, 2048], P('cube', 'row', 'col'), as said below
- child_pattern: int32 [4, 128, 4], P('cube'), may hold values 0 or 1
- block_map: int32 [4, 128], replicated, may hold values from -1 to 127, as said below
- parent_front: float32 [32768, 1024], P(('cube', 'row'), 'col'), as said below
- parent_pattern: int32 [128, 2], replicated, may hold values 0 or 1
Outputs:
- child_out: float32 [4, 32768, 2048], P('cube', 'row', 'col')
- parent_out: float32 [32768, 1024], P(('cube', 'row'), 'col')
The draws below stay inside these ranges and needn't reach their ends.
Inputs may be any that keep to these rules, and one draw needn't show every extreme that they name: `block_map`: entries for child block rows b < 8 are -1; for each child the other entries are distinct parent block rows. Parent block row p is held by index p % (32) of cube+row. Of the block rows that one device of a child holds, at most 4 go to holders with one cube index, with distinct values of p // 32, and at most 1 go to any one holder. `child_front`: each entry on the diagonal of the first (8) * 256 front rows is raised by 3.5 to 7 times sqrt(2048). `parent_front`: each entry on the diagonal of the first 1024 front rows is raised by 9 to 18 times sqrt(1024).
All inputs are finite; a program needn't handle non-finite values. No bound on the sum of `child_pattern` on one device may be relied on, other than what follows from the above.
Results may differ from the reference program's by a relative error of at most 0.0001.
Values sent between devices are 32-bit elements; how exact they have to be, the bound alone decides.
No kernel may reach another device: no remote copies, remote signals or barrier semaphores. Data moves between devices by JAX's collectives and lax.ppermute only.
A program may use at most 128 MiB of HBM per device.

```python
import math
import jax
import jax.numpy as jnp
from jax import lax

NB = 256
K = 4
S = 4
KP = 2
RBD = 16
NBLK = 128
N_CUBE = 4
N_ROW = 8
N_COL = 4


def front_order(count, parts, local):
    position = jnp.arange(count)
    part_index = position // (local * NB)
    inner_block = position // NB % local
    return (inner_block * parts + part_index) * NB + position % NB


def diagonal_boost(key, leading, row_order, col_order, square, low, high):
    factors = jnp.exp(jax.random.uniform(key, (leading, square), jnp.float32, math.log(low), math.log(high)))
    picked = factors[:, jnp.minimum(row_order, square - 1)]
    on_diagonal = (row_order[:, None] == col_order[None, :]) & (row_order[:, None] < square)
    return jnp.where(on_diagonal[None], picked[:, :, None] * math.sqrt(square), 0.0)


def leading_offset(row_order, square):
    return jnp.where(row_order < square, 1.0, 0.0).astype(jnp.float32)


def draw_child_front(key, part):
    key = jax.random.fold_in(key, 11)
    entry_key, boost_key = jax.random.split(key)
    rows_total = RBD * N_ROW * NB
    cols_total = (K + S) * NB
    full_shape = (N_CUBE, rows_total, cols_total)
    entries = jax.random.normal(entry_key, full_shape, jnp.float32)
    row_order = front_order(rows_total, N_ROW, RBD)
    col_order = front_order(cols_total, N_COL, (K + S) // N_COL)
    offset = leading_offset(row_order, cols_total)[None, :, None]
    return entries + offset + diagonal_boost(boost_key, N_CUBE, row_order, col_order, cols_total, 3.5, 7.0)


def draw_parent_front(key, part):
    key = jax.random.fold_in(key, 17)
    entry_key, boost_key = jax.random.split(key)
    rows_total = RBD * N_ROW * NB
    cols_total = S * NB
    full_shape = (rows_total, cols_total)
    entries = jax.random.normal(entry_key, full_shape, jnp.float32)
    row_order = front_order(rows_total, N_CUBE * N_ROW, RBD // N_CUBE)
    col_order = front_order(cols_total, N_COL, S // N_COL)
    offset = leading_offset(row_order, cols_total)[:, None]
    return entries + offset + diagonal_boost(boost_key, 1, row_order, col_order, cols_total, 9.0, 18.0)[0]


def draw_block_map(key, part):
    key = jax.random.fold_in(key, 23)
    holders = N_CUBE * N_ROW
    per_cube = RBD // N_CUBE
    spread = max(per_cube, N_ROW)
    order_keys = jax.random.split(jax.random.fold_in(key, 1), N_CUBE)
    orders = jax.vmap(lambda subkey: jax.random.permutation(subkey, RBD))(order_keys)
    shift_keys = jax.random.split(jax.random.fold_in(key, 2), N_CUBE * N_CUBE)
    shifts = jax.vmap(lambda subkey: jax.random.permutation(subkey, spread))(shift_keys)
    shifts = shifts.reshape(N_CUBE, N_CUBE, spread)[:, :, :per_cube] % N_ROW
    target_cube = orders % N_CUBE
    parent_slot = orders // N_CUBE
    offset = jnp.take_along_axis(shifts.reshape(N_CUBE, N_CUBE * per_cube), target_cube * per_cube + parent_slot, axis=1)
    row_index = jnp.arange(N_ROW)
    owner = target_cube[:, :, None] * N_ROW + (row_index[None, None, :] + offset[:, :, None]) % N_ROW
    parent_block = parent_slot[:, :, None] * holders + owner
    block_index = jnp.arange(RBD)[:, None] * N_ROW + row_index[None, :]
    result = jnp.where(block_index[None] >= K + S, parent_block, -1)
    return result.reshape(N_CUBE, RBD * N_ROW).astype(jnp.int32)


def plant(values, own_key, smallest, high):
    longest = values.shape.index(max(values.shape))
    spots = []
    for shift in (0, 1):
        where = [jax.random.randint(jax.random.fold_in(own_key, axis), (), 0, length) for axis, length in enumerate(values.shape)]
        where[longest] = (where[longest] + shift) % values.shape[longest]
        spots.append(tuple(where))
    return values.at[spots[0]].set(smallest).at[spots[1]].set(high)


def setup_inputs(seed: int = 0) -> dict:
    splits = jax.random.split(jax.random.key(seed), 6)
    return {
        "child_front": draw_child_front(jax.random.fold_in(splits[5], 71), 0),
        "child_pattern": plant((jax.random.randint(splits[1], (N_CUBE, NBLK, K), 0, 4) < 3).astype(jnp.int32), jax.random.fold_in(splits[1], 1), 0, 1),
        "block_map": draw_block_map(jax.random.fold_in(splits[5], 71), 0),
        "parent_front": draw_parent_front(jax.random.fold_in(splits[5], 71), 0),
        "parent_pattern": plant((jax.random.randint(splits[4], (NBLK, KP), 0, 4) < 3).astype(jnp.int32), jax.random.fold_in(splits[4], 1), 0, 1),
    }


def to_front(matrix, row_parts, row_local, col_parts, col_local):
    rows_total, cols_total = matrix.shape
    shaped = matrix.reshape(row_parts, row_local, NB, col_parts, col_local, NB)
    return shaped.transpose(1, 0, 2, 4, 3, 5).reshape(rows_total, cols_total)

def to_storage(matrix, row_parts, row_local, col_parts, col_local):
    rows_total, cols_total = matrix.shape
    shaped = matrix.reshape(row_local, row_parts, NB, col_local, col_parts, NB)
    return shaped.transpose(1, 0, 2, 4, 3, 5).reshape(rows_total, cols_total)

def factor_steps(matrix, pattern, count):
    rows_total, cols_total = matrix.shape
    block_of_row = jnp.arange(rows_total) // NB
    for step_index in range(count):
        first_col = step_index * NB
        panel_rows = matrix[:, first_col:first_col + NB]
        diagonal = panel_rows[first_col:first_col + NB]
        symmetric = jnp.tril(diagonal) + jnp.tril(diagonal, -1).T
        factor = jnp.linalg.cholesky(symmetric)
        inverse = jax.scipy.linalg.solve_triangular(factor, jnp.eye(NB, dtype=matrix.dtype), lower=True)
        solved = jnp.dot(panel_rows, inverse.T, precision=lax.Precision.HIGHEST)
        kept_rows = pattern[:, step_index][block_of_row] != 0
        column = jnp.where(((block_of_row > step_index) & kept_rows)[:, None], solved, jnp.zeros_like(solved))
        column = column.at[first_col:first_col + NB].set(factor)
        matrix = matrix.at[:, first_col:first_col + NB].set(column)
        lower_part = jnp.where((block_of_row > step_index)[:, None], column, jnp.zeros_like(column))
        crossing = column[first_col + NB:cols_total]
        update = jnp.dot(lower_part, crossing.T, precision=lax.Precision.HIGHEST)
        matrix = matrix.at[:, first_col + NB:].add(-update)
    return matrix

def reference(child_front, child_pattern, block_map, parent_front, parent_pattern):
    child_cols = (K + S) // N_COL
    parent_parts = N_CUBE * N_ROW
    parent_rows = RBD // N_CUBE
    parent = to_front(parent_front, parent_parts, parent_rows, N_COL, S // N_COL)
    results = []
    for child_index in range(N_CUBE):
        matrix = to_front(child_front[child_index], N_ROW, RBD, N_COL, child_cols)
        matrix = factor_steps(matrix, child_pattern[child_index], K)
        results.append(to_storage(matrix, N_ROW, RBD, N_COL, child_cols))
        schur_part = matrix[(K + S) * NB:, K * NB:].reshape(-1, NB, S * NB)
        targets = block_map[child_index, K + S:]
        parent = parent.reshape(-1, NB, S * NB).at[targets].add(schur_part).reshape(-1, S * NB)
    parent = factor_steps(parent, parent_pattern, KP)
    return (jnp.stack(results), to_storage(parent, parent_parts, parent_rows, N_COL, S // N_COL))
```

```python
import functools

import jax
import jax.numpy as jnp
from jax import lax
from jax.experimental import pallas as pl
from jax.experimental.pallas import tpu as pltpu
from jax.sharding import PartitionSpec as P

NB = 256
K = 4
KP = 2
PB = 32

f32, bf16 = jnp.float32, jnp.bfloat16


def dims(a, b):
    return (((a,), (b,)), ((), ()))


NN, NT, TN = dims(1, 0), dims(1, 1), dims(0, 0)


def split(x):
    high = x.astype(bf16)
    return high, (x - high.astype(f32)).astype(bf16)


def dot3(x, y, d):
    xh, xl = x
    yh, yl = y
    part = lambda p, q: lax.dot_general(p, q, d, preferred_element_type=f32)
    return part(xh, yh) + (part(xh, yl) + part(xl, yh))


def small_factor(t):
    tiles = [t[8 * i : 8 * i + 8] for i in range(4)]
    full = (8, 128)
    sub = lax.broadcasted_iota(jnp.int32, full, 0)
    for s in range(4):
        c0 = PB + 8 * s
        cols = [
            [jnp.broadcast_to(tiles[q][:, c0 + k : c0 + k + 1], full) for k in range(8)]
            for q in range(s, 4)
        ]
        a = [
            [jnp.broadcast_to(cols[0][k][i : i + 1], full) if i >= k else None for k in range(8)]
            for i in range(8)
        ]
        rows = [jnp.broadcast_to(tiles[s][k : k + 1], full) for k in range(8)]
        mults = [[] for _ in range(s, 4)]
        scale = None
        for k in range(8):
            r = 1.0 / a[k][k]
            root = lax.rsqrt(a[k][k])
            scale = root if k == 0 else jnp.where(sub == k, root, scale)
            m = [a[i][k] * r if i > k else None for i in range(8)]
            for q in range(4 - s):
                mult = cols[q][k] * r
                if q == 0:
                    mult = jnp.where(sub > k, mult, 0.0)
                mults[q].append(mult)
            for i in range(k + 1, 8):
                rows[i] = rows[i] - m[i] * rows[k]
                for q in range(4 - s):
                    cols[q][i] = cols[q][i] - mults[q][k] * a[i][k]
                for j in range(k + 1, i + 1):
                    a[i][j] = a[i][j] - m[i] * a[j][k]
        for q in range(4 - s):
            acc = tiles[s + q]
            for k in range(8):
                acc = acc - mults[q][k] * rows[k]
            tiles[s + q] = acc
        tiles[s] = tiles[s] * scale
    return jnp.concatenate(tiles, axis=0)


def factor(block, work, out):
    row = lax.broadcasted_iota(jnp.int32, (NB, NB), 0)
    lane = lax.broadcasted_iota(jnp.int32, (NB, NB), 1)
    low = jnp.where(row >= lane, block, 0.0)
    work[:, :NB] = low + jnp.where(row > lane, block, 0.0).T
    work[:, NB:] = jnp.where(row == lane, 1.0, 0.0)
    lane32 = lax.broadcasted_iota(jnp.int32, (PB, 128), 1)
    row32 = lax.broadcasted_iota(jnp.int32, (PB, 128), 0)
    lane256 = lax.broadcasted_iota(jnp.int32, (PB, NB), 1)

    def body(p, _):
        base = pl.multiple_of(p * PB, PB)
        slab = work[pl.ds(base, PB), :]
        turned = pltpu.roll(slab[:, :NB], jnp.where(p == 0, PB, NB + PB - base), 1)[:, :128]
        unit = jnp.where(lane32 == row32, 1.0, 0.0)
        t = jnp.where((lane32 >= PB) & (lane32 < 2 * PB), turned, unit)
        j = small_factor(t)[:, :PB]
        u = dot3(split(j), split(slab), NN)
        out[pl.ds(base, PB), :] = u
        uh, ul = split(u)
        keep = lane256 >= base + PB
        zero = jnp.zeros((PB, NB), bf16)
        left = (jnp.where(keep, uh[:, :NB], zero), jnp.where(keep, ul[:, :NB], zero))
        work[...] -= dot3(left, (uh, ul), TN)
        return 0

    lax.fori_loop(0, NB // PB, body, 0)
    g = jnp.where(lane >= row, out[:, :NB], 0.0).T
    return g, out[:, NB:]


FACTOR_SCRATCH = [pltpu.VMEM((NB, 2 * NB), f32), pltpu.VMEM((NB, 2 * NB), f32)]


def kept(flag, value):
    return jnp.where(flag != 0, value, 0.0)


def call(kernel, out_shape, us, **kwargs):
    kwargs.setdefault("compiler_params", pltpu.CompilerParams(vmem_limit_bytes=56 << 20))
    return pl.pallas_call(
        kernel,
        out_shape=out_shape,
        cost_estimate=pl.CostEstimate(flops=us * 10**9, bytes_accessed=us * 3 * 10**6, transcendentals=0),
        **kwargs,
    )


VMEM = pl.BlockSpec(memory_space=pltpu.VMEM)
SMEM = pl.BlockSpec(memory_space=pltpu.SMEM)


def block_shape(*lead):
    return jax.ShapeDtypeStruct(lead + (NB, NB), f32)


def whole(ref, index):
    return ref[:, index].reshape(NB, NB)


def first_kernel(pattern, piece, g, h, l, work, out):
    g0, h0 = factor(whole(piece, 0), work, out)
    g[0], h[0] = g0, h0
    l10 = kept(pattern[1, 0], dot3(split(whole(piece, 1)), split(h0), NT))
    l[0] = l10
    s10 = split(l10)
    g[1], h[1] = factor(whole(piece, 2) - dot3(s10, s10, NT), work, out)


def later_kernel(k, pattern, piece, hs, ls, g, h, l, work, out):
    row = [whole(piece, j) for j in range(k + 1)]
    for j in range(k):
        value = split(kept(pattern[k, j], dot3(split(row[j]), split(hs[j]), NT)))
        l[j] = value[0].astype(f32) + value[1].astype(f32)
        for i in range(j + 1, k):
            row[i] = row[i] - dot3(value, split(ls[pair(i, j)]), NT)
        row[k] = row[k] - dot3(value, value, NT)
    g[0], h[0] = factor(row[k], work, out)


def pair(i, j):
    return i * (i - 1) // 2 + j


def solve_rows(columns, mask, h, l):
    solved = []
    columns = list(columns)
    for k in range(len(columns)):
        value = mask(k, dot3(split(columns[k]), h(k), NT))
        solved.append(value)
        value = split(value)
        for j in range(k + 1, len(columns)):
            columns[j] = columns[j] - dot3(value, l(j, k), NT)
    return solved


def weights_kernel(pattern, piece, hs, ls, hh, hl, lh, ll, ch, cl):
    for k in range(K):
        hh[k], hl[k] = split(hs[k])
    for k in range(K * (K - 1) // 2):
        lh[k], ll[k] = split(ls[k])
    columns = [jnp.concatenate([whole(piece, j * K + k) for j in range(K)], axis=0) for k in range(K)]

    def mask(k, value):
        parts = [kept(pattern[K + j, k], value[j * NB : (j + 1) * NB]) for j in range(K)]
        return jnp.concatenate(parts, axis=0)

    solved = solve_rows(
        columns, mask, lambda k: (hh[k], hl[k]), lambda j, k: (lh[pair(j, k)], ll[pair(j, k)])
    )
    for k in range(K):
        ch[:, k * NB : (k + 1) * NB], cl[:, k * NB : (k + 1) * NB] = split(solved[k])


def rows_kernel(lead, groups, octets, info, front, g, hh, hl, lh, ll, ch, cl, *outs):
    step = 0 if lead else pl.program_id(0) * groups
    height = front.shape[2]

    def mask(k, value):
        parts = [
            kept(info[step + i, 1 + k], value[i * height : (i + 1) * height]) for i in range(groups)
        ]
        return jnp.concatenate(parts, axis=0) if groups > 1 else parts[0]

    columns = [front[k, :, :, :NB].reshape(groups * height, NB) for k in range(K)]
    solved = solve_rows(
        columns, mask, lambda k: (hh[k], hl[k]), lambda j, k: (lh[pair(j, k)], ll[pair(j, k)])
    )
    wide = (2 if lead else K) * NB
    high, low = split(jnp.concatenate(solved, axis=1))
    update = dot3((high, low), (ch[:wide], cl[:wide]), NT)
    if lead:
        (top,) = outs
        for v in range(K):
            j, half = v // 2, v % 2
            lanes = slice(half * 128, half * 128 + 128)
            raw = front[j, 0, :, NB + half * 128 : NB + half * 128 + 128]
            top[v] = (raw - update[:, v * 128 : v * 128 + 128]).reshape(octets, 1, 8, 128)
        return
    back, extend = outs
    for k in range(K):
        back[k, :, :, :NB] = solved[k].reshape(groups, height, NB)
        schur = front[k, :, :, NB:].reshape(groups * height, NB) - update[:, k * NB : (k + 1) * NB]
        back[k, :, :, NB:] = schur.reshape(groups, height, NB)
        shaped = schur.reshape(groups, octets, 8, NB)
        for i in range(groups):
            extend[:, i, :, k * NB : (k + 1) * NB] = shaped[i]
        for i in range(groups):

            @pl.when(info[step + i, 0] == k)
            def _():
                back[k, i, :, :NB] = g[k]


def parent_kernel(pattern, top, g, hh, hl, lh, ll, work, out):
    def block(i, j):
        halves = [
            jnp.swapaxes(top[2 * j + v, :, :, i], 0, 1).reshape(NB, 128) for v in range(2)
        ]
        return jnp.concatenate(halves, axis=1)

    g0, h0 = factor(block(0, 0), work, out)
    g[0] = g0
    h0 = split(h0)
    hh[0], hl[0] = h0
    first = []
    for i in range(1, 4):
        value = split(kept(pattern[i, 0], dot3(split(block(i, 0)), h0, NT)))
        lh[i - 1], ll[i - 1] = value
        first.append(value)
    g1, h1 = factor(block(1, 1) - dot3(first[0], first[0], NT), work, out)
    g[1] = g1
    h1 = split(h1)
    hh[1], hl[1] = h1
    for i in range(2, 4):
        rest = block(i, 1) - dot3(first[i - 1], first[0], NT)
        lh[i + 1], ll[i + 1] = split(kept(pattern[i, 1], dot3(split(rest), h1, NT)))


def parent_rows_kernel(info, target, extend, own, g, hh, hl, lh, ll, out, acc):
    slots, members = own.shape[0], own.shape[1]
    acc[...] = own[...]

    def add(q, _):
        for s in range(slots):
            where = target[q, s]

            @pl.when(where >= 0)
            def _():
                acc[s, where] += extend[q, s]

        return 0

    lax.fori_loop(0, extend.shape[0], add, 0)
    columns = [acc[:, :, :, j * NB : (j + 1) * NB].reshape(slots * members * 8, NB) for j in range(4)]

    def mask(k, value):
        parts = [kept(info[i, 1 + k], value[i * 8 : i * 8 + 8]) for i in range(slots * members)]
        return jnp.concatenate(parts, axis=0)

    one = mask(0, dot3(split(columns[0]), (hh[0], hl[0]), NT))
    first = split(one)
    two = mask(1, dot3(split(columns[1] - dot3(first, (lh[0], ll[0]), NT)), (hh[1], hl[1]), NT))
    second = split(two)
    results = [one, two]
    for j in range(2, 4):
        left = dot3(first, (lh[j - 1], ll[j - 1]), NT) + dot3(second, (lh[j + 1], ll[j + 1]), NT)
        results.append(columns[j] - left)
    for j in range(4):
        shaped = results[j].reshape(slots, members, 8, NB)
        for s in range(slots):
            out[:, j, s] = shaped[s]
    for k in range(KP):

        @pl.when(info[k, 0] == k)
        def _():
            out[k, k, 0] = g[k]


def exchange(array, axes):
    return lax.all_to_all(array, axes, split_axis=0, concat_axis=0, tiled=True)


def gather_pieces(pieces, axes, count):
    return exchange(jnp.broadcast_to(pieces[None], (count,) + pieces.shape), axes)


def per_device(child_front, child_pattern, block_map, parent_front, parent_pattern):
    nr, nx, nc = lax.axis_size("row"), lax.axis_size("col"), lax.axis_size("cube")
    r, x, c = lax.axis_index("row"), lax.axis_index("col"), lax.axis_index("cube")
    local = child_front.shape[1] // NB
    slots = parent_front.shape[0] // NB
    height = NB // nx
    octets = height // 8
    holders = nc * nr
    front = child_front[0]
    pattern = child_pattern[0]

    tables = block_map.reshape(nc, local, nr).transpose(0, 2, 1)
    live = tables >= 0
    cubes = jnp.where(live, tables % holders // nr, -1)
    places = jnp.where(live, tables // holders, -1)
    members = jnp.where(live, tables % nr, -1)
    mine = tables[c, r]
    spot = jnp.where(mine >= 0, cubes[c, r] * slots + places[c, r], -1)
    fits = spot[None, :] == jnp.arange(local)[:, None]
    order = jnp.sum(jnp.where(fits, jnp.arange(local)[None, :], 0), axis=1)
    back_order = jnp.sum(
        jnp.where(order[None, :] == jnp.arange(local)[:, None], jnp.arange(local)[None, :], 0), axis=1
    )
    block_row = order * nr + r
    row_info = jnp.concatenate(
        [
            block_row[:, None],
            jnp.where(block_row[:, None] > jnp.arange(K)[None], jnp.take(pattern, block_row, axis=0, mode="clip"), 0),
        ],
        axis=1,
    ).astype(jnp.int32)

    corner = front[:NB, :NB].reshape(nr * nx, 1, 8, NB)
    pieces = exchange(corner, ("row", "col"))[:, 0]
    line = lambda i: pieces[i * nx : i * nx + i + 1]
    part_one = gather_pieces(jnp.concatenate([line(0), line(1)], axis=0), ("row", "col"), nr * nx)
    part_two = gather_pieces(line(2), ("row", "col"), nr * nx)
    part_three = gather_pieces(line(3), ("row", "col"), nr * nx)
    lower = gather_pieces(pieces[K * nx : 2 * K * nx], ("col",), nx)
    lower = lower.transpose(1, 0, 2, 3).reshape(K * nx, nx * 8, NB)
    lower = gather_pieces(lower, ("row",), nr)

    arranged = jnp.take(front.reshape(local, nx, height, -1), order, axis=0, mode="clip").transpose(1, 0, 2, 3)
    rows = exchange(arranged, ("col",))

    own = parent_front.reshape(slots, nx, octets, 8, NB).transpose(2, 1, 0, 3, 4)
    own = exchange(own.reshape(nr * nx, slots, 8, NB), ("row", "col"))
    own = own.reshape(nr, nx, slots, 8, NB).transpose(2, 0, 3, 1, 4).reshape(slots, nr, 8, nx * NB)
    own_top = own[0, :4, :, : nc * 128].reshape(4, 8, nc, 128).transpose(2, 0, 1, 3)
    own_top = exchange(own_top, ("cube",))[0]

    square = block_shape
    g01, h01, l1 = call(
        first_kernel,
        [square(2), square(2), square(1)],
        26,
        in_specs=[SMEM, VMEM],
        out_specs=[VMEM] * 3,
        scratch_shapes=FACTOR_SCRATCH,
    )(pattern[: 2 * K], part_one)
    g2, h2, l2 = call(
        functools.partial(later_kernel, 2),
        [square(1), square(1), square(2)],
        14,
        in_specs=[SMEM] + [VMEM] * 3,
        out_specs=[VMEM] * 3,
        scratch_shapes=FACTOR_SCRATCH,
    )(pattern[: 2 * K], part_two, h01, l1)
    hs, ls = jnp.concatenate([h01, h2], axis=0), jnp.concatenate([l1, l2], axis=0)
    g3, h3, l3 = call(
        functools.partial(later_kernel, 3),
        [square(1), square(1), square(3)],
        15,
        in_specs=[SMEM] + [VMEM] * 3,
        out_specs=[VMEM] * 3,
        scratch_shapes=FACTOR_SCRATCH,
    )(pattern[: 2 * K], part_three, hs, ls)
    hs, ls = jnp.concatenate([hs, h3], axis=0), jnp.concatenate([ls, l3], axis=0)
    gs = jnp.concatenate([g01, g2, g3], axis=0)
    half = lambda *shape: jax.ShapeDtypeStruct(shape, bf16)
    weights = call(
        weights_kernel,
        [half(K, NB, NB)] * 2 + [half(6, NB, NB)] * 2 + [half(K * NB, K * NB)] * 2,
        6,
        in_specs=[SMEM] + [VMEM] * 3,
        out_specs=[VMEM] * 6,
    )(pattern[: 2 * K], lower, hs, ls)
    g_rows = lax.dynamic_slice_in_dim(gs, x * height, height, axis=1)

    top = call(
        functools.partial(rows_kernel, True, 1, octets),
        jax.ShapeDtypeStruct((nc, octets, 1, 8, 128), f32),
        3,
        in_specs=[SMEM] + [VMEM] * 8,
        out_specs=VMEM,
    )(row_info[:1], rows[:, :1], g_rows, *weights)
    top = exchange(top.reshape(holders, 1, 8, 128), ("cube", "row"))[:, 0]
    top_row = jnp.max(jnp.where((cubes == 0) & (places == 0), members, -1), axis=-1).reshape(holders)
    chosen = top_row[None, :] == jnp.arange(4)[:, None]
    top = own_top + jnp.sum(jnp.where(chosen[:, :, None, None], top[None], 0.0), axis=1)
    top = gather_pieces(top, ("cube", "row", "col"), nc * nr * nx)
    top = top.reshape(nc, nr, nx, 4, 8, 128)

    steps = local // slots
    full = lambda a: pl.BlockSpec(a.shape, lambda i, n=a.ndim: (0,) * n)
    back, extend = call(
        functools.partial(rows_kernel, False, slots, octets),
        [
            jax.ShapeDtypeStruct(rows.shape, f32),
            jax.ShapeDtypeStruct((nc * octets, slots, 8, nx * NB), f32),
        ],
        16,
        grid=(steps,),
        in_specs=[SMEM, pl.BlockSpec((nx, slots, height, 2 * NB), lambda i: (0, i, 0, 0))]
        + [full(a) for a in (g_rows,) + tuple(weights)],
        out_specs=[
            pl.BlockSpec((nx, slots, height, 2 * NB), lambda i: (0, i, 0, 0)),
            pl.BlockSpec((octets, slots, 8, nx * NB), lambda i: (i, 0, 0, 0)),
        ],
    )(row_info, rows, g_rows, *weights)
    extend = exchange(extend, ("cube", "row"))
    back = exchange(back, ("col",))
    child_out = jnp.take(back.transpose(1, 0, 2, 3), back_order, axis=0, mode="clip").reshape(child_front.shape)

    parent_weights = call(
        parent_kernel,
        [square(2)] + [half(2, NB, NB)] * 2 + [half(5, NB, NB)] * 2,
        30,
        in_specs=[SMEM, VMEM],
        out_specs=[VMEM] * 5,
        scratch_shapes=FACTOR_SCRATCH,
    )(parent_pattern[:4], top)
    g_parent = lax.dynamic_slice_in_dim(parent_weights[0], x * height + r * 8, 8, axis=1)
    parent_row = (
        jnp.arange(slots)[:, None] * holders + c * nr + jnp.arange(nr)[None, :]
    ).reshape(slots * nr)
    parent_info = jnp.concatenate(
        [
            parent_row[:, None],
            jnp.where(
                parent_row[:, None] > jnp.arange(KP)[None],
                jnp.take(parent_pattern, parent_row, axis=0, mode="clip"),
                0,
            ),
        ],
        axis=1,
    ).astype(jnp.int32)
    here = (cubes == c)[:, :, None, :] & (places[:, :, None, :] == jnp.arange(slots)[None, None, :, None])
    target = jnp.max(jnp.where(here, members[:, :, None, :], -1), axis=-1).reshape(holders, slots)
    result = call(
        parent_rows_kernel,
        jax.ShapeDtypeStruct((nr, nx, slots, 8, NB), f32),
        6,
        in_specs=[SMEM, SMEM] + [VMEM] * 7,
        out_specs=VMEM,
        scratch_shapes=[pltpu.VMEM(own.shape, f32)],
    )(parent_info, target.astype(jnp.int32), extend, own, g_parent, *parent_weights[1:])
    result = exchange(result.reshape(nr * nx, slots, 8, NB), ("row", "col"))
    result = result.reshape(nr, nx, slots, 8, NB).transpose(2, 1, 0, 3, 4).reshape(parent_front.shape)
    return child_out, result


def solution(mesh):
    placed = (P("cube", "row", "col"), P("cube", None, None), P(), P(("cube", "row"), "col"), P())
    return jax.shard_map(
        per_device,
        mesh=mesh,
        in_specs=placed,
        out_specs=(P("cube", "row", "col"), P(("cube", "row"), "col")),
        check_vma=False,
    )
```

```python
import functools

import jax
import jax.numpy as jnp
from jax import lax
from jax.experimental import pallas as pl
from jax.experimental.pallas import tpu as pltpu
from jax.sharding import PartitionSpec as P

NB = 256
K = 4
KP = 2
PB = 32

f32, bf16 = jnp.float32, jnp.bfloat16


def dims(a, b):
    return (((a,), (b,)), ((), ()))


NN, NT, TN = dims(1, 0), dims(1, 1), dims(0, 0)


def split(x):
    high = x.astype(bf16)
    return high, (x - high.astype(f32)).astype(bf16)


def dot3(x, y, d):
    xh, xl = x
    yh, yl = y
    part = lambda p, q: lax.dot_general(p, q, d, preferred_element_type=f32)
    return part(xh, yh) + (part(xh, yl) + part(xl, yh))


def small_factor(t):
    tiles = [t[8 * i : 8 * i + 8] for i in range(4)]
    full = (8, 128)
    sub = lax.broadcasted_iota(jnp.int32, full, 0)
    for s in range(4):
        c0 = PB + 8 * s
        cols = [
            [jnp.broadcast_to(tiles[q][:, c0 + k : c0 + k + 1], full) for k in range(8)]
            for q in range(s, 4)
        ]
        a = [
            [jnp.broadcast_to(cols[0][k][i : i + 1], full) if i >= k else None for k in range(8)]
            for i in range(8)
        ]
        rows = [jnp.broadcast_to(tiles[s][k : k + 1], full) for k in range(8)]
        mults = [[] for _ in range(s, 4)]
        scale = None
        for k in range(8):
            r = 1.0 / a[k][k]
            root = lax.rsqrt(a[k][k])
            scale = root if k == 0 else jnp.where(sub == k, root, scale)
            m = [a[i][k] * r if i > k else None for i in range(8)]
            for q in range(4 - s):
                mult = cols[q][k] * r
                if q == 0:
                    mult = jnp.where(sub > k, mult, 0.0)
                mults[q].append(mult)
            for i in range(k + 1, 8):
                rows[i] = rows[i] - m[i] * rows[k]
                for q in range(4 - s):
                    cols[q][i] = cols[q][i] - mults[q][k] * a[i][k]
                for j in range(k + 1, i + 1):
                    a[i][j] = a[i][j] - m[i] * a[j][k]
        for q in range(4 - s):
            acc = tiles[s + q]
            for k in range(8):
                acc = acc - mults[q][k] * rows[k]
            tiles[s + q] = acc
        tiles[s] = tiles[s] * scale
    return jnp.concatenate(tiles, axis=0)


def factor(block, work, out):
    row = lax.broadcasted_iota(jnp.int32, (NB, NB), 0)
    lane = lax.broadcasted_iota(jnp.int32, (NB, NB), 1)
    low = jnp.where(row >= lane, block, 0.0)
    work[:, :NB] = low + jnp.where(row > lane, block, 0.0).T
    work[:, NB:] = jnp.where(row == lane, 1.0, 0.0)
    lane32 = lax.broadcasted_iota(jnp.int32, (PB, 128), 1)
    row32 = lax.broadcasted_iota(jnp.int32, (PB, 128), 0)
    lane256 = lax.broadcasted_iota(jnp.int32, (PB, NB), 1)

    def body(p, _):
        base = pl.multiple_of(p * PB, PB)
        slab = work[pl.ds(base, PB), :]
        turned = pltpu.roll(slab[:, :NB], jnp.where(p == 0, PB, NB + PB - base), 1)[:, :128]
        unit = jnp.where(lane32 == row32, 1.0, 0.0)
        t = jnp.where((lane32 >= PB) & (lane32 < 2 * PB), turned, unit)
        j = small_factor(t)[:, :PB]
        u = dot3(split(j), split(slab), NN)
        out[pl.ds(base, PB), :] = u
        uh, ul = split(u)
        keep = lane256 >= base + PB
        zero = jnp.zeros((PB, NB), bf16)
        left = (jnp.where(keep, uh[:, :NB], zero), jnp.where(keep, ul[:, :NB], zero))
        work[...] -= dot3(left, (uh, ul), TN)
        return 0

    lax.fori_loop(0, NB // PB, body, 0)
    g = jnp.where(lane >= row, out[:, :NB], 0.0).T
    return g, out[:, NB:]


FACTOR_SCRATCH = [pltpu.VMEM((NB, 2 * NB), f32), pltpu.VMEM((NB, 2 * NB), f32)]


def kept(flag, value):
    return jnp.where(flag != 0, value, 0.0)


def call(kernel, out_shape, **kwargs):
    kwargs.setdefault("compiler_params", pltpu.CompilerParams(vmem_limit_bytes=56 << 20))
    return pl.pallas_call(
        kernel,
        out_shape=out_shape,
        cost_estimate=pl.CostEstimate(flops=1, bytes_accessed=1, transcendentals=0),
        **kwargs,
    )


VMEM = pl.BlockSpec(memory_space=pltpu.VMEM)
SMEM = pl.BlockSpec(memory_space=pltpu.SMEM)
ANY = pl.BlockSpec(memory_space=pl.ANY)


def block_shape(*lead):
    return jax.ShapeDtypeStruct(lead + (NB, NB), f32)


def whole(ref, index):
    return ref[:, index].reshape(NB, NB)


def pair(i, j):
    return i * (i - 1) // 2 + j


def first_kernel(pattern, piece, g, h, l, work, out):
    g0, h0 = factor(whole(piece, 0), work, out)
    g[0], h[0] = g0, h0
    l10 = kept(pattern[1, 0], dot3(split(whole(piece, 1)), split(h0), NT))
    l[0] = l10
    s10 = split(l10)
    g[1], h[1] = factor(whole(piece, 2) - dot3(s10, s10, NT), work, out)


def own_kernel(later, place, e0, e1, e2, e3, *refs):
    sent = refs[-3]
    octets, slots = sent.shape[0], sent.shape[1]
    height = octets * 8
    base = e0.shape[0] - slots * height
    for d, early in enumerate([e0, e1, e2, e3]):
        lanes = pl.ds(pl.multiple_of(place[d] * NB, NB), NB)
        for s in range(slots):
            sent[:, s, :, lanes] = early[base + s * height : base + (s + 1) * height].reshape(octets, 8, NB)
    later(*refs[:-3], *refs[-2:])


def later_kernel(k, first, pattern, piece, *refs):
    count = k - 1
    h_refs, l_refs = refs[:count], refs[count : 2 * count]
    g, h, l, work, out = refs[2 * count :]
    hs, ls = listed(h_refs), listed(l_refs)
    row = [whole(piece, first + j) for j in range(k + 1)]
    for j in range(k):
        l[j] = kept(pattern[k, j], dot3(split(row[j]), split(hs[j][...]), NT))
        value = split(l[j])
        for i in range(j + 1, k):
            row[i] = row[i] - dot3(value, split(ls[pair(i, j)][...]), NT)
        row[k] = row[k] - dot3(value, value, NT)
    g[0], h[0] = factor(row[k], work, out)


def listed(refs):
    return [ref.at[i] for ref in refs for i in range(ref.shape[0])]


def solve_rows(columns, mask, h, l):
    solved = []
    columns = list(columns)
    for k in range(len(columns)):
        value = mask(k, dot3(split(columns[k]), h(k), NT))
        solved.append(value)
        value = split(value)
        for j in range(k + 1, len(columns)):
            columns[j] = columns[j] - dot3(value, l(j, k), NT)
    return solved


def row_mask(info, first, groups, height):
    def mask(k, value):
        parts = [
            kept(info[first + i, 1 + k], value[i * height : (i + 1) * height]) for i in range(groups)
        ]
        return jnp.concatenate(parts, axis=0) if groups > 1 else parts[0]

    return mask


def lead_kernel(info, place, pattern, lower, lowest, h01, h2, h3, l1, l2, l3, e0, e1, e2, e3, *refs):
    hh, hl, lh, ll, ch, cl, top, rows = refs[-8:]
    for k, block in enumerate(listed([h01, h2, h3])):
        hh[k], hl[k] = split(block[...])
    for k, block in enumerate(listed([l1, l2, l3])):
        lh[k], ll[k] = split(block[...])
    h = lambda k: (hh[k], hl[k])
    l = lambda j, k: (lh[pair(j, k)], ll[pair(j, k)])
    blocks = [(lower, lowest)[j // 2].at[:, j % 2 * K + k] for j in range(K) for k in range(K)]
    columns = [
        jnp.concatenate([blocks[j * K + k][...].reshape(NB, NB) for j in range(K)], axis=0) for k in range(K)
    ]

    def mask(k, value):
        parts = [kept(pattern[K + j, k], value[j * NB : (j + 1) * NB]) for j in range(K)]
        return jnp.concatenate(parts, axis=0)

    solved = solve_rows(columns, mask, h, l)
    for k in range(K):
        ch[:, k * NB : (k + 1) * NB], cl[:, k * NB : (k + 1) * NB] = split(solved[k])
    height = rows.shape[2]
    base = e0.shape[0] - 6 * height
    for d, early in enumerate([e0, e1, e2, e3]):
        rows[place[d]] = early[base : base + 3 * height].reshape(3, height, NB)
    solved = solve_rows([rows[k, 0] for k in range(K)], row_mask(info, info[0, 2 + K], 1, height), h, l)
    update = dot3(split(jnp.concatenate(solved, axis=1)), (ch[: 2 * NB], cl[: 2 * NB]), NT)
    for v in range(K):
        start = v % 2 * 128
        lanes = slice(start, start + 128)
        schur = rows[v // 2, 1, :, lanes] - update[:, v * 128 : v * 128 + 128]
        top[v, :, 0] = schur.reshape(height // 8, 8, 128)
        top[v, :, 1] = rows[v // 2, 2, :, lanes].reshape(height // 8, 8, 128)


def rows_kernel(info, place, front, p1, p2, p3, g01, g2, g3, hh, hl, lh, ll, ch, cl, *refs):
    child, b1, b2, b3, extend, fin, fout, eout, insem, outsem, extsem = refs[-11:]
    step, steps = pl.program_id(0), pl.num_programs(0)
    groups, height = fin.shape[2], fin.shape[3]
    octets = height // 8
    slot = lax.rem(step, 2)

    def load(at, slot):
        for s in range(groups):
            here = at * groups + s
            for d, source in enumerate([front.at[here, place[0]], p1.at[here], p2.at[here], p3.at[here]]):
                pltpu.make_async_copy(source, fin.at[slot, place[d], s], insem.at[slot]).start()

    def store(at, slot):
        for s in range(groups):
            here = at * groups + s
            for d, target in enumerate([child.at[here, place[0]], b1.at[here], b2.at[here], b3.at[here]]):
                pltpu.make_async_copy(fout.at[slot, place[d], s], target, outsem.at[slot]).start()

    def wait(buffer, slot, sem):
        pltpu.make_async_copy(buffer.at[slot], buffer.at[slot], sem.at[slot]).wait()

    @pl.when(step == 0)
    def _():
        load(0, 0)

    @pl.when(step + 1 < steps)
    def _():
        load(step + 1, 1 - slot)

    wait(fin, slot, insem)

    @pl.when(step >= 2)
    def _():
        wait(fout, slot, outsem)
        wait(eout, slot, extsem)

    first = step * groups
    columns = [fin[slot, k, :, :, :NB].reshape(groups * height, NB) for k in range(K)]
    solved = solve_rows(
        columns,
        row_mask(info, first, groups, height),
        lambda k: (hh[k], hl[k]),
        lambda j, k: (lh[pair(j, k)], ll[pair(j, k)]),
    )
    update = dot3(split(jnp.concatenate(solved, axis=1)), (ch[...], cl[...]), NT)
    for k, g in enumerate(listed([g01, g2, g3])):
        fout[slot, k, :, :, :NB] = solved[k].reshape(groups, height, NB)
        schur = fin[slot, k, :, :, NB:].reshape(groups * height, NB) - update[:, k * NB : (k + 1) * NB]
        fout[slot, k, :, :, NB:] = schur.reshape(groups, height, NB)
        eout[slot, :, :, :, k * NB : (k + 1) * NB] = schur.reshape(groups, octets, 8, NB)
        for i in range(groups):

            @pl.when(info[first + i, 0] == k)
            def _():
                mine = pl.ds(pl.multiple_of(place[0] * height, height), height)
                fout[slot, k, i, :, :NB] = g[mine, :]

    store(step, slot)

    def send(i):
        at = info[first + i, 1 + K]
        holder = pl.multiple_of(lax.div(at, groups) * octets, octets)
        target = extend.at[pl.ds(holder, octets), lax.rem(at, groups)]
        return pltpu.make_async_copy(eout.at[slot, i], target, extsem.at[slot])

    for i in range(groups):
        send(i).start()

    @pl.when(step == steps - 1)
    def _():
        for other in range(2):
            wait(fout, other, outsem)
            wait(eout, other, extsem)


def parent_kernel(pattern, top, g, hh, hl, lh, ll, work, out):
    def block(i, j):
        halves = [
            jnp.swapaxes(top[2 * j + v, :, :, i], 0, 1).reshape(NB, 128) for v in range(2)
        ]
        return jnp.concatenate(halves, axis=1)

    g0, h0 = factor(block(0, 0), work, out)
    g[0] = g0
    h0 = split(h0)
    hh[0], hl[0] = h0
    first = []
    for i in range(1, 4):
        value = split(kept(pattern[i, 0], dot3(split(block(i, 0)), h0, NT)))
        lh[i - 1], ll[i - 1] = value
        first.append(value)
    g1, h1 = factor(block(1, 1) - dot3(first[0], first[0], NT), work, out)
    g[1] = g1
    h1 = split(h1)
    hh[1], hl[1] = h1
    for i in range(2, 4):
        rest = block(i, 1) - dot3(first[i - 1], first[0], NT)
        lh[i + 1], ll[i + 1] = split(kept(pattern[i, 1], dot3(split(rest), h1, NT)))


def parent_steps(columns, mask, hh, hl, lh, ll):
    one = mask(0, dot3(split(columns[0]), (hh[0], hl[0]), NT))
    first = split(one)
    two = mask(1, dot3(split(columns[1] - dot3(first, (lh[0], ll[0]), NT)), (hh[1], hl[1]), NT))
    second = split(two)
    results = [one, two]
    for j in range(2, 4):
        left = dot3(first, (lh[j - 1], ll[j - 1]), NT) + dot3(second, (lh[j + 1], ll[j + 1]), NT)
        results.append(columns[j] - left)
    return results


def parent_rows_kernel(info, place, target, extend, own, g, hh, hl, lh, ll, out, acc):
    slots, members = acc.shape[0], acc.shape[1]
    for s in range(slots):
        acc[s] = own[:, s]

    def add(q, _):
        for s in range(slots):
            where = target[q, s]

            @pl.when(where >= 0)
            def _():
                acc[s, where] += extend[q, s]

        return 0

    lax.fori_loop(0, extend.shape[0], add, 0)
    columns = [acc[:, :, :, j * NB : (j + 1) * NB].reshape(slots * members * 8, NB) for j in range(4)]
    results = parent_steps(columns, row_mask(info, 0, slots * members, 8), hh, hl, lh, ll)
    for j in range(4):
        shaped = results[j].reshape(slots, members, 8, NB)
        for s in range(slots):
            out[:, j, s] = shaped[s]
    for k in range(KP):

        @pl.when(info[k, 0] == k)
        def _():
            mine = pl.ds(pl.multiple_of(place[K] * 8, 8), 8)
            out[k, k, 0] = g[k, mine, :]


def exchange(array, axes):
    return lax.all_to_all(array, axes, split_axis=0, concat_axis=0, tiled=True)


def gather_pieces(pieces, axes, count):
    return exchange(jnp.broadcast_to(pieces[None], (count,) + pieces.shape), axes)


def shift(array, d, n):
    return lax.ppermute(array, "col", [(i, (i + d) % n) for i in range(n)])


def nought(array):
    one = array[(0,) * array.ndim]
    return (one != one).astype(jnp.int32)


def once(arrays, others):
    count = len(arrays)
    return pl.pallas_call(
        lambda *refs: None,
        out_shape=[jax.ShapeDtypeStruct(array.shape, array.dtype) for array in arrays],
        in_specs=[ANY] * (count + len(others)),
        out_specs=[ANY] * count,
        input_output_aliases={i: i for i in range(count)},
    )(*arrays, *others)


def per_device(child_front, child_pattern, block_map, parent_front, parent_pattern):
    nr, nx, nc = lax.axis_size("row"), lax.axis_size("col"), lax.axis_size("cube")
    r, x, c = lax.axis_index("row"), lax.axis_index("col"), lax.axis_index("cube")
    local = child_front.shape[1] // NB
    slots = parent_front.shape[0] // NB
    height = NB // nx
    octets = height // 8
    holders = nc * nr
    front = child_front[0]
    pattern = child_pattern[0]

    place = jnp.stack([(x - d) % nx for d in range(nx)] + [x * octets + r]).astype(jnp.int32)
    square = block_shape
    half = lambda *shape: jax.ShapeDtypeStruct(shape, bf16)

    corner = front[:NB, :NB].reshape(nr * nx, 1, 8, NB)
    pieces = exchange(corner, ("row", "col"))[:, 0]
    lines = [pieces[i * nx : i * nx + i + 1] for i in range(K)] + [pieces[K * nx : 2 * K * nx]]
    lines = jnp.concatenate(lines, axis=0)
    begun = nought(pieces)
    lines = jnp.stack([lines] + [shift(lines, d, nx) for d in range(1, nx)])
    lines = jnp.take(lines, (x - jnp.arange(nx)) % nx, axis=0, mode="clip")
    lines = lines.transpose(1, 0, 2, 3).reshape(-1, nx * 8, NB)
    part_one = gather_pieces(lines[:3], ("row",), nr)

    tables = block_map.reshape(nc, local, nr).transpose(0, 2, 1)
    live = tables >= 0
    cubes = jnp.where(live, tables % holders // nr, -1)
    places = jnp.where(live, tables // holders, -1)
    members = jnp.where(live, tables % nr, -1)
    mine = tables[c, r]
    spot = jnp.where(mine >= 0, cubes[c, r] * slots + places[c, r], -1)
    spot = jnp.where(spot >= 0, spot, local * (local - 1) // 2 - jnp.sum(jnp.maximum(spot, 0)))
    lead = jnp.sum(jnp.where(spot == 0, jnp.arange(local), 0))
    block_row = jnp.arange(local) * nr + r
    kept_rows = jnp.where(
        block_row[:, None] > jnp.arange(K)[None], jnp.take(pattern, block_row, axis=0, mode="clip"), 0
    )
    row_info = jnp.concatenate(
        [block_row[:, None], kept_rows, spot[:, None], jnp.full((local, 1), lead)], axis=1
    ).astype(jnp.int32)

    quarters = front.reshape(local, nx, height, -1)
    ahead = lax.dynamic_index_in_dim(quarters, lead, axis=0, keepdims=False)
    ahead = ahead.reshape(nx, height, 2, NB).transpose(0, 2, 1, 3)
    own = parent_front.reshape(slots, nx, height, NB).transpose(1, 0, 2, 3)
    ahead = jnp.concatenate([ahead, own], axis=1)
    ahead = ahead.reshape(nx, -1, NB)
    early = [lax.dynamic_index_in_dim(ahead, (x + d + begun) % nx, axis=0, keepdims=False) for d in range(nx)]
    early = early[:1] + [shift(early[d], d, nx) for d in range(1, nx)]
    sent = [lax.dynamic_index_in_dim(quarters, (x + d + begun) % nx, axis=1, keepdims=False) for d in range(1, nx)]
    sent = once(sent, [part_one, *early[1:]])
    parts = [shift(part, d + 1, nx) for d, part in enumerate(sent)]

    def panels():
        part_two = gather_pieces(lines[3:10], ("row",), nr)
        lower = [lax.all_gather(lines[10 + K * i : 10 + K * i + 2 * K], "row") for i in (0, 2)]
        g01, h01, l1, own = call(
            functools.partial(own_kernel, first_kernel),
            [square(2), square(2), square(1), jax.ShapeDtypeStruct((octets, slots, 8, nx * NB), f32)],
            in_specs=[SMEM] + [VMEM] * 4 + [SMEM, VMEM],
            out_specs=[VMEM] * 4,
            scratch_shapes=FACTOR_SCRATCH,
        )(place, *early, pattern[: 2 * K], part_one)
        own = exchange(own, ("row",))
        g2, h2, l2 = call(
            functools.partial(later_kernel, 2, 0),
            [square(1), square(1), square(2)],
            in_specs=[SMEM] + [VMEM] * 3,
            out_specs=[VMEM] * 3,
            scratch_shapes=FACTOR_SCRATCH,
        )(pattern[: 2 * K], part_two, h01, l1)
        g3, h3, l3 = call(
            functools.partial(later_kernel, 3, 3),
            [square(1), square(1), square(3)],
            in_specs=[SMEM] + [VMEM] * 5,
            out_specs=[VMEM] * 3,
            scratch_shapes=FACTOR_SCRATCH,
        )(pattern[: 2 * K], part_two, h01, h2, l1, l2)

        *weights, top = call(
            lead_kernel,
            [half(K, NB, NB)] * 2
            + [half(6, NB, NB)] * 2
            + [half(K * NB, K * NB)] * 2
            + [jax.ShapeDtypeStruct((nc, octets, 2, 8, 128), f32)],
            in_specs=[SMEM] * 3 + [VMEM] * 12 + [ANY],
            out_specs=[VMEM] * 7,
            scratch_shapes=[pltpu.VMEM((nx, 3, height, NB), f32)],
        )(row_info, place, pattern[: 2 * K], *lower, h01, h2, h3, l1, l2, l3, *early, own)
        top = exchange(top.reshape(holders, 2, 8, 128), ("cube", "row"))
        top_row = jnp.max(jnp.where((cubes == 0) & (places == 0), members, -1), axis=-1).reshape(holders)
        chosen = top_row[None, :] == jnp.arange(4)[:, None]
        top = top[:4, 1] + jnp.sum(jnp.where(chosen[:, :, None, None], top[None, :, 0], 0.0), axis=1)
        return top, own, g01, g2, g3, weights

    empty = jax.tree.map(lambda leaf: jnp.zeros(leaf.shape, leaf.dtype), jax.eval_shape(panels))
    top, own, g01, g2, g3, weights = lax.cond(nought(part_one) == 0, panels, lambda: empty)
    (top,) = once([top], parts)
    top_sent = jnp.broadcast_to(top[None], (nc * nr * nx,) + top.shape)
    top = exchange(top_sent, ("cube", "row", "col")).reshape(nc, nr, nx, 4, 8, 128)

    full = lambda a: pl.BlockSpec(a.shape, lambda i, n=a.ndim: (0,) * n)
    buffer = pltpu.VMEM((2, nx, slots, height, 2 * NB), f32)
    wide = jax.ShapeDtypeStruct((nc * octets, slots, 8, nx * NB), f32)
    child_out, *back, extend = call(
        rows_kernel,
        [jax.ShapeDtypeStruct(quarters.shape, f32), *[jax.ShapeDtypeStruct(parts[0].shape, f32)] * 3, wide],
        grid=(local // slots,),
        in_specs=[SMEM] * 2 + [ANY] * 4 + [full(a) for a in (g01, g2, g3, *weights)] + [ANY],
        out_specs=[ANY] * 5,
        scratch_shapes=[buffer, buffer, pltpu.VMEM((2, slots, octets, 8, nx * NB), f32)]
        + [pltpu.SemaphoreType.DMA((2,))] * 3,
    )(row_info, place, quarters, *parts, g01, g2, g3, *weights, top_sent)
    extend = exchange(extend, ("cube", "row"))

    g_parent, *parent_weights = call(
        parent_kernel,
        [square(2)] + [half(2, NB, NB)] * 2 + [half(5, NB, NB)] * 2,
        in_specs=[SMEM, VMEM],
        out_specs=[VMEM] * 5,
        scratch_shapes=FACTOR_SCRATCH,
    )(parent_pattern[:4], top)

    def parent_info(block_row):
        flags = jnp.take(parent_pattern, block_row, axis=0, mode="clip")
        flags = jnp.where(block_row[:, None] > jnp.arange(KP)[None], flags, 0)
        return jnp.concatenate([block_row[:, None], flags], axis=1).astype(jnp.int32)

    slot_row = jnp.arange(slots) * holders + c * nr
    here = (cubes == c)[:, :, None, :] & (places[:, :, None, :] == jnp.arange(slots)[None, None, :, None])
    target = jnp.max(jnp.where(here, members[:, :, None, :], -1), axis=-1).reshape(holders, slots)
    result = call(
        parent_rows_kernel,
        jax.ShapeDtypeStruct((nr, nx, slots, 8, NB), f32),
        in_specs=[SMEM] * 3 + [VMEM] * 7,
        out_specs=VMEM,
        scratch_shapes=[pltpu.VMEM((slots, nr, 8, nx * NB), f32)],
    )(
        parent_info((slot_row[:, None] + jnp.arange(nr)[None, :]).reshape(-1)),
        place,
        target.astype(jnp.int32),
        extend,
        own,
        g_parent,
        *parent_weights,
    )
    late = x + nought(result)
    for d in range(1, nx):
        part = shift(back[d - 1], -d, nx)[:, None]
        child_out = lax.dynamic_update_slice(child_out, part, (0, (late + d) % nx, 0, 0))
    child_out = child_out.reshape(child_front.shape)
    result = exchange(result.reshape(nr * nx, slots, 8, NB), ("row", "col"))
    result = result.reshape(nr, nx, slots, 8, NB).transpose(2, 1, 0, 3, 4).reshape(parent_front.shape)
    return child_out, result


def solution(mesh):
    placed = (P("cube", "row", "col"), P("cube", None, None), P(), P(("cube", "row"), "col"), P())
    return jax.shard_map(
        per_device,
        mesh=mesh,
        in_specs=placed,
        out_specs=(P("cube", "row", "col"), P(("cube", "row"), "col")),
        check_vma=False,
    )
```

```python
import functools

import jax
import jax.numpy as jnp
from jax import lax
from jax.experimental import pallas as pl
from jax.experimental.pallas import tpu as pltpu
from jax.sharding import PartitionSpec as P

NB = 256
K = 4
KP = 2
PB = 64

f32, bf16 = jnp.float32, jnp.bfloat16


def dims(a, b):
    return (((a,), (b,)), ((), ()))


NN, NT, TN = dims(1, 0), dims(1, 1), dims(0, 0)


def split(x):
    high = x.astype(bf16)
    return high, (x - high.astype(f32)).astype(bf16)


def dot3(x, y, d):
    xh, xl = x
    yh, yl = y
    part = lambda p, q: lax.dot_general(p, q, d, preferred_element_type=f32)
    return part(xh, yh) + (part(xh, yl) + part(xl, yh))


def small_factor(t):
    count = PB // 8
    tiles = [t[8 * i : 8 * i + 8] for i in range(count)]
    full = (8, 128)
    sub = lax.broadcasted_iota(jnp.int32, full, 0)
    for s in range(count):
        c0 = PB + 8 * s
        cols = [
            [jnp.broadcast_to(tiles[q][:, c0 + k : c0 + k + 1], full) for k in range(8)]
            for q in range(s, count)
        ]
        a = [
            [jnp.broadcast_to(cols[0][k][i : i + 1], full) if i >= k else None for k in range(8)]
            for i in range(8)
        ]
        rows = [jnp.broadcast_to(tiles[s][k : k + 1], full) for k in range(8)]
        mults = [[] for _ in range(s, count)]
        scale = None
        for k in range(8):
            r = 1.0 / a[k][k]
            root = lax.rsqrt(a[k][k])
            scale = root if k == 0 else jnp.where(sub == k, root, scale)
            m = [a[i][k] * r if i > k else None for i in range(8)]
            for q in range(count - s):
                mult = cols[q][k] * r
                if q == 0:
                    mult = jnp.where(sub > k, mult, 0.0)
                mults[q].append(mult)
            for i in range(k + 1, 8):
                rows[i] = rows[i] - m[i] * rows[k]
                for q in range(count - s):
                    cols[q][i] = cols[q][i] - mults[q][k] * a[i][k]
                for j in range(k + 1, i + 1):
                    a[i][j] = a[i][j] - m[i] * a[j][k]
        for q in range(count - s):
            acc = tiles[s + q]
            for k in range(8):
                acc = acc - mults[q][k] * rows[k]
            tiles[s + q] = acc
        tiles[s] = tiles[s] * scale
    return jnp.concatenate(tiles, axis=0)


def factor(block, work, out):
    row = lax.broadcasted_iota(jnp.int32, (NB, NB), 0)
    lane = lax.broadcasted_iota(jnp.int32, (NB, NB), 1)
    low = jnp.where(row >= lane, block, 0.0)
    work[:, :NB] = low + jnp.where(row > lane, block, 0.0).T
    work[:, NB:] = jnp.where(row == lane, 1.0, 0.0)
    lane_of = lax.broadcasted_iota(jnp.int32, (PB, 128), 1)
    row_of = lax.broadcasted_iota(jnp.int32, (PB, 128), 0)
    wide_lane = lax.broadcasted_iota(jnp.int32, (PB, NB), 1)

    def body(p, _):
        base = pl.multiple_of(p * PB, PB)
        slab = work[pl.ds(base, PB), :]
        turned = pltpu.roll(slab[:, :NB], jnp.where(p == 0, PB, NB + PB - base), 1)[:, :128]
        unit = jnp.where(lane_of == row_of, 1.0, 0.0)
        t = jnp.where((lane_of >= PB) & (lane_of < 2 * PB), turned, unit)
        j = small_factor(t)[:, :PB]
        u = dot3(split(j), split(slab), NN)
        out[pl.ds(base, PB), :] = u
        uh, ul = split(u)
        keep = wide_lane >= base + PB
        zero = jnp.zeros((PB, NB), bf16)
        left = (jnp.where(keep, uh[:, :NB], zero), jnp.where(keep, ul[:, :NB], zero))
        work[...] -= dot3(left, (uh, ul), TN)
        return 0

    lax.fori_loop(0, NB // PB, body, 0)
    g = jnp.where(lane >= row, out[:, :NB], 0.0).T
    return g, out[:, NB:]


FACTOR_SCRATCH = [pltpu.VMEM((NB, 2 * NB), f32), pltpu.VMEM((NB, 2 * NB), f32)]


def kept(flag, value):
    return jnp.where(flag != 0, value, 0.0)


def call(kernel, out_shape, **kwargs):
    kwargs.setdefault("compiler_params", pltpu.CompilerParams(vmem_limit_bytes=56 << 20))
    return pl.pallas_call(
        kernel,
        out_shape=out_shape,
        cost_estimate=pl.CostEstimate(flops=1, bytes_accessed=1, transcendentals=0),
        **kwargs,
    )


VMEM = pl.BlockSpec(memory_space=pltpu.VMEM)
SMEM = pl.BlockSpec(memory_space=pltpu.SMEM)
ANY = pl.BlockSpec(memory_space=pl.ANY)


def block_shape(*lead):
    return jax.ShapeDtypeStruct(lead + (NB, NB), f32)


def whole(ref, index):
    return ref[:, index].reshape(NB, NB)


def pair(i, j):
    return i * (i - 1) // 2 + j


def first_kernel(pattern, piece, g, h, l, work, out):
    g0, h0 = factor(whole(piece, 0), work, out)
    g[0], h[0] = g0, h0
    l10 = kept(pattern[1, 0], dot3(split(whole(piece, 1)), split(h0), NT))
    l[0] = l10
    s10 = split(l10)
    g[1], h[1] = factor(whole(piece, 2) - dot3(s10, s10, NT), work, out)


def own_kernel(later, place, e0, e1, e2, e3, *refs):
    sent = refs[-3]
    octets, slots = sent.shape[0], sent.shape[1]
    height = octets * 8
    base = e0.shape[0] - slots * height
    for d, early in enumerate([e0, e1, e2, e3]):
        lanes = pl.ds(pl.multiple_of(place[d] * NB, NB), NB)
        for s in range(slots):
            sent[:, s, :, lanes] = early[base + s * height : base + (s + 1) * height].reshape(octets, 8, NB)
    later(*refs[:-3], *refs[-2:])


def later_kernel(k, first, pattern, piece, *refs):
    count = k - 1
    h_refs, l_refs = refs[:count], refs[count : 2 * count]
    g, h, l, work, out = refs[2 * count :]
    hs, ls = listed(h_refs), listed(l_refs)
    row = [whole(piece, first + j) for j in range(k + 1)]
    for j in range(k):
        l[j] = kept(pattern[k, j], dot3(split(row[j]), split(hs[j][...]), NT))
        value = split(l[j])
        for i in range(j + 1, k):
            row[i] = row[i] - dot3(value, split(ls[pair(i, j)][...]), NT)
        row[k] = row[k] - dot3(value, value, NT)
    g[0], h[0] = factor(row[k], work, out)


def listed(refs):
    return [ref.at[i] for ref in refs for i in range(ref.shape[0])]


def solve_rows(columns, mask, h, l):
    solved = []
    columns = list(columns)
    for k in range(len(columns)):
        value = mask(k, dot3(split(columns[k]), h(k), NT))
        solved.append(value)
        value = split(value)
        for j in range(k + 1, len(columns)):
            columns[j] = columns[j] - dot3(value, l(j, k), NT)
    return solved


def row_mask(info, first, groups, height):
    def mask(k, value):
        parts = [
            kept(info[first + i, 1 + k], value[i * height : (i + 1) * height]) for i in range(groups)
        ]
        return jnp.concatenate(parts, axis=0) if groups > 1 else parts[0]

    return mask


def lead_kernel(info, place, pattern, lower, h01, h2, h3, l1, l2, l3, e0, e1, e2, e3, *refs):
    hh, hl, lh, ll, ch, cl, top, rows = refs[-8:]
    for k, block in enumerate(listed([h01, h2, h3])):
        hh[k], hl[k] = split(block[...])
    for k, block in enumerate(listed([l1, l2, l3])):
        lh[k], ll[k] = split(block[...])
    h = lambda k: (hh[k], hl[k])
    l = lambda j, k: (lh[pair(j, k)], ll[pair(j, k)])
    columns = [jnp.concatenate([whole(lower, j * K + k) for j in range(K)], axis=0) for k in range(K)]

    def mask(k, value):
        parts = [kept(pattern[K + j, k], value[j * NB : (j + 1) * NB]) for j in range(K)]
        return jnp.concatenate(parts, axis=0)

    solved = solve_rows(columns, mask, h, l)
    for k in range(K):
        ch[:, k * NB : (k + 1) * NB], cl[:, k * NB : (k + 1) * NB] = split(solved[k])
    height = rows.shape[2]
    base = e0.shape[0] - 6 * height
    for d, early in enumerate([e0, e1, e2, e3]):
        rows[place[d]] = early[base : base + 3 * height].reshape(3, height, NB)
    solved = solve_rows([rows[k, 0] for k in range(K)], row_mask(info, info[0, 2 + K], 1, height), h, l)
    update = dot3(split(jnp.concatenate(solved, axis=1)), (ch[: 2 * NB], cl[: 2 * NB]), NT)
    for v in range(K):
        start = v % 2 * 128
        lanes = slice(start, start + 128)
        schur = rows[v // 2, 1, :, lanes] - update[:, v * 128 : v * 128 + 128]
        top[v, :, 0] = schur.reshape(height // 8, 8, 128)
        top[v, :, 1] = rows[v // 2, 2, :, lanes].reshape(height // 8, 8, 128)


def rows_kernel(begin, info, place, front, p1, p2, p3, g01, g2, g3, hh, hl, lh, ll, ch, cl, *refs):
    child, b1, b2, b3, extend, fin, fout, eout, insem, outsem, extsem = refs[-11:]
    step, steps = pl.program_id(0), pl.num_programs(0)
    groups, height = fin.shape[2], fin.shape[3]
    octets = height // 8
    slot = lax.rem(step, 2)

    def load(at, slot):
        for s in range(groups):
            here = begin + at * groups + s
            for d, source in enumerate([front.at[here, place[0]], p1.at[here], p2.at[here], p3.at[here]]):
                pltpu.make_async_copy(source, fin.at[slot, place[d], s], insem.at[slot]).start()

    def store(at, slot):
        for s in range(groups):
            here = at * groups + s
            for d, target in enumerate([child.at[begin + here, place[0]], b1.at[here], b2.at[begin + here], b3.at[here]]):
                pltpu.make_async_copy(fout.at[slot, place[d], s], target, outsem.at[slot]).start()

    def wait(buffer, slot, sem):
        pltpu.make_async_copy(buffer.at[slot], buffer.at[slot], sem.at[slot]).wait()

    @pl.when(step == 0)
    def _():
        load(0, 0)

    @pl.when(step + 1 < steps)
    def _():
        load(step + 1, 1 - slot)

    wait(fin, slot, insem)

    @pl.when(step >= 2)
    def _():
        wait(fout, slot, outsem)
        wait(eout, slot, extsem)

    first = begin + step * groups
    columns = [fin[slot, k, :, :, :NB].reshape(groups * height, NB) for k in range(K)]
    solved = solve_rows(
        columns,
        row_mask(info, first, groups, height),
        lambda k: (hh[k], hl[k]),
        lambda j, k: (lh[pair(j, k)], ll[pair(j, k)]),
    )
    update = dot3(split(jnp.concatenate(solved, axis=1)), (ch[...], cl[...]), NT)
    for k, g in enumerate(listed([g01, g2, g3])):
        fout[slot, k, :, :, :NB] = solved[k].reshape(groups, height, NB)
        schur = fin[slot, k, :, :, NB:].reshape(groups * height, NB) - update[:, k * NB : (k + 1) * NB]
        fout[slot, k, :, :, NB:] = schur.reshape(groups, height, NB)
        eout[slot, :, :, :, k * NB : (k + 1) * NB] = schur.reshape(groups, octets, 8, NB)
        for i in range(groups):

            @pl.when(info[first + i, 0] == k)
            def _():
                mine = pl.ds(pl.multiple_of(place[0] * height, height), height)
                fout[slot, k, i, :, :NB] = g[mine, :]

    store(step, slot)

    def send(i):
        at = info[first + i, 1 + K]
        holder = pl.multiple_of(lax.div(at, groups) * octets, octets)
        target = extend.at[pl.ds(holder, octets), lax.rem(at, groups)]
        return pltpu.make_async_copy(eout.at[slot, i], target, extsem.at[slot])

    for i in range(groups):
        send(i).start()

    @pl.when(step == steps - 1)
    def _():
        for other in range(2):
            wait(fout, other, outsem)
            wait(eout, other, extsem)


def parent_kernel(pattern, top, g, hh, hl, lh, ll, work, out):
    def block(i, j):
        halves = [
            jnp.swapaxes(top[2 * j + v, :, :, i], 0, 1).reshape(NB, 128) for v in range(2)
        ]
        return jnp.concatenate(halves, axis=1)

    g0, h0 = factor(block(0, 0), work, out)
    g[0] = g0
    h0 = split(h0)
    hh[0], hl[0] = h0
    first = []
    for i in range(1, 4):
        value = split(kept(pattern[i, 0], dot3(split(block(i, 0)), h0, NT)))
        lh[i - 1], ll[i - 1] = value
        first.append(value)
    g1, h1 = factor(block(1, 1) - dot3(first[0], first[0], NT), work, out)
    g[1] = g1
    h1 = split(h1)
    hh[1], hl[1] = h1
    for i in range(2, 4):
        rest = block(i, 1) - dot3(first[i - 1], first[0], NT)
        lh[i + 1], ll[i + 1] = split(kept(pattern[i, 1], dot3(split(rest), h1, NT)))


def parent_steps(columns, mask, hh, hl, lh, ll):
    one = mask(0, dot3(split(columns[0]), (hh[0], hl[0]), NT))
    first = split(one)
    two = mask(1, dot3(split(columns[1] - dot3(first, (lh[0], ll[0]), NT)), (hh[1], hl[1]), NT))
    second = split(two)
    results = [one, two]
    for j in range(2, 4):
        left = dot3(first, (lh[j - 1], ll[j - 1]), NT) + dot3(second, (lh[j + 1], ll[j + 1]), NT)
        results.append(columns[j] - left)
    return results


def parent_rows_kernel(info, place, target, extend, own, g, hh, hl, lh, ll, out, acc):
    slots, members = acc.shape[0], acc.shape[1]
    for s in range(slots):
        acc[s] = own[:, s]

    def add(q, _):
        for s in range(slots):
            where = target[q, s]

            @pl.when(where >= 0)
            def _():
                acc[s, where] += extend[q, s]

        return 0

    lax.fori_loop(0, extend.shape[0], add, 0)
    columns = [acc[:, :, :, j * NB : (j + 1) * NB].reshape(slots * members * 8, NB) for j in range(4)]
    results = parent_steps(columns, row_mask(info, 0, slots * members, 8), hh, hl, lh, ll)
    for j in range(4):
        shaped = results[j].reshape(slots, members, 8, NB)
        for s in range(slots):
            out[:, j, s] = shaped[s]
    for k in range(KP):

        @pl.when(info[k, 0] == k)
        def _():
            mine = pl.ds(pl.multiple_of(place[K] * 8, 8), 8)
            out[k, k, 0] = g[k, mine, :]


def exchange(array, axes):
    return lax.all_to_all(array, axes, split_axis=0, concat_axis=0, tiled=True)


def gather_pieces(pieces, axes, count):
    return exchange(jnp.broadcast_to(pieces[None], (count,) + pieces.shape), axes)


def shift(array, d, n):
    return lax.ppermute(array, "col", [(i, (i + d) % n) for i in range(n)])


def nought(array):
    one = array[(0,) * array.ndim]
    return (one != one).astype(jnp.int32)


def once(arrays, others):
    count = len(arrays)
    return pl.pallas_call(
        lambda *refs: None,
        out_shape=[jax.ShapeDtypeStruct(array.shape, array.dtype) for array in arrays],
        in_specs=[ANY] * (count + len(others)),
        out_specs=[ANY] * count,
        input_output_aliases={i: i for i in range(count)},
    )(*arrays, *others)


def per_device(child_front, child_pattern, block_map, parent_front, parent_pattern):
    nr, nx, nc = lax.axis_size("row"), lax.axis_size("col"), lax.axis_size("cube")
    r, x, c = lax.axis_index("row"), lax.axis_index("col"), lax.axis_index("cube")
    local = child_front.shape[1] // NB
    slots = parent_front.shape[0] // NB
    height = NB // nx
    octets = height // 8
    holders = nc * nr
    front = child_front[0]
    pattern = child_pattern[0]

    place = jnp.stack([(x - d) % nx for d in range(nx)] + [x * octets + r]).astype(jnp.int32)
    square = block_shape
    half = lambda *shape: jax.ShapeDtypeStruct(shape, bf16)

    corner = front[:NB, :NB].reshape(nr * nx, 1, 8, NB)
    pieces = exchange(corner, ("row", "col"))[:, 0]
    lines = [pieces[i * nx : i * nx + i + 1] for i in range(K)] + [pieces[K * nx : 2 * K * nx]]
    lines = jnp.concatenate(lines, axis=0)
    begun = nought(pieces)
    lines = jnp.stack([lines] + [shift(lines, d, nx) for d in range(1, nx)])
    lines = jnp.take(lines, (x - jnp.arange(nx)) % nx, axis=0, mode="clip")
    lines = lines.transpose(1, 0, 2, 3).reshape(-1, nx * 8, NB)
    part_one = gather_pieces(lines[:3], ("row",), nr)
    lower = lax.all_gather(lines[10:], "row")

    tables = block_map.reshape(nc, local, nr).transpose(0, 2, 1)
    live = tables >= 0
    cubes = jnp.where(live, tables % holders // nr, -1)
    places = jnp.where(live, tables // holders, -1)
    members = jnp.where(live, tables % nr, -1)
    mine = tables[c, r]
    spot = jnp.where(mine >= 0, cubes[c, r] * slots + places[c, r], -1)
    spot = jnp.where(spot >= 0, spot, local * (local - 1) // 2 - jnp.sum(jnp.maximum(spot, 0)))
    lead = jnp.sum(jnp.where(spot == 0, jnp.arange(local), 0))
    block_row = jnp.arange(local) * nr + r
    kept_rows = jnp.where(
        block_row[:, None] > jnp.arange(K)[None], jnp.take(pattern, block_row, axis=0, mode="clip"), 0
    )
    row_info = jnp.concatenate(
        [block_row[:, None], kept_rows, spot[:, None], jnp.full((local, 1), lead)], axis=1
    ).astype(jnp.int32)

    quarters = front.reshape(local, nx, height, -1)
    ahead = lax.dynamic_index_in_dim(quarters, lead, axis=0, keepdims=False)
    ahead = ahead.reshape(nx, height, 2, NB).transpose(0, 2, 1, 3)
    own = parent_front.reshape(slots, nx, height, NB).transpose(1, 0, 2, 3)
    ahead = jnp.concatenate([ahead, own], axis=1)
    ahead = ahead.reshape(nx, -1, NB)
    early = [lax.dynamic_index_in_dim(ahead, (x + d + begun) % nx, axis=0, keepdims=False) for d in range(nx)]
    early = early[:1] + [shift(early[d], d, nx) for d in range(1, nx)]
    sent = [lax.dynamic_index_in_dim(quarters, (x + d + begun) % nx, axis=1, keepdims=False) for d in range(1, nx)]
    spread = lambda blocks: jnp.broadcast_to(blocks[None], (nr,) + blocks.shape)
    ready = [spread(lines[3:10]), early[0], row_info]
    *sent, sent_two, first, row_info = once(sent + ready, [part_one, *early[1:]])
    early[0] = first
    parts = [shift(part, d + 1, nx) for d, part in enumerate(sent)]

    def panels():
        part_two = exchange(sent_two, ("row",))
        g01, h01, l1 = call(
            first_kernel,
            [square(2), square(2), square(1)],
            in_specs=[SMEM, VMEM],
            out_specs=[VMEM] * 3,
            scratch_shapes=FACTOR_SCRATCH,
        )(pattern[: 2 * K], part_one)
        g2, h2, l2, own = call(
            functools.partial(own_kernel, functools.partial(later_kernel, 2, 0)),
            [square(1), square(1), square(2), jax.ShapeDtypeStruct((octets, slots, 8, nx * NB), f32)],
            in_specs=[SMEM] + [VMEM] * 4 + [SMEM] + [VMEM] * 3,
            out_specs=[VMEM] * 4,
            scratch_shapes=FACTOR_SCRATCH,
        )(place, *early, pattern[: 2 * K], part_two, h01, l1)
        own = exchange(own, ("row",))
        g3, h3, l3 = call(
            functools.partial(later_kernel, 3, 3),
            [square(1), square(1), square(3)],
            in_specs=[SMEM] + [VMEM] * 5,
            out_specs=[VMEM] * 3,
            scratch_shapes=FACTOR_SCRATCH,
        )(pattern[: 2 * K], part_two, h01, h2, l1, l2)

        return own, g01, g2, g3, h01, h2, h3, l1, l2, l3

    empty = jax.tree.map(lambda leaf: jnp.zeros(leaf.shape, leaf.dtype), jax.eval_shape(panels))
    own, g01, g2, g3, h01, h2, h3, l1, l2, l3 = lax.cond(nought(part_one) == 0, panels, lambda: empty)

    *weights, top = call(
        lead_kernel,
        [half(K, NB, NB)] * 2
        + [half(6, NB, NB)] * 2
        + [half(K * NB, K * NB)] * 2
        + [jax.ShapeDtypeStruct((nc, octets, 2, 8, 128), f32)],
        in_specs=[SMEM] * 3 + [VMEM] * 11,
        out_specs=[VMEM] * 7,
        scratch_shapes=[pltpu.VMEM((nx, 3, height, NB), f32)],
    )(row_info, place, pattern[: 2 * K], lower, h01, h2, h3, l1, l2, l3, *early)
    (top,) = once([top], [*parts, own])
    top = exchange(top.reshape(holders, 2, 8, 128), ("cube", "row"))
    top_row = jnp.max(jnp.where((cubes == 0) & (places == 0), members, -1), axis=-1).reshape(holders)
    chosen = top_row[None, :] == jnp.arange(4)[:, None]
    top = top[:4, 1] + jnp.sum(jnp.where(chosen[:, :, None, None], top[None, :, 0], 0.0), axis=1)

    full = lambda a: pl.BlockSpec(a.shape, lambda i, n=a.ndim: (0,) * n)
    buffer = pltpu.VMEM((2, nx, slots, height, 2 * NB), f32)
    count = local // 2
    some_rows = jax.ShapeDtypeStruct((count,) + parts[0].shape[1:], f32)
    all_rows = jax.ShapeDtypeStruct(parts[0].shape, f32)
    wide = jax.ShapeDtypeStruct((nc * octets, slots, 8, nx * NB), f32)
    operands = (row_info, place, quarters, *parts, g01, g2, g3, *weights)

    def rows(begin, *extra):
        return call(
            functools.partial(rows_kernel, begin),
            [jax.ShapeDtypeStruct(quarters.shape, f32), some_rows, all_rows, some_rows, wide],
            grid=(count // slots,),
            in_specs=[SMEM] * 2 + [ANY] * 4 + [full(a) for a in operands[6:]] + [ANY] * len(extra),
            out_specs=[ANY] * 5,
            scratch_shapes=[buffer, buffer, pltpu.VMEM((2, slots, octets, 8, nx * NB), f32)]
            + [pltpu.SemaphoreType.DMA((2,))] * 3,
            input_output_aliases={len(operands) + i: out for i, out in enumerate((0, 2, 4))} if extra else {},
        )(*operands, *extra)

    child_out, one, both, three, extend = rows(0)
    (top,) = once([top], [extend])
    top_sent = jnp.broadcast_to(top[None], (nc * nr * nx,) + top.shape)
    top = exchange(top_sent, ("cube", "row", "col")).reshape(nc, nr, nx, 4, 8, 128)
    back = [(1, 0, one), (3, 0, three)]
    child_out, one, both, three, extend = rows(count, child_out, both, extend, top_sent)
    back += [(2, 0, both), (1, count, one), (3, count, three)]
    extend = exchange(extend, ("cube", "row"))

    g_parent, *parent_weights = call(
        parent_kernel,
        [square(2)] + [half(2, NB, NB)] * 2 + [half(5, NB, NB)] * 2,
        in_specs=[SMEM, VMEM],
        out_specs=[VMEM] * 5,
        scratch_shapes=FACTOR_SCRATCH,
    )(parent_pattern[:4], top)

    def parent_info(block_row):
        flags = jnp.take(parent_pattern, block_row, axis=0, mode="clip")
        flags = jnp.where(block_row[:, None] > jnp.arange(KP)[None], flags, 0)
        return jnp.concatenate([block_row[:, None], flags], axis=1).astype(jnp.int32)

    slot_row = jnp.arange(slots) * holders + c * nr
    here = (cubes == c)[:, :, None, :] & (places[:, :, None, :] == jnp.arange(slots)[None, None, :, None])
    target = jnp.max(jnp.where(here, members[:, :, None, :], -1), axis=-1).reshape(holders, slots)
    result = call(
        parent_rows_kernel,
        jax.ShapeDtypeStruct((nr, nx, slots, 8, NB), f32),
        in_specs=[SMEM] * 3 + [VMEM] * 7,
        out_specs=VMEM,
        scratch_shapes=[pltpu.VMEM((slots, nr, 8, nx * NB), f32)],
    )(
        parent_info((slot_row[:, None] + jnp.arange(nr)[None, :]).reshape(-1)),
        place,
        target.astype(jnp.int32),
        extend,
        own,
        g_parent,
        *parent_weights,
    )
    late = x + nought(result)
    for d, begin, some in back:
        part = shift(some, -d, nx)[:, None]
        child_out = lax.dynamic_update_slice(child_out, part, (begin, (late + d) % nx, 0, 0))
    child_out = child_out.reshape(child_front.shape)
    result = exchange(result.reshape(nr * nx, slots, 8, NB), ("row", "col"))
    result = result.reshape(nr, nx, slots, 8, NB).transpose(2, 1, 0, 3, 4).reshape(parent_front.shape)
    return child_out, result


def solution(mesh):
    placed = (P("cube", "row", "col"), P("cube", None, None), P(), P(("cube", "row"), "col"), P())
    return jax.shard_map(
        per_device,
        mesh=mesh,
        in_specs=placed,
        out_specs=(P("cube", "row", "col"), P(("cube", "row"), "col")),
        check_vma=False,
    )
```

```python
import functools

import jax
import jax.numpy as jnp
from jax import lax
from jax.experimental import pallas as pl
from jax.experimental.pallas import tpu as pltpu
from jax.sharding import PartitionSpec as P

NB = 256
K = 4
KP = 2
PB = 64

f32, bf16 = jnp.float32, jnp.bfloat16


def dims(a, b):
    return (((a,), (b,)), ((), ()))


NN, NT, TN = dims(1, 0), dims(1, 1), dims(0, 0)


def split(x):
    high = x.astype(bf16)
    return high, (x - high.astype(f32)).astype(bf16)


def dot3(x, y, d):
    xh, xl = x
    yh, yl = y
    part = lambda p, q: lax.dot_general(p, q, d, preferred_element_type=f32)
    return part(xh, yh) + (part(xh, yl) + part(xl, yh))


def small_factor(t):
    count = PB // 8
    tiles = [t[8 * i : 8 * i + 8] for i in range(count)]
    full = (8, 128)
    sub = lax.broadcasted_iota(jnp.int32, full, 0)
    for s in range(count):
        c0 = PB + 8 * s
        cols = [
            [jnp.broadcast_to(tiles[q][:, c0 + k : c0 + k + 1], full) for k in range(8)]
            for q in range(s, count)
        ]
        a = [
            [jnp.broadcast_to(cols[0][k][i : i + 1], full) if i >= k else None for k in range(8)]
            for i in range(8)
        ]
        rows = [jnp.broadcast_to(tiles[s][k : k + 1], full) for k in range(8)]
        mults = [[] for _ in range(s, count)]
        scale = None
        for k in range(8):
            r = 1.0 / a[k][k]
            root = lax.rsqrt(a[k][k])
            scale = root if k == 0 else jnp.where(sub == k, root, scale)
            m = [a[i][k] * r if i > k else None for i in range(8)]
            for q in range(count - s):
                mult = cols[q][k] * r
                if q == 0:
                    mult = jnp.where(sub > k, mult, 0.0)
                mults[q].append(mult)
            for i in range(k + 1, 8):
                rows[i] = rows[i] - m[i] * rows[k]
                for q in range(count - s):
                    cols[q][i] = cols[q][i] - mults[q][k] * a[i][k]
                for j in range(k + 1, i + 1):
                    a[i][j] = a[i][j] - m[i] * a[j][k]
        for q in range(count - s):
            acc = tiles[s + q]
            for k in range(8):
                acc = acc - mults[q][k] * rows[k]
            tiles[s + q] = acc
        tiles[s] = tiles[s] * scale
    return jnp.concatenate(tiles, axis=0)


def factor(block, work, out):
    row = lax.broadcasted_iota(jnp.int32, (NB, NB), 0)
    lane = lax.broadcasted_iota(jnp.int32, (NB, NB), 1)
    low = jnp.where(row >= lane, block, 0.0)
    work[:, :NB] = low + jnp.where(row > lane, block, 0.0).T
    work[:, NB:] = jnp.where(row == lane, 1.0, 0.0)
    lane_of = lax.broadcasted_iota(jnp.int32, (PB, 128), 1)
    row_of = lax.broadcasted_iota(jnp.int32, (PB, 128), 0)
    wide_lane = lax.broadcasted_iota(jnp.int32, (PB, NB), 1)

    def body(p, _):
        base = pl.multiple_of(p * PB, PB)
        slab = work[pl.ds(base, PB), :]
        turned = pltpu.roll(slab[:, :NB], jnp.where(p == 0, PB, NB + PB - base), 1)[:, :128]
        unit = jnp.where(lane_of == row_of, 1.0, 0.0)
        t = jnp.where((lane_of >= PB) & (lane_of < 2 * PB), turned, unit)
        j = small_factor(t)[:, :PB]
        u = dot3(split(j), split(slab), NN)
        out[pl.ds(base, PB), :] = u
        uh, ul = split(u)
        keep = wide_lane >= base + PB
        zero = jnp.zeros((PB, NB), bf16)
        left = (jnp.where(keep, uh[:, :NB], zero), jnp.where(keep, ul[:, :NB], zero))
        work[...] -= dot3(left, (uh, ul), TN)
        return 0

    lax.fori_loop(0, NB // PB, body, 0)
    g = jnp.where(lane >= row, out[:, :NB], 0.0).T
    return g, out[:, NB:]


FACTOR_SCRATCH = [pltpu.VMEM((NB, 2 * NB), f32), pltpu.VMEM((NB, 2 * NB), f32)]


def kept(flag, value):
    return jnp.where(flag != 0, value, 0.0)


def call(kernel, out_shape, **kwargs):
    kwargs.setdefault("compiler_params", pltpu.CompilerParams(vmem_limit_bytes=56 << 20))
    return pl.pallas_call(
        kernel,
        out_shape=out_shape,
        cost_estimate=pl.CostEstimate(flops=1, bytes_accessed=1, transcendentals=0),
        **kwargs,
    )


VMEM = pl.BlockSpec(memory_space=pltpu.VMEM)
SMEM = pl.BlockSpec(memory_space=pltpu.SMEM)
ANY = pl.BlockSpec(memory_space=pl.ANY)


def block_shape(*lead):
    return jax.ShapeDtypeStruct(lead + (NB, NB), f32)


def whole(ref, index):
    return ref[:, index].reshape(NB, NB)


def pair(i, j):
    return i * (i - 1) // 2 + j


def first_kernel(pattern, piece, g, h, l, work, out):
    g0, h0 = factor(whole(piece, 0), work, out)
    g[0], h[0] = g0, h0
    l10 = kept(pattern[1, 0], dot3(split(whole(piece, 1)), split(h0), NT))
    l[0] = l10
    s10 = split(l10)
    g[1], h[1] = factor(whole(piece, 2) - dot3(s10, s10, NT), work, out)


def own_kernel(later, place, e0, e1, e2, e3, *refs):
    sent = refs[-3]
    octets, slots = sent.shape[0], sent.shape[1]
    height = octets * 8
    base = e0.shape[0] - slots * height
    for d, early in enumerate([e0, e1, e2, e3]):
        lanes = pl.ds(pl.multiple_of(place[d] * NB, NB), NB)
        for s in range(slots):
            sent[:, s, :, lanes] = early[base + s * height : base + (s + 1) * height].reshape(octets, 8, NB)
    later(*refs[:-3], *refs[-2:])


def later_kernel(k, first, pattern, piece, *refs):
    count = k - 1
    h_refs, l_refs = refs[:count], refs[count : 2 * count]
    g, h, l, work, out = refs[2 * count :]
    hs, ls = listed(h_refs), listed(l_refs)
    row = [whole(piece, first + j) for j in range(k + 1)]
    for j in range(k):
        l[j] = kept(pattern[k, j], dot3(split(row[j]), split(hs[j][...]), NT))
        value = split(l[j])
        for i in range(j + 1, k):
            row[i] = row[i] - dot3(value, split(ls[pair(i, j)][...]), NT)
        row[k] = row[k] - dot3(value, value, NT)
    g[0], h[0] = factor(row[k], work, out)


def listed(refs):
    return [ref.at[i] for ref in refs for i in range(ref.shape[0])]


def solve_rows(columns, mask, h, l):
    solved = []
    columns = list(columns)
    for k in range(len(columns)):
        value = mask(k, dot3(split(columns[k]), h(k), NT))
        solved.append(value)
        value = split(value)
        for j in range(k + 1, len(columns)):
            columns[j] = columns[j] - dot3(value, l(j, k), NT)
    return solved


def row_mask(info, first, groups, height):
    def mask(k, value):
        parts = [
            kept(info[first + i, 1 + k], value[i * height : (i + 1) * height]) for i in range(groups)
        ]
        return jnp.concatenate(parts, axis=0) if groups > 1 else parts[0]

    return mask


def lead_kernel(info, place, pattern, lower, h01, h2, h3, l1, l2, l3, e0, e1, e2, e3, *refs):
    hh, hl, lh, ll, ch, cl, top, rows = refs[-8:]
    for k, block in enumerate(listed([h01, h2, h3])):
        hh[k], hl[k] = split(block[...])
    for k, block in enumerate(listed([l1, l2, l3])):
        lh[k], ll[k] = split(block[...])
    h = lambda k: (hh[k], hl[k])
    l = lambda j, k: (lh[pair(j, k)], ll[pair(j, k)])
    columns = [jnp.concatenate([whole(lower, j * K + k) for j in range(K)], axis=0) for k in range(K)]

    def mask(k, value):
        parts = [kept(pattern[K + j, k], value[j * NB : (j + 1) * NB]) for j in range(K)]
        return jnp.concatenate(parts, axis=0)

    solved = solve_rows(columns, mask, h, l)
    for k in range(K):
        ch[:, k * NB : (k + 1) * NB], cl[:, k * NB : (k + 1) * NB] = split(solved[k])
    height = rows.shape[2]
    base = e0.shape[0] - 6 * height
    for d, early in enumerate([e0, e1, e2, e3]):
        rows[place[d]] = early[base : base + 3 * height].reshape(3, height, NB)
    solved = solve_rows([rows[k, 0] for k in range(K)], row_mask(info, info[0, 2 + K], 1, height), h, l)
    update = dot3(split(jnp.concatenate(solved, axis=1)), (ch[: 2 * NB], cl[: 2 * NB]), NT)
    for v in range(K):
        start = v % 2 * 128
        lanes = slice(start, start + 128)
        schur = rows[v // 2, 1, :, lanes] - update[:, v * 128 : v * 128 + 128]
        top[v, :, 0] = schur.reshape(height // 8, 8, 128)
        top[v, :, 1] = rows[v // 2, 2, :, lanes].reshape(height // 8, 8, 128)


def rows_kernel(info, place, front, p1, p2, p3, g01, g2, g3, hh, hl, lh, ll, ch, cl, *refs):
    child, b1, b2, b3, extend, fin, fout, eout, insem, outsem, extsem = refs[-11:]
    step, steps = pl.program_id(0), pl.num_programs(0)
    groups, height = fin.shape[2], fin.shape[3]
    octets = height // 8
    slot = lax.rem(step, 2)

    def load(at, slot):
        for s in range(groups):
            here = at * groups + s
            for d, source in enumerate([front.at[here, place[0]], p1.at[here], p2.at[here], p3.at[here]]):
                pltpu.make_async_copy(source, fin.at[slot, place[d], s], insem.at[slot]).start()

    def store(at, slot):
        for s in range(groups):
            here = at * groups + s
            for d, target in enumerate([child.at[here, place[0]], b1.at[here], b2.at[here], b3.at[here]]):
                pltpu.make_async_copy(fout.at[slot, place[d], s], target, outsem.at[slot]).start()

    def wait(buffer, slot, sem):
        pltpu.make_async_copy(buffer.at[slot], buffer.at[slot], sem.at[slot]).wait()

    @pl.when(step == 0)
    def _():
        load(0, 0)

    @pl.when(step + 1 < steps)
    def _():
        load(step + 1, 1 - slot)

    wait(fin, slot, insem)

    @pl.when(step >= 2)
    def _():
        wait(fout, slot, outsem)
        wait(eout, slot, extsem)

    first = step * groups
    columns = [fin[slot, k, :, :, :NB].reshape(groups * height, NB) for k in range(K)]
    solved = solve_rows(
        columns,
        row_mask(info, first, groups, height),
        lambda k: (hh[k], hl[k]),
        lambda j, k: (lh[pair(j, k)], ll[pair(j, k)]),
    )
    update = dot3(split(jnp.concatenate(solved, axis=1)), (ch[...], cl[...]), NT)
    for k, g in enumerate(listed([g01, g2, g3])):
        fout[slot, k, :, :, :NB] = solved[k].reshape(groups, height, NB)
        schur = fin[slot, k, :, :, NB:].reshape(groups * height, NB) - update[:, k * NB : (k + 1) * NB]
        fout[slot, k, :, :, NB:] = schur.reshape(groups, height, NB)
        eout[slot, :, :, :, k * NB : (k + 1) * NB] = schur.reshape(groups, octets, 8, NB)
        for i in range(groups):

            @pl.when(info[first + i, 0] == k)
            def _():
                mine = pl.ds(pl.multiple_of(place[0] * height, height), height)
                fout[slot, k, i, :, :NB] = g[mine, :]

    store(step, slot)

    def send(i):
        at = info[first + i, 1 + K]
        holder = pl.multiple_of(lax.div(at, groups) * octets, octets)
        target = extend.at[pl.ds(holder, octets), lax.rem(at, groups)]
        return pltpu.make_async_copy(eout.at[slot, i], target, extsem.at[slot])

    for i in range(groups):
        send(i).start()

    @pl.when(step == steps - 1)
    def _():
        for other in range(2):
            wait(fout, other, outsem)
            wait(eout, other, extsem)


def parent_kernel(pattern, top, g, hh, hl, lh, ll, work, out):
    def block(i, j):
        halves = [
            jnp.swapaxes(top[2 * j + v, :, :, i], 0, 1).reshape(NB, 128) for v in range(2)
        ]
        return jnp.concatenate(halves, axis=1)

    g0, h0 = factor(block(0, 0), work, out)
    g[0] = g0
    h0 = split(h0)
    hh[0], hl[0] = h0
    first = []
    for i in range(1, 4):
        value = split(kept(pattern[i, 0], dot3(split(block(i, 0)), h0, NT)))
        lh[i - 1], ll[i - 1] = value
        first.append(value)
    g1, h1 = factor(block(1, 1) - dot3(first[0], first[0], NT), work, out)
    g[1] = g1
    h1 = split(h1)
    hh[1], hl[1] = h1
    for i in range(2, 4):
        rest = block(i, 1) - dot3(first[i - 1], first[0], NT)
        lh[i + 1], ll[i + 1] = split(kept(pattern[i, 1], dot3(split(rest), h1, NT)))


def parent_steps(columns, mask, hh, hl, lh, ll):
    one = mask(0, dot3(split(columns[0]), (hh[0], hl[0]), NT))
    first = split(one)
    two = mask(1, dot3(split(columns[1] - dot3(first, (lh[0], ll[0]), NT)), (hh[1], hl[1]), NT))
    second = split(two)
    results = [one, two]
    for j in range(2, 4):
        left = dot3(first, (lh[j - 1], ll[j - 1]), NT) + dot3(second, (lh[j + 1], ll[j + 1]), NT)
        results.append(columns[j] - left)
    return results


def parent_rows_kernel(info, place, target, extend, own, g, hh, hl, lh, ll, out, acc):
    slots, members = acc.shape[0], acc.shape[1]
    for s in range(slots):
        acc[s] = own[:, s]

    def add(q, _):
        for s in range(slots):
            where = target[q, s]

            @pl.when(where >= 0)
            def _():
                acc[s, where] += extend[q, s]

        return 0

    lax.fori_loop(0, extend.shape[0], add, 0)
    columns = [acc[:, :, :, j * NB : (j + 1) * NB].reshape(slots * members * 8, NB) for j in range(4)]
    results = parent_steps(columns, row_mask(info, 0, slots * members, 8), hh, hl, lh, ll)
    for j in range(4):
        shaped = results[j].reshape(slots, members, 8, NB)
        for s in range(slots):
            out[:, j, s] = shaped[s]
    for k in range(KP):

        @pl.when(info[k, 0] == k)
        def _():
            mine = pl.ds(pl.multiple_of(place[K] * 8, 8), 8)
            out[k, k, 0] = g[k, mine, :]


def exchange(array, axes):
    return lax.all_to_all(array, axes, split_axis=0, concat_axis=0, tiled=True)


def gather_pieces(pieces, axes, count):
    return exchange(jnp.broadcast_to(pieces[None], (count,) + pieces.shape), axes)


def shift(array, d, n):
    return lax.ppermute(array, "col", [(i, (i + d) % n) for i in range(n)])


def nought(array):
    one = array[(0,) * array.ndim]
    return (one != one).astype(jnp.int32)


def once(arrays, others):
    count = len(arrays)
    return pl.pallas_call(
        lambda *refs: None,
        out_shape=[jax.ShapeDtypeStruct(array.shape, array.dtype) for array in arrays],
        in_specs=[ANY] * (count + len(others)),
        out_specs=[ANY] * count,
        input_output_aliases={i: i for i in range(count)},
    )(*arrays, *others)


def per_device(child_front, child_pattern, block_map, parent_front, parent_pattern):
    nr, nx, nc = lax.axis_size("row"), lax.axis_size("col"), lax.axis_size("cube")
    r, x, c = lax.axis_index("row"), lax.axis_index("col"), lax.axis_index("cube")
    local = child_front.shape[1] // NB
    slots = parent_front.shape[0] // NB
    height = NB // nx
    octets = height // 8
    holders = nc * nr
    front = child_front[0]
    pattern = child_pattern[0]

    place = jnp.stack([(x - d) % nx for d in range(nx)] + [x * octets + r]).astype(jnp.int32)
    square = block_shape
    half = lambda *shape: jax.ShapeDtypeStruct(shape, bf16)

    tables = block_map.reshape(nc, local, nr).transpose(0, 2, 1)
    live = tables >= 0
    cubes = jnp.where(live, tables % holders // nr, -1)
    places = jnp.where(live, tables // holders, -1)
    members = jnp.where(live, tables % nr, -1)
    mine = tables[c, r]
    spot = jnp.where(mine >= 0, cubes[c, r] * slots + places[c, r], -1)
    spot = jnp.where(spot >= 0, spot, local * (local - 1) // 2 - jnp.sum(jnp.maximum(spot, 0)))
    lead = jnp.sum(jnp.where(spot == 0, jnp.arange(local), 0))
    block_row = jnp.arange(local) * nr + r
    kept_rows = jnp.where(
        block_row[:, None] > jnp.arange(K)[None], jnp.take(pattern, block_row, axis=0, mode="clip"), 0
    )
    row_info = jnp.concatenate(
        [block_row[:, None], kept_rows, spot[:, None], jnp.full((local, 1), lead)], axis=1
    ).astype(jnp.int32)

    quarters = front.reshape(local, nx, height, -1)
    ahead = lax.dynamic_index_in_dim(quarters, lead, axis=0, keepdims=False)
    ahead = ahead.reshape(nx, height, 2, NB).transpose(0, 2, 1, 3)
    own = parent_front.reshape(slots, nx, height, NB).transpose(1, 0, 2, 3)
    ahead = jnp.concatenate([ahead, own], axis=1)
    ahead = ahead.reshape(nx, -1, NB)

    parent_row = (jnp.arange(slots)[:, None] * holders + c * nr + jnp.arange(nr)[None, :]).reshape(-1)
    flags = jnp.take(parent_pattern, parent_row, axis=0, mode="clip")
    flags = jnp.where(parent_row[:, None] > jnp.arange(KP)[None], flags, 0)
    parent_info = jnp.concatenate([parent_row[:, None], flags], axis=1).astype(jnp.int32)
    here = (cubes == c)[:, :, None, :] & (places[:, :, None, :] == jnp.arange(slots)[None, None, :, None])
    target = jnp.max(jnp.where(here, members[:, :, None, :], -1), axis=-1).reshape(holders, slots)
    target = target.astype(jnp.int32)

    corner = front[:NB, :NB].reshape(nr * nx, 1, 8, NB)
    pieces = exchange(corner, ("row", "col"))[:, 0]
    lines = [pieces[i * nx : i * nx + i + 1] for i in range(K)] + [pieces[K * nx : 2 * K * nx]]
    lines = jnp.concatenate(lines, axis=0)
    early = [lax.dynamic_index_in_dim(ahead, (x + d) % nx, axis=0, keepdims=False) for d in range(nx)]
    lines, row_info, *early = once([lines, row_info, *early], [])
    begun = nought(pieces)
    lines = jnp.stack([lines] + [shift(lines, d, nx) for d in range(1, nx)])
    lines = jnp.take(lines, (x - jnp.arange(nx)) % nx, axis=0, mode="clip")
    lines = lines.transpose(1, 0, 2, 3).reshape(-1, nx * 8, NB)
    part_one = gather_pieces(lines[:3], ("row",), nr)
    lower = lax.all_gather(lines[10:], "row")

    early = early[:1] + [shift(early[d], d, nx) for d in range(1, nx)]
    sent = [lax.dynamic_index_in_dim(quarters, (x + d + begun) % nx, axis=1, keepdims=False) for d in range(1, nx)]
    spread = lambda blocks: jnp.broadcast_to(blocks[None], (nr,) + blocks.shape)
    ready = [spread(lines[3:10]), place, pattern[: 2 * K], parent_pattern[:4], parent_info, target]
    *sent, sent_two, place, lead_pattern, top_pattern, parent_info, target = once(
        sent + ready, [part_one, *early[1:]]
    )
    parts = [shift(part, d + 1, nx) for d, part in enumerate(sent)]

    def panels():
        part_two = exchange(sent_two, ("row",))
        g01, h01, l1 = call(
            first_kernel,
            [square(2), square(2), square(1)],
            in_specs=[SMEM, VMEM],
            out_specs=[VMEM] * 3,
            scratch_shapes=FACTOR_SCRATCH,
        )(lead_pattern, part_one)
        g2, h2, l2, own = call(
            functools.partial(own_kernel, functools.partial(later_kernel, 2, 0)),
            [square(1), square(1), square(2), jax.ShapeDtypeStruct((octets, slots, 8, nx * NB), f32)],
            in_specs=[SMEM] + [VMEM] * 4 + [SMEM] + [VMEM] * 3,
            out_specs=[VMEM] * 4,
            scratch_shapes=FACTOR_SCRATCH,
        )(place, *early, lead_pattern, part_two, h01, l1)
        own = exchange(own, ("row",))
        g3, h3, l3 = call(
            functools.partial(later_kernel, 3, 3),
            [square(1), square(1), square(3)],
            in_specs=[SMEM] + [VMEM] * 5,
            out_specs=[VMEM] * 3,
            scratch_shapes=FACTOR_SCRATCH,
        )(lead_pattern, part_two, h01, h2, l1, l2)

        return own, g01, g2, g3, h01, h2, h3, l1, l2, l3

    empty = jax.tree.map(lambda leaf: jnp.zeros(leaf.shape, leaf.dtype), jax.eval_shape(panels))
    own, g01, g2, g3, h01, h2, h3, l1, l2, l3 = lax.cond(nought(part_one) == 0, panels, lambda: empty)

    *weights, top = call(
        lead_kernel,
        [half(K, NB, NB)] * 2
        + [half(6, NB, NB)] * 2
        + [half(K * NB, K * NB)] * 2
        + [jax.ShapeDtypeStruct((nc, octets, 2, 8, 128), f32)],
        in_specs=[SMEM] * 3 + [VMEM] * 11,
        out_specs=[VMEM] * 7,
        scratch_shapes=[pltpu.VMEM((nx, 3, height, NB), f32)],
    )(row_info, place, lead_pattern, lower, h01, h2, h3, l1, l2, l3, *early)
    (top,) = once([top], [*parts, own])
    top = exchange(top.reshape(holders, 2, 8, 128), ("cube", "row"))
    top_row = jnp.max(jnp.where((cubes == 0) & (places == 0), members, -1), axis=-1).reshape(holders)
    chosen = top_row[None, :] == jnp.arange(4)[:, None]
    top = top[:4, 1] + jnp.sum(jnp.where(chosen[:, :, None, None], top[None, :, 0], 0.0), axis=1)

    top_sent = jnp.broadcast_to(top[None], (nc * nr * nx,) + top.shape)
    top = exchange(top_sent, ("cube", "row", "col")).reshape(nc, nr, nx, 4, 8, 128)

    full = lambda a: pl.BlockSpec(a.shape, lambda i, n=a.ndim: (0,) * n)
    buffer = pltpu.VMEM((2, nx, slots, height, 2 * NB), f32)
    wide = jax.ShapeDtypeStruct((nc * octets, slots, 8, nx * NB), f32)
    child_out, *back, extend = call(
        rows_kernel,
        [jax.ShapeDtypeStruct(quarters.shape, f32), *[jax.ShapeDtypeStruct(parts[0].shape, f32)] * 3, wide],
        grid=(local // slots,),
        in_specs=[SMEM] * 2 + [ANY] * 4 + [full(a) for a in (g01, g2, g3, *weights)] + [ANY],
        out_specs=[ANY] * 5,
        scratch_shapes=[buffer, buffer, pltpu.VMEM((2, slots, octets, 8, nx * NB), f32)]
        + [pltpu.SemaphoreType.DMA((2,))] * 3,
    )(row_info, place, quarters, *parts, g01, g2, g3, *weights, top_sent)
    extend = exchange(extend, ("cube", "row"))

    g_parent, *parent_weights = call(
        parent_kernel,
        [square(2)] + [half(2, NB, NB)] * 2 + [half(5, NB, NB)] * 2,
        in_specs=[SMEM, VMEM],
        out_specs=[VMEM] * 5,
        scratch_shapes=FACTOR_SCRATCH,
    )(top_pattern, top)

    result = call(
        parent_rows_kernel,
        jax.ShapeDtypeStruct((nr, nx, slots, 8, NB), f32),
        in_specs=[SMEM] * 3 + [VMEM] * 7,
        out_specs=VMEM,
        scratch_shapes=[pltpu.VMEM((slots, nr, 8, nx * NB), f32)],
    )(
        parent_info,
        place,
        target,
        extend,
        own,
        g_parent,
        *parent_weights,
    )
    late = x + nought(result)
    for d in range(1, nx):
        part = shift(back[d - 1], -d, nx)[:, None]
        child_out = lax.dynamic_update_slice(child_out, part, (0, (late + d) % nx, 0, 0))
    child_out = child_out.reshape(child_front.shape)
    result = exchange(result.reshape(nr * nx, slots, 8, NB), ("row", "col"))
    result = result.reshape(nr, nx, slots, 8, NB).transpose(2, 1, 0, 3, 4).reshape(parent_front.shape)
    return child_out, result


def solution(mesh):
    placed = (P("cube", "row", "col"), P("cube", None, None), P(), P(("cube", "row"), "col"), P())
    return jax.shard_map(
        per_device,
        mesh=mesh,
        in_specs=placed,
        out_specs=(P("cube", "row", "col"), P(("cube", "row"), "col")),
        check_vma=False,
    )
```

```python
import functools

import jax
import jax.numpy as jnp
from jax import lax
from jax.experimental import pallas as pl
from jax.experimental.pallas import tpu as pltpu
from jax.sharding import PartitionSpec as P

NB = 256
K = 4
KP = 2
PB = 64

f32, bf16 = jnp.float32, jnp.bfloat16


def dims(a, b):
    return (((a,), (b,)), ((), ()))


NN, NT, TN = dims(1, 0), dims(1, 1), dims(0, 0)


def split(x):
    high = x.astype(bf16)
    return high, (x - high.astype(f32)).astype(bf16)


def dot3(x, y, d):
    xh, xl = x
    yh, yl = y
    part = lambda p, q: lax.dot_general(p, q, d, preferred_element_type=f32)
    return part(xh, yh) + (part(xh, yl) + part(xl, yh))


def small_factor(t):
    count = PB // 8
    tiles = [t[8 * i : 8 * i + 8] for i in range(count)]
    full = (8, 128)
    sub = lax.broadcasted_iota(jnp.int32, full, 0)
    for s in range(count):
        c0 = PB + 8 * s
        cols = [
            [jnp.broadcast_to(tiles[q][:, c0 + k : c0 + k + 1], full) for k in range(8)]
            for q in range(s, count)
        ]
        a = [
            [jnp.broadcast_to(cols[0][k][i : i + 1], full) if i >= k else None for k in range(8)]
            for i in range(8)
        ]
        rows = [jnp.broadcast_to(tiles[s][k : k + 1], full) for k in range(8)]
        mults = [[] for _ in range(s, count)]
        scale = None
        for k in range(8):
            r = 1.0 / a[k][k]
            root = lax.rsqrt(a[k][k])
            scale = root if k == 0 else jnp.where(sub == k, root, scale)
            m = [a[i][k] * r if i > k else None for i in range(8)]
            for q in range(count - s):
                mult = cols[q][k] * r
                if q == 0:
                    mult = jnp.where(sub > k, mult, 0.0)
                mults[q].append(mult)
            for i in range(k + 1, 8):
                rows[i] = rows[i] - m[i] * rows[k]
                for q in range(count - s):
                    cols[q][i] = cols[q][i] - mults[q][k] * a[i][k]
                for j in range(k + 1, i + 1):
                    a[i][j] = a[i][j] - m[i] * a[j][k]
        for q in range(count - s):
            acc = tiles[s + q]
            for k in range(8):
                acc = acc - mults[q][k] * rows[k]
            tiles[s + q] = acc
        tiles[s] = tiles[s] * scale
    return jnp.concatenate(tiles, axis=0)


def factor(block, work, out):
    row = lax.broadcasted_iota(jnp.int32, (NB, NB), 0)
    lane = lax.broadcasted_iota(jnp.int32, (NB, NB), 1)
    low = jnp.where(row >= lane, block, 0.0)
    work[:, :NB] = low + jnp.where(row > lane, block, 0.0).T
    work[:, NB:] = jnp.where(row == lane, 1.0, 0.0)
    lane_of = lax.broadcasted_iota(jnp.int32, (PB, 128), 1)
    row_of = lax.broadcasted_iota(jnp.int32, (PB, 128), 0)
    wide_lane = lax.broadcasted_iota(jnp.int32, (PB, NB), 1)

    def body(p, _):
        base = pl.multiple_of(p * PB, PB)
        slab = work[pl.ds(base, PB), :]
        turned = pltpu.roll(slab[:, :NB], jnp.where(p == 0, PB, NB + PB - base), 1)[:, :128]
        unit = jnp.where(lane_of == row_of, 1.0, 0.0)
        t = jnp.where((lane_of >= PB) & (lane_of < 2 * PB), turned, unit)
        j = small_factor(t)[:, :PB]
        u = dot3(split(j), split(slab), NN)
        out[pl.ds(base, PB), :] = u
        uh, ul = split(u)
        keep = wide_lane >= base + PB
        zero = jnp.zeros((PB, NB), bf16)
        left = (jnp.where(keep, uh[:, :NB], zero), jnp.where(keep, ul[:, :NB], zero))
        work[...] -= dot3(left, (uh, ul), TN)
        return 0

    lax.fori_loop(0, NB // PB, body, 0)
    g = jnp.where(lane >= row, out[:, :NB], 0.0).T
    return g, out[:, NB:]


FACTOR_SCRATCH = [pltpu.VMEM((NB, 2 * NB), f32), pltpu.VMEM((NB, 2 * NB), f32)]


def kept(flag, value):
    return jnp.where(flag != 0, value, 0.0)


def call(kernel, out_shape, **kwargs):
    kwargs.setdefault("compiler_params", pltpu.CompilerParams(vmem_limit_bytes=56 << 20))
    return pl.pallas_call(
        kernel,
        out_shape=out_shape,
        cost_estimate=pl.CostEstimate(flops=1, bytes_accessed=1, transcendentals=0),
        **kwargs,
    )


VMEM = pl.BlockSpec(memory_space=pltpu.VMEM)
SMEM = pl.BlockSpec(memory_space=pltpu.SMEM)
ANY = pl.BlockSpec(memory_space=pl.ANY)


def block_shape(*lead):
    return jax.ShapeDtypeStruct(lead + (NB, NB), f32)


def whole(ref, index):
    return ref[:, index].reshape(NB, NB)


def pair(i, j):
    return i * (i - 1) // 2 + j


def first_kernel(pattern, piece, g, h, l, work, out):
    g0, h0 = factor(whole(piece, 0), work, out)
    g[0], h[0] = g0, h0
    l10 = kept(pattern[1, 0], dot3(split(whole(piece, 1)), split(h0), NT))
    l[0] = l10
    s10 = split(l10)
    g[1], h[1] = factor(whole(piece, 2) - dot3(s10, s10, NT), work, out)


def later_kernel(k, first, pattern, piece, *refs):
    count = k - 1
    h_refs, l_refs = refs[:count], refs[count : 2 * count]
    g, h, l, work, out = refs[2 * count :]
    hs, ls = listed(h_refs), listed(l_refs)
    row = [whole(piece, first + j) for j in range(k + 1)]
    for j in range(k):
        l[j] = kept(pattern[k, j], dot3(split(row[j]), split(hs[j][...]), NT))
        value = split(l[j])
        for i in range(j + 1, k):
            row[i] = row[i] - dot3(value, split(ls[pair(i, j)][...]), NT)
        row[k] = row[k] - dot3(value, value, NT)
    g[0], h[0] = factor(row[k], work, out)


def listed(refs):
    return [ref.at[i] for ref in refs for i in range(ref.shape[0])]


def solve_rows(columns, mask, h, l):
    solved = []
    columns = list(columns)
    for k in range(len(columns)):
        value = mask(k, dot3(split(columns[k]), h(k), NT))
        solved.append(value)
        value = split(value)
        for j in range(k + 1, len(columns)):
            columns[j] = columns[j] - dot3(value, l(j, k), NT)
    return solved


def row_mask(info, first, groups, height):
    def mask(k, value):
        parts = [
            kept(info[first + i, 1 + k], value[i * height : (i + 1) * height]) for i in range(groups)
        ]
        return jnp.concatenate(parts, axis=0) if groups > 1 else parts[0]

    return mask


def lead_kernel(info, place, pattern, lower, h01, h2, h3, l1, l2, l3, own, e0, e1, e2, e3, *refs):
    hh, hl, lh, ll, ch, cl, top, rows = refs[-8:]
    for k, block in enumerate(listed([h01, h2, h3])):
        hh[k], hl[k] = split(block[...])
    for k, block in enumerate(listed([l1, l2, l3])):
        lh[k], ll[k] = split(block[...])
    h = lambda k: (hh[k], hl[k])
    l = lambda j, k: (lh[pair(j, k)], ll[pair(j, k)])
    columns = [jnp.concatenate([whole(lower, j * K + k) for j in range(K)], axis=0) for k in range(K)]

    def mask(k, value):
        parts = [kept(pattern[K + j, k], value[j * NB : (j + 1) * NB]) for j in range(K)]
        return jnp.concatenate(parts, axis=0)

    solved = solve_rows(columns, mask, h, l)
    for k in range(K):
        ch[:, k * NB : (k + 1) * NB], cl[:, k * NB : (k + 1) * NB] = split(solved[k])
    count, height = rows.shape[:2]
    for d, early in enumerate([e0, e1, e2, e3]):
        rows[place[d]] = early[...]
    solved = solve_rows([rows[k, :, :NB] for k in range(K)], row_mask(info, info[0, 2 + K], 1, height), h, l)
    update = dot3(split(jnp.concatenate(solved, axis=1)), (ch[: 2 * NB], cl[: 2 * NB]), NT)
    for v in range(K):
        start = v % 2 * 128
        schur = rows[v // 2, :, NB + start : NB + start + 128] - update[:, v * 128 : v * 128 + 128]
        top[v, :, 0] = schur.reshape(height // 8, 8, 128)
        for t in range(4):
            mine = own[t * count + v // 2, 1, :, start : start + 128]
            top[v, :, 1 + t] = jnp.broadcast_to(mine[None], (height // 8, 8, 128))


def rows_kernel(info, place, front, p1, p2, p3, g01, g2, g3, hh, hl, lh, ll, ch, cl, *refs):
    child, b1, b2, b3, extend, fin, fout, eout, insem, outsem, extsem = refs[-11:]
    step, steps = pl.program_id(0), pl.num_programs(0)
    groups, height = fin.shape[2], fin.shape[3]
    octets = height // 8
    slot = lax.rem(step, 2)

    def load(at, slot):
        for s in range(groups):
            here = at * groups + s
            for d, source in enumerate([front.at[here, place[0]], p1.at[here], p2.at[here], p3.at[here]]):
                pltpu.make_async_copy(source, fin.at[slot, place[d], s], insem.at[slot]).start()

    def store(at, slot):
        for s in range(groups):
            here = at * groups + s
            for d, target in enumerate([child.at[here, place[0]], b1.at[here], b2.at[here], b3.at[here]]):
                pltpu.make_async_copy(fout.at[slot, place[d], s], target, outsem.at[slot]).start()

    def wait(buffer, slot, sem):
        pltpu.make_async_copy(buffer.at[slot], buffer.at[slot], sem.at[slot]).wait()

    @pl.when(step == 0)
    def _():
        load(0, 0)

    @pl.when(step + 1 < steps)
    def _():
        load(step + 1, 1 - slot)

    wait(fin, slot, insem)

    @pl.when(step >= 2)
    def _():
        wait(fout, slot, outsem)
        wait(eout, slot, extsem)

    first = step * groups
    columns = [fin[slot, k, :, :, :NB].reshape(groups * height, NB) for k in range(K)]
    solved = solve_rows(
        columns,
        row_mask(info, first, groups, height),
        lambda k: (hh[k], hl[k]),
        lambda j, k: (lh[pair(j, k)], ll[pair(j, k)]),
    )
    update = dot3(split(jnp.concatenate(solved, axis=1)), (ch[...], cl[...]), NT)
    for k, g in enumerate(listed([g01, g2, g3])):
        fout[slot, k, :, :, :NB] = solved[k].reshape(groups, height, NB)
        schur = fin[slot, k, :, :, NB:].reshape(groups * height, NB) - update[:, k * NB : (k + 1) * NB]
        fout[slot, k, :, :, NB:] = schur.reshape(groups, height, NB)
        eout[slot, :, :, :, k * NB : (k + 1) * NB] = schur.reshape(groups, octets, 8, NB)
        for i in range(groups):

            @pl.when(info[first + i, 0] == k)
            def _():
                mine = pl.ds(pl.multiple_of(place[0] * height, height), height)
                fout[slot, k, i, :, :NB] = g[mine, :]

    store(step, slot)

    def send(i):
        at = info[first + i, 1 + K]
        holder = pl.multiple_of(lax.div(at, groups) * octets, octets)
        target = extend.at[pl.ds(holder, octets), lax.rem(at, groups)]
        return pltpu.make_async_copy(eout.at[slot, i], target, extsem.at[slot])

    for i in range(groups):
        send(i).start()

    @pl.when(step == steps - 1)
    def _():
        for other in range(2):
            wait(fout, other, outsem)
            wait(eout, other, extsem)


def parent_kernel(pattern, top, g, hh, hl, lh, ll, work, out):
    def block(i, j):
        halves = [
            jnp.swapaxes(top[2 * j + v, :, :, i], 0, 1).reshape(NB, 128) for v in range(2)
        ]
        return jnp.concatenate(halves, axis=1)

    g0, h0 = factor(block(0, 0), work, out)
    g[0] = g0
    h0 = split(h0)
    hh[0], hl[0] = h0
    first = []
    for i in range(1, 4):
        value = split(kept(pattern[i, 0], dot3(split(block(i, 0)), h0, NT)))
        lh[i - 1], ll[i - 1] = value
        first.append(value)
    g1, h1 = factor(block(1, 1) - dot3(first[0], first[0], NT), work, out)
    g[1] = g1
    h1 = split(h1)
    hh[1], hl[1] = h1
    for i in range(2, 4):
        rest = block(i, 1) - dot3(first[i - 1], first[0], NT)
        lh[i + 1], ll[i + 1] = split(kept(pattern[i, 1], dot3(split(rest), h1, NT)))


def parent_steps(columns, mask, hh, hl, lh, ll):
    one = mask(0, dot3(split(columns[0]), (hh[0], hl[0]), NT))
    first = split(one)
    two = mask(1, dot3(split(columns[1] - dot3(first, (lh[0], ll[0]), NT)), (hh[1], hl[1]), NT))
    second = split(two)
    results = [one, two]
    for j in range(2, 4):
        left = dot3(first, (lh[j - 1], ll[j - 1]), NT) + dot3(second, (lh[j + 1], ll[j + 1]), NT)
        results.append(columns[j] - left)
    return results


def parent_rows_kernel(info, place, target, extend, own, g, hh, hl, lh, ll, out, acc):
    slots, members = acc.shape[0], acc.shape[1]
    count = own.shape[0] // members
    for s in range(slots):
        for i in range(members):
            for j in range(count):
                acc[s, i, :, j * NB : (j + 1) * NB] = own[i * count + j, 1 + s]

    def add(q, _):
        for s in range(slots):
            where = target[q, s]

            @pl.when(where >= 0)
            def _():
                acc[s, where] += extend[q, s]

        return 0

    lax.fori_loop(0, extend.shape[0], add, 0)
    columns = [acc[:, :, :, j * NB : (j + 1) * NB].reshape(slots * members * 8, NB) for j in range(4)]
    results = parent_steps(columns, row_mask(info, 0, slots * members, 8), hh, hl, lh, ll)
    for j in range(4):
        shaped = results[j].reshape(slots, members, 8, NB)
        for s in range(slots):
            out[:, j, s] = shaped[s]
    for k in range(KP):

        @pl.when(info[k, 0] == k)
        def _():
            mine = pl.ds(pl.multiple_of(place[K] * 8, 8), 8)
            out[k, k, 0] = g[k, mine, :]


def exchange(array, axes):
    return lax.all_to_all(array, axes, split_axis=0, concat_axis=0, tiled=True)


def gather_pieces(pieces, axes, count):
    return exchange(jnp.broadcast_to(pieces[None], (count,) + pieces.shape), axes)


def shift(array, d, n):
    return lax.ppermute(array, "col", [(i, (i + d) % n) for i in range(n)])


def nought(array):
    one = array[(0,) * array.ndim]
    return (one != one).astype(jnp.int32)


def once(arrays, others):
    count = len(arrays)
    return pl.pallas_call(
        lambda *refs: None,
        out_shape=[jax.ShapeDtypeStruct(array.shape, array.dtype) for array in arrays],
        in_specs=[ANY] * (count + len(others)),
        out_specs=[ANY] * count,
        input_output_aliases={i: i for i in range(count)},
    )(*arrays, *others)


def per_device(child_front, child_pattern, block_map, parent_front, parent_pattern):
    nr, nx, nc = lax.axis_size("row"), lax.axis_size("col"), lax.axis_size("cube")
    r, x, c = lax.axis_index("row"), lax.axis_index("col"), lax.axis_index("cube")
    local = child_front.shape[1] // NB
    slots = parent_front.shape[0] // NB
    height = NB // nx
    octets = height // 8
    holders = nc * nr
    front = child_front[0]
    pattern = child_pattern[0]

    place = jnp.stack([(x - d) % nx for d in range(nx)] + [x * octets + r]).astype(jnp.int32)
    square = block_shape
    half = lambda *shape: jax.ShapeDtypeStruct(shape, bf16)

    tables = block_map.reshape(nc, local, nr).transpose(0, 2, 1)
    live = tables >= 0
    cubes = jnp.where(live, tables % holders // nr, -1)
    places = jnp.where(live, tables // holders, -1)
    members = jnp.where(live, tables % nr, -1)
    mine = tables[c, r]
    spot = jnp.where(mine >= 0, cubes[c, r] * slots + places[c, r], -1)
    spot = jnp.where(spot >= 0, spot, local * (local - 1) // 2 - jnp.sum(jnp.maximum(spot, 0)))
    lead = jnp.sum(jnp.where(spot == 0, jnp.arange(local), 0))
    block_row = jnp.arange(local) * nr + r
    kept_rows = jnp.where(
        block_row[:, None] > jnp.arange(K)[None], jnp.take(pattern, block_row, axis=0, mode="clip"), 0
    )
    row_info = jnp.concatenate(
        [block_row[:, None], kept_rows, spot[:, None], jnp.full((local, 1), lead)], axis=1
    ).astype(jnp.int32)

    quarters = front.reshape(local, nx, height, -1)
    ahead = lax.dynamic_index_in_dim(quarters, lead, axis=0, keepdims=False)

    parent_row = (jnp.arange(slots)[:, None] * holders + c * nr + jnp.arange(nr)[None, :]).reshape(-1)
    flags = jnp.take(parent_pattern, parent_row, axis=0, mode="clip")
    flags = jnp.where(parent_row[:, None] > jnp.arange(KP)[None], flags, 0)
    parent_info = jnp.concatenate([parent_row[:, None], flags], axis=1).astype(jnp.int32)
    here = (cubes == c)[:, :, None, :] & (places[:, :, None, :] == jnp.arange(slots)[None, None, :, None])
    target = jnp.max(jnp.where(here, members[:, :, None, :], -1), axis=-1).reshape(holders, slots)
    target = target.astype(jnp.int32)

    corner = front[:NB, :NB].reshape(nr * nx, 1, 8, NB)
    own = parent_front.reshape(slots, nx, octets, 8, NB).transpose(2, 1, 0, 3, 4).reshape(nr * nx, slots, 8, NB)
    own = exchange(jnp.concatenate([corner, own], axis=1), ("row", "col"))
    pieces = own[:, 0]
    lines = [pieces[i * nx : i * nx + i + 1] for i in range(K)] + [pieces[K * nx : 2 * K * nx]]
    lines = jnp.concatenate(lines, axis=0)
    early = [lax.dynamic_index_in_dim(ahead, (x + d) % nx, axis=0, keepdims=False) for d in range(nx)]
    lines, row_info, *early = once([lines, row_info, *early], [])
    begun = nought(lines)
    lines = jnp.stack([lines] + [shift(lines, d, nx) for d in range(1, nx)])
    lines = jnp.take(lines, (x - jnp.arange(nx)) % nx, axis=0, mode="clip")
    lines = lines.transpose(1, 0, 2, 3).reshape(-1, nx * 8, NB)
    square_parts = gather_pieces(lines[:10], ("row",), nr)
    lower = lax.all_gather(lines[10:], "row")
    early = early[:1] + [shift(early[d], d, nx) for d in range(1, nx)]
    sent = [lax.dynamic_index_in_dim(quarters, (x + d + begun) % nx, axis=1, keepdims=False) for d in range(1, nx)]
    ready = [place, pattern[: 2 * K], parent_pattern[:4], parent_info, target]
    *sent, place, lead_pattern, top_pattern, parent_info, target = once(sent + ready, early[1:])
    parts = [shift(part, d + 1, nx) for d, part in enumerate(sent)]

    def panels():
        g01, h01, l1 = call(
            first_kernel,
            [square(2), square(2), square(1)],
            in_specs=[SMEM, VMEM],
            out_specs=[VMEM] * 3,
            scratch_shapes=FACTOR_SCRATCH,
        )(lead_pattern, square_parts)
        g2, h2, l2 = call(
            functools.partial(later_kernel, 2, 3),
            [square(1), square(1), square(2)],
            in_specs=[SMEM] + [VMEM] * 3,
            out_specs=[VMEM] * 3,
            scratch_shapes=FACTOR_SCRATCH,
        )(lead_pattern, square_parts, h01, l1)
        g3, h3, l3 = call(
            functools.partial(later_kernel, 3, 6),
            [square(1), square(1), square(3)],
            in_specs=[SMEM] + [VMEM] * 5,
            out_specs=[VMEM] * 3,
            scratch_shapes=FACTOR_SCRATCH,
        )(lead_pattern, square_parts, h01, h2, l1, l2)
        return g01, g2, g3, h01, h2, h3, l1, l2, l3

    empty = jax.tree.map(lambda leaf: jnp.zeros(leaf.shape, leaf.dtype), jax.eval_shape(panels))
    g01, g2, g3, h01, h2, h3, l1, l2, l3 = lax.cond(nought(square_parts) == 0, panels, lambda: empty)

    *weights, top = call(
        lead_kernel,
        [half(K, NB, NB)] * 2
        + [half(6, NB, NB)] * 2
        + [half(K * NB, K * NB)] * 2
        + [jax.ShapeDtypeStruct((nc, octets, 5, 8, 128), f32)],
        in_specs=[SMEM] * 3 + [VMEM] * 12,
        out_specs=[VMEM] * 7,
        scratch_shapes=[pltpu.VMEM((nx, height, 2 * NB), f32)],
    )(row_info, place, lead_pattern, lower, h01, h2, h3, l1, l2, l3, own, *early)
    (top,) = once([top], parts)
    top = exchange(top.reshape(holders, 5, 8, 128), ("cube", "row"))
    top_row = jnp.max(jnp.where((cubes == 0) & (places == 0), members, -1), axis=-1).reshape(holders)
    chosen = top_row[None, :] == jnp.arange(4)[:, None]
    top = lax.dynamic_index_in_dim(top, r, axis=0, keepdims=False)[1:] + jnp.sum(jnp.where(chosen[:, :, None, None], top[None, :, 0], 0.0), axis=1)

    top_sent = jnp.broadcast_to(top[None], (nc * nr * nx,) + top.shape)
    top = exchange(top_sent, ("cube", "row", "col")).reshape(nc, nr, nx, 4, 8, 128)

    full = lambda a: pl.BlockSpec(a.shape, lambda i, n=a.ndim: (0,) * n)
    buffer = pltpu.VMEM((2, nx, slots, height, 2 * NB), f32)
    wide = jax.ShapeDtypeStruct((nc * octets, slots, 8, nx * NB), f32)
    child_out, *back, extend = call(
        rows_kernel,
        [jax.ShapeDtypeStruct(quarters.shape, f32), *[jax.ShapeDtypeStruct(parts[0].shape, f32)] * 3, wide],
        grid=(local // slots,),
        in_specs=[SMEM] * 2 + [ANY] * 4 + [full(a) for a in (g01, g2, g3, *weights)] + [ANY],
        out_specs=[ANY] * 5,
        scratch_shapes=[buffer, buffer, pltpu.VMEM((2, slots, octets, 8, nx * NB), f32)]
        + [pltpu.SemaphoreType.DMA((2,))] * 3,
    )(row_info, place, quarters, *parts, g01, g2, g3, *weights, top_sent)
    extend = exchange(extend, ("cube", "row"))

    g_parent, *parent_weights = call(
        parent_kernel,
        [square(2)] + [half(2, NB, NB)] * 2 + [half(5, NB, NB)] * 2,
        in_specs=[SMEM, VMEM],
        out_specs=[VMEM] * 5,
        scratch_shapes=FACTOR_SCRATCH,
    )(top_pattern, top)

    result = call(
        parent_rows_kernel,
        jax.ShapeDtypeStruct((nr, nx, slots, 8, NB), f32),
        in_specs=[SMEM] * 3 + [VMEM] * 7,
        out_specs=VMEM,
        scratch_shapes=[pltpu.VMEM((slots, nr, 8, nx * NB), f32)],
    )(
        parent_info,
        place,
        target,
        extend,
        own,
        g_parent,
        *parent_weights,
    )
    late = x + nought(result)
    for d in range(1, nx):
        part = shift(back[d - 1], -d, nx)[:, None]
        child_out = lax.dynamic_update_slice(child_out, part, (0, (late + d) % nx, 0, 0))
    child_out = child_out.reshape(child_front.shape)
    result = exchange(result.reshape(nr * nx, slots, 8, NB), ("row", "col"))
    result = result.reshape(nr, nx, slots, 8, NB).transpose(2, 1, 0, 3, 4).reshape(parent_front.shape)
    return child_out, result


def solution(mesh):
    placed = (P("cube", "row", "col"), P("cube", None, None), P(), P(("cube", "row"), "col"), P())
    return jax.shard_map(
        per_device,
        mesh=mesh,
        in_specs=placed,
        out_specs=(P("cube", "row", "col"), P(("cube", "row"), "col")),
        check_vma=False,
    )
```

```python
import functools

import jax
import jax.numpy as jnp
from jax import lax
from jax.experimental import pallas as pl
from jax.experimental.pallas import tpu as pltpu
from jax.sharding import PartitionSpec as P

NB = 256
K = 4
KP = 2
PB = 64

f32, bf16 = jnp.float32, jnp.bfloat16


def dims(a, b):
    return (((a,), (b,)), ((), ()))


NN, NT, TN = dims(1, 0), dims(1, 1), dims(0, 0)


def split(x):
    high = x.astype(bf16)
    return high, (x - high.astype(f32)).astype(bf16)


def dot3(x, y, d):
    xh, xl = x
    yh, yl = y
    part = lambda p, q: lax.dot_general(p, q, d, preferred_element_type=f32)
    return part(xh, yh) + (part(xh, yl) + part(xl, yh))


def small_factor(t):
    count = PB // 8
    tiles = [t[8 * i : 8 * i + 8] for i in range(count)]
    full = (8, 128)
    sub = lax.broadcasted_iota(jnp.int32, full, 0)
    for s in range(count):
        c0 = PB + 8 * s
        cols = [
            [jnp.broadcast_to(tiles[q][:, c0 + k : c0 + k + 1], full) for k in range(8)]
            for q in range(s, count)
        ]
        a = [
            [jnp.broadcast_to(cols[0][k][i : i + 1], full) if i >= k else None for k in range(8)]
            for i in range(8)
        ]
        rows = [jnp.broadcast_to(tiles[s][k : k + 1], full) for k in range(8)]
        mults = [[] for _ in range(s, count)]
        scale = None
        for k in range(8):
            r = 1.0 / a[k][k]
            root = lax.rsqrt(a[k][k])
            scale = root if k == 0 else jnp.where(sub == k, root, scale)
            m = [a[i][k] * r if i > k else None for i in range(8)]
            for q in range(count - s):
                mult = cols[q][k] * r
                if q == 0:
                    mult = jnp.where(sub > k, mult, 0.0)
                mults[q].append(mult)
            for i in range(k + 1, 8):
                rows[i] = rows[i] - m[i] * rows[k]
                for q in range(count - s):
                    cols[q][i] = cols[q][i] - mults[q][k] * a[i][k]
                for j in range(k + 1, i + 1):
                    a[i][j] = a[i][j] - m[i] * a[j][k]
        for q in range(count - s):
            acc = tiles[s + q]
            for k in range(8):
                acc = acc - mults[q][k] * rows[k]
            tiles[s + q] = acc
        tiles[s] = tiles[s] * scale
    return jnp.concatenate(tiles, axis=0)


def factor(block, work, out):
    row = lax.broadcasted_iota(jnp.int32, (NB, NB), 0)
    lane = lax.broadcasted_iota(jnp.int32, (NB, NB), 1)
    low = jnp.where(row >= lane, block, 0.0)
    work[:, :NB] = low + jnp.where(row > lane, block, 0.0).T
    work[:, NB:] = jnp.where(row == lane, 1.0, 0.0)
    lane_of = lax.broadcasted_iota(jnp.int32, (PB, 128), 1)
    row_of = lax.broadcasted_iota(jnp.int32, (PB, 128), 0)
    wide_lane = lax.broadcasted_iota(jnp.int32, (PB, NB), 1)

    def body(p, _):
        base = pl.multiple_of(p * PB, PB)
        slab = work[pl.ds(base, PB), :]
        turned = pltpu.roll(slab[:, :NB], jnp.where(p == 0, PB, NB + PB - base), 1)[:, :128]
        unit = jnp.where(lane_of == row_of, 1.0, 0.0)
        t = jnp.where((lane_of >= PB) & (lane_of < 2 * PB), turned, unit)
        j = small_factor(t)[:, :PB]
        u = dot3(split(j), split(slab), NN)
        out[pl.ds(base, PB), :] = u
        uh, ul = split(u)
        keep = wide_lane >= base + PB
        zero = jnp.zeros((PB, NB), bf16)
        left = (jnp.where(keep, uh[:, :NB], zero), jnp.where(keep, ul[:, :NB], zero))
        work[...] -= dot3(left, (uh, ul), TN)
        return 0

    lax.fori_loop(0, NB // PB, body, 0)
    g = jnp.where(lane >= row, out[:, :NB], 0.0).T
    return g, out[:, NB:]


FACTOR_SCRATCH = [pltpu.VMEM((NB, 2 * NB), f32), pltpu.VMEM((NB, 2 * NB), f32)]


def kept(flag, value):
    return jnp.where(flag != 0, value, 0.0)


def call(kernel, out_shape, **kwargs):
    kwargs.setdefault("compiler_params", pltpu.CompilerParams(vmem_limit_bytes=56 << 20))
    return pl.pallas_call(
        kernel,
        out_shape=out_shape,
        cost_estimate=pl.CostEstimate(flops=1, bytes_accessed=1, transcendentals=0),
        **kwargs,
    )


VMEM = pl.BlockSpec(memory_space=pltpu.VMEM)
SMEM = pl.BlockSpec(memory_space=pltpu.SMEM)
ANY = pl.BlockSpec(memory_space=pl.ANY)


def block_shape(*lead):
    return jax.ShapeDtypeStruct(lead + (NB, NB), f32)


def whole(ref, index):
    return ref[:, index].reshape(NB, NB)


def pair(i, j):
    return i * (i - 1) // 2 + j


def first_kernel(pattern, piece, g, h, l, work, out):
    g0, h0 = factor(whole(piece, 0), work, out)
    g[0], h[0] = g0, h0
    l10 = kept(pattern[1, 0], dot3(split(whole(piece, 1)), split(h0), NT))
    l[0] = l10
    s10 = split(l10)
    g[1], h[1] = factor(whole(piece, 2) - dot3(s10, s10, NT), work, out)


def later_kernel(k, first, pattern, piece, *refs):
    count = k - 1
    h_refs, l_refs = refs[:count], refs[count : 2 * count]
    g, h, l, work, out = refs[2 * count :]
    hs, ls = listed(h_refs), listed(l_refs)
    row = [whole(piece, first + j) for j in range(k + 1)]
    for j in range(k):
        l[j] = kept(pattern[k, j], dot3(split(row[j]), split(hs[j][...]), NT))
        value = split(l[j])
        for i in range(j + 1, k):
            row[i] = row[i] - dot3(value, split(ls[pair(i, j)][...]), NT)
        row[k] = row[k] - dot3(value, value, NT)
    g[0], h[0] = factor(row[k], work, out)


def listed(refs):
    return [ref.at[i] for ref in refs for i in range(ref.shape[0])]


def solve_rows(columns, mask, h, l):
    solved = []
    columns = list(columns)
    for k in range(len(columns)):
        value = mask(k, dot3(split(columns[k]), h(k), NT))
        solved.append(value)
        value = split(value)
        for j in range(k + 1, len(columns)):
            columns[j] = columns[j] - dot3(value, l(j, k), NT)
    return solved


def row_mask(info, first, groups, height):
    def mask(k, value):
        parts = [
            kept(info[first + i, 1 + k], value[i * height : (i + 1) * height]) for i in range(groups)
        ]
        return jnp.concatenate(parts, axis=0) if groups > 1 else parts[0]

    return mask


def lead_kernel(info, place, pattern, lower, h01, h2, h3, l1, l2, l3, own, e0, e1, e2, e3, *refs):
    hh, hl, lh, ll, ch, cl, top, rows = refs[-8:]
    for k, block in enumerate(listed([h01, h2, h3])):
        hh[k], hl[k] = split(block[...])
    for k, block in enumerate(listed([l1, l2, l3])):
        lh[k], ll[k] = split(block[...])
    h = lambda k: (hh[k], hl[k])
    l = lambda j, k: (lh[pair(j, k)], ll[pair(j, k)])
    columns = [jnp.concatenate([whole(lower, j * K + k) for j in range(K)], axis=0) for k in range(K)]

    def mask(k, value):
        parts = [kept(pattern[K + j, k], value[j * NB : (j + 1) * NB]) for j in range(K)]
        return jnp.concatenate(parts, axis=0)

    solved = solve_rows(columns, mask, h, l)
    for k in range(K):
        ch[:, k * NB : (k + 1) * NB], cl[:, k * NB : (k + 1) * NB] = split(solved[k])
    count, height = rows.shape[:2]
    for d, early in enumerate([e0, e1, e2, e3]):
        rows[place[d]] = early[...]
    solved = solve_rows([rows[k, :, :NB] for k in range(K)], row_mask(info, info[0, 2 + K], 1, height), h, l)
    update = dot3(split(jnp.concatenate(solved, axis=1)), (ch[: 2 * NB], cl[: 2 * NB]), NT)
    for v in range(K):
        start = v % 2 * 128
        schur = rows[v // 2, :, NB + start : NB + start + 128] - update[:, v * 128 : v * 128 + 128]
        top[v, :, 0] = schur.reshape(height // 8, 8, 128)
        for t in range(4):
            mine = own[t * count + v // 2, 1, :, start : start + 128]
            top[v, :, 1 + t] = jnp.broadcast_to(mine[None], (height // 8, 8, 128))


def rows_kernel(info, place, front, p1, p2, p3, g01, g2, g3, hh, hl, lh, ll, ch, cl, *refs):
    child, b1, b2, b3, extend, fin, fout, eout, insem, outsem, extsem = refs[-11:]
    step, steps = pl.program_id(0), pl.num_programs(0)
    groups, height = fin.shape[2], fin.shape[3]
    octets = height // 8
    slot = lax.rem(step, 2)

    def load(at, slot):
        for s in range(groups):
            here = at * groups + s
            for d, source in enumerate([front.at[here, place[0]], p1.at[here], p2.at[here], p3.at[here]]):
                pltpu.make_async_copy(source, fin.at[slot, place[d], s], insem.at[slot]).start()

    def store(at, slot):
        for s in range(groups):
            here = at * groups + s
            for d, target in enumerate([child.at[here, place[0]], b1.at[here], b2.at[here], b3.at[here]]):
                pltpu.make_async_copy(fout.at[slot, place[d], s], target, outsem.at[slot]).start()

    def wait(buffer, slot, sem):
        pltpu.make_async_copy(buffer.at[slot], buffer.at[slot], sem.at[slot]).wait()

    @pl.when(step == 0)
    def _():
        load(0, 0)

    @pl.when(step + 1 < steps)
    def _():
        load(step + 1, 1 - slot)

    wait(fin, slot, insem)

    @pl.when(step >= 2)
    def _():
        wait(fout, slot, outsem)
        wait(eout, slot, extsem)

    first = step * groups
    columns = [fin[slot, k, :, :, :NB].reshape(groups * height, NB) for k in range(K)]
    solved = solve_rows(
        columns,
        row_mask(info, first, groups, height),
        lambda k: (hh[k], hl[k]),
        lambda j, k: (lh[pair(j, k)], ll[pair(j, k)]),
    )
    update = dot3(split(jnp.concatenate(solved, axis=1)), (ch[...], cl[...]), NT)
    for k, g in enumerate(listed([g01, g2, g3])):
        fout[slot, k, :, :, :NB] = solved[k].reshape(groups, height, NB)
        schur = fin[slot, k, :, :, NB:].reshape(groups * height, NB) - update[:, k * NB : (k + 1) * NB]
        fout[slot, k, :, :, NB:] = schur.reshape(groups, height, NB)
        eout[slot, :, :, :, k * NB : (k + 1) * NB] = schur.reshape(groups, octets, 8, NB)
        for i in range(groups):

            @pl.when(info[first + i, 0] == k)
            def _():
                mine = pl.ds(pl.multiple_of(place[0] * height, height), height)
                fout[slot, k, i, :, :NB] = g[mine, :]

    store(step, slot)

    def send(i):
        at = info[first + i, 1 + K]
        holder = pl.multiple_of(lax.div(at, groups) * octets, octets)
        target = extend.at[pl.ds(holder, octets), lax.rem(at, groups)]
        return pltpu.make_async_copy(eout.at[slot, i], target, extsem.at[slot])

    for i in range(groups):
        send(i).start()

    @pl.when(step == steps - 1)
    def _():
        for other in range(2):
            wait(fout, other, outsem)
            wait(eout, other, extsem)


def parent_kernel(pattern, top, g, hh, hl, lh, ll, work, out):
    def block(i, j):
        halves = [
            jnp.swapaxes(top[2 * j + v, :, :, i], 0, 1).reshape(NB, 128) for v in range(2)
        ]
        return jnp.concatenate(halves, axis=1)

    g0, h0 = factor(block(0, 0), work, out)
    g[0] = g0
    h0 = split(h0)
    hh[0], hl[0] = h0
    first = []
    for i in range(1, 4):
        value = split(kept(pattern[i, 0], dot3(split(block(i, 0)), h0, NT)))
        lh[i - 1], ll[i - 1] = value
        first.append(value)
    g1, h1 = factor(block(1, 1) - dot3(first[0], first[0], NT), work, out)
    g[1] = g1
    h1 = split(h1)
    hh[1], hl[1] = h1
    for i in range(2, 4):
        rest = block(i, 1) - dot3(first[i - 1], first[0], NT)
        lh[i + 1], ll[i + 1] = split(kept(pattern[i, 1], dot3(split(rest), h1, NT)))


def parent_steps(columns, mask, hh, hl, lh, ll):
    one = mask(0, dot3(split(columns[0]), (hh[0], hl[0]), NT))
    first = split(one)
    two = mask(1, dot3(split(columns[1] - dot3(first, (lh[0], ll[0]), NT)), (hh[1], hl[1]), NT))
    second = split(two)
    results = [one, two]
    for j in range(2, 4):
        left = dot3(first, (lh[j - 1], ll[j - 1]), NT) + dot3(second, (lh[j + 1], ll[j + 1]), NT)
        results.append(columns[j] - left)
    return results


def parent_rows_kernel(info, place, target, extend, own, g, hh, hl, lh, ll, out, acc):
    slots, members = acc.shape[0], acc.shape[1]
    count = own.shape[0] // members
    for s in range(slots):
        for i in range(members):
            for j in range(count):
                acc[s, i, :, j * NB : (j + 1) * NB] = own[i * count + j, 1 + s]

    def add(q, _):
        for s in range(slots):
            where = target[q, s]

            @pl.when(where >= 0)
            def _():
                acc[s, where] += extend[q, s]

        return 0

    lax.fori_loop(0, extend.shape[0], add, 0)
    columns = [acc[:, :, :, j * NB : (j + 1) * NB].reshape(slots * members * 8, NB) for j in range(4)]
    results = parent_steps(columns, row_mask(info, 0, slots * members, 8), hh, hl, lh, ll)
    for j in range(4):
        shaped = results[j].reshape(slots, members, 8, NB)
        for s in range(slots):
            out[:, j, s] = shaped[s]
    for k in range(KP):

        @pl.when(info[k, 0] == k)
        def _():
            mine = pl.ds(pl.multiple_of(place[K] * 8, 8), 8)
            out[k, k, 0] = g[k, mine, :]


def exchange(array, axes):
    return lax.all_to_all(array, axes, split_axis=0, concat_axis=0, tiled=True)


def gather_pieces(pieces, axes, count):
    return exchange(jnp.broadcast_to(pieces[None], (count,) + pieces.shape), axes)


def shift(array, d, n):
    return lax.ppermute(array, "col", [(i, (i + d) % n) for i in range(n)])


def nought(array):
    one = array[(0,) * array.ndim]
    return (one != one).astype(jnp.int32)


def once(arrays, others):
    count = len(arrays)
    return pl.pallas_call(
        lambda *refs: None,
        out_shape=[jax.ShapeDtypeStruct(array.shape, array.dtype) for array in arrays],
        in_specs=[ANY] * (count + len(others)),
        out_specs=[ANY] * count,
        input_output_aliases={i: i for i in range(count)},
    )(*arrays, *others)


def per_device(child_front, child_pattern, block_map, parent_front, parent_pattern):
    nr, nx, nc = lax.axis_size("row"), lax.axis_size("col"), lax.axis_size("cube")
    r, x, c = lax.axis_index("row"), lax.axis_index("col"), lax.axis_index("cube")
    local = child_front.shape[1] // NB
    slots = parent_front.shape[0] // NB
    height = NB // nx
    octets = height // 8
    holders = nc * nr
    front = child_front[0]
    pattern = child_pattern[0]

    place = jnp.stack([(x - d) % nx for d in range(nx)] + [x * octets + r]).astype(jnp.int32)
    square = block_shape
    half = lambda *shape: jax.ShapeDtypeStruct(shape, bf16)

    tables = block_map.reshape(nc, local, nr).transpose(0, 2, 1)
    live = tables >= 0
    cubes = jnp.where(live, tables % holders // nr, -1)
    places = jnp.where(live, tables // holders, -1)
    members = jnp.where(live, tables % nr, -1)
    mine = tables[c, r]
    spot = jnp.where(mine >= 0, cubes[c, r] * slots + places[c, r], -1)
    spot = jnp.where(spot >= 0, spot, local * (local - 1) // 2 - jnp.sum(jnp.maximum(spot, 0)))
    lead = jnp.sum(jnp.where(spot == 0, jnp.arange(local), 0))
    block_row = jnp.arange(local) * nr + r
    kept_rows = jnp.where(
        block_row[:, None] > jnp.arange(K)[None], jnp.take(pattern, block_row, axis=0, mode="clip"), 0
    )
    row_info = jnp.concatenate(
        [block_row[:, None], kept_rows, spot[:, None], jnp.full((local, 1), lead)], axis=1
    ).astype(jnp.int32)

    quarters = front.reshape(local, nx, height, -1)
    ahead = lax.dynamic_index_in_dim(quarters, lead, axis=0, keepdims=False)

    parent_row = (jnp.arange(slots)[:, None] * holders + c * nr + jnp.arange(nr)[None, :]).reshape(-1)
    flags = jnp.take(parent_pattern, parent_row, axis=0, mode="clip")
    flags = jnp.where(parent_row[:, None] > jnp.arange(KP)[None], flags, 0)
    parent_info = jnp.concatenate([parent_row[:, None], flags], axis=1).astype(jnp.int32)
    here = (cubes == c)[:, :, None, :] & (places[:, :, None, :] == jnp.arange(slots)[None, None, :, None])
    target = jnp.max(jnp.where(here, members[:, :, None, :], -1), axis=-1).reshape(holders, slots)
    target = target.astype(jnp.int32)

    corner = front[:NB, :NB].reshape(nr * nx, 1, 8, NB)
    own = parent_front.reshape(slots, nx, octets, 8, NB).transpose(2, 1, 0, 3, 4).reshape(nr * nx, slots, 8, NB)
    own = exchange(jnp.concatenate([corner, own], axis=1), ("row", "col"))
    pieces = own[:, 0]
    lines = [pieces[i * nx : i * nx + i + 1] for i in range(K)] + [pieces[K * nx : 2 * K * nx]]
    lines = jnp.concatenate(lines, axis=0)
    early = [lax.dynamic_index_in_dim(ahead, (x + d) % nx, axis=0, keepdims=False) for d in range(nx)]
    tables = [row_info, place, pattern[: 2 * K], parent_pattern[:4], parent_info, target]
    lines, row_info, place, lead_pattern, top_pattern, parent_info, target, *early = once(
        [lines, *tables, *early], []
    )
    begun = nought(lines)
    lines = jnp.stack([lines] + [shift(lines, d, nx) for d in range(1, nx)])
    lines = jnp.take(lines, (x - jnp.arange(nx)) % nx, axis=0, mode="clip")
    lines = lines.transpose(1, 0, 2, 3).reshape(-1, nx * 8, NB)
    square_parts = gather_pieces(lines[:10], ("row",), nr)
    lower = lax.all_gather(lines[10:], "row")
    early = early[:1] + [shift(early[d], d, nx) for d in range(1, nx)]
    sent = [lax.dynamic_index_in_dim(quarters, (x + d + begun) % nx, axis=1, keepdims=False) for d in range(1, nx)]
    sent = once(sent, early[1:])
    parts = [shift(part, d + 1, nx) for d, part in enumerate(sent)]

    def panels():
        g01, h01, l1 = call(
            first_kernel,
            [square(2), square(2), square(1)],
            in_specs=[SMEM, VMEM],
            out_specs=[VMEM] * 3,
            scratch_shapes=FACTOR_SCRATCH,
        )(lead_pattern, square_parts)
        g2, h2, l2 = call(
            functools.partial(later_kernel, 2, 3),
            [square(1), square(1), square(2)],
            in_specs=[SMEM] + [VMEM] * 3,
            out_specs=[VMEM] * 3,
            scratch_shapes=FACTOR_SCRATCH,
        )(lead_pattern, square_parts, h01, l1)
        g3, h3, l3 = call(
            functools.partial(later_kernel, 3, 6),
            [square(1), square(1), square(3)],
            in_specs=[SMEM] + [VMEM] * 5,
            out_specs=[VMEM] * 3,
            scratch_shapes=FACTOR_SCRATCH,
        )(lead_pattern, square_parts, h01, h2, l1, l2)
        return g01, g2, g3, h01, h2, h3, l1, l2, l3

    empty = jax.tree.map(lambda leaf: jnp.zeros(leaf.shape, leaf.dtype), jax.eval_shape(panels))
    g01, g2, g3, h01, h2, h3, l1, l2, l3 = lax.cond(nought(square_parts) == 0, panels, lambda: empty)

    *weights, top = call(
        lead_kernel,
        [half(K, NB, NB)] * 2
        + [half(6, NB, NB)] * 2
        + [half(K * NB, K * NB)] * 2
        + [jax.ShapeDtypeStruct((nc, octets, 5, 8, 128), f32)],
        in_specs=[SMEM] * 3 + [VMEM] * 12,
        out_specs=[VMEM] * 7,
        scratch_shapes=[pltpu.VMEM((nx, height, 2 * NB), f32)],
    )(row_info, place, lead_pattern, lower, h01, h2, h3, l1, l2, l3, own, *early)
    (top,) = once([top], parts)
    top = exchange(top.reshape(holders, 5, 8, 128), ("cube", "row"))
    top_row = jnp.max(jnp.where((cubes == 0) & (places == 0), members, -1), axis=-1).reshape(holders)
    chosen = top_row[None, :] == jnp.arange(4)[:, None]
    top = lax.dynamic_index_in_dim(top, r, axis=0, keepdims=False)[1:] + jnp.sum(jnp.where(chosen[:, :, None, None], top[None, :, 0], 0.0), axis=1)

    top_sent = jnp.broadcast_to(top[None], (nc * nr * nx,) + top.shape)
    top = exchange(top_sent, ("cube", "row", "col")).reshape(nc, nr, nx, 4, 8, 128)

    full = lambda a: pl.BlockSpec(a.shape, lambda i, n=a.ndim: (0,) * n)
    buffer = pltpu.VMEM((2, nx, slots, height, 2 * NB), f32)
    wide = jax.ShapeDtypeStruct((nc * octets, slots, 8, nx * NB), f32)
    child_out, *back, extend = call(
        rows_kernel,
        [jax.ShapeDtypeStruct(quarters.shape, f32), *[jax.ShapeDtypeStruct(parts[0].shape, f32)] * 3, wide],
        grid=(local // slots,),
        in_specs=[SMEM] * 2 + [ANY] * 4 + [full(a) for a in (g01, g2, g3, *weights)] + [ANY],
        out_specs=[ANY] * 5,
        scratch_shapes=[buffer, buffer, pltpu.VMEM((2, slots, octets, 8, nx * NB), f32)]
        + [pltpu.SemaphoreType.DMA((2,))] * 3,
    )(row_info, place, quarters, *parts, g01, g2, g3, *weights, top_sent)
    def parent():
        arrived = exchange(extend, ("cube", "row"))

        g_parent, *parent_weights = call(
            parent_kernel,
            [square(2)] + [half(2, NB, NB)] * 2 + [half(5, NB, NB)] * 2,
            in_specs=[SMEM, VMEM],
            out_specs=[VMEM] * 5,
            scratch_shapes=FACTOR_SCRATCH,
        )(top_pattern, top)

        result = call(
            parent_rows_kernel,
            jax.ShapeDtypeStruct((nr, nx, slots, 8, NB), f32),
            in_specs=[SMEM] * 3 + [VMEM] * 7,
            out_specs=VMEM,
            scratch_shapes=[pltpu.VMEM((slots, nr, 8, nx * NB), f32)],
        )(
            parent_info,
            place,
            target,
            arrived,
            own,
            g_parent,
            *parent_weights,
        )
        return result

    empty = jax.tree.map(lambda leaf: jnp.zeros(leaf.shape, leaf.dtype), jax.eval_shape(parent))
    result = lax.cond(nought(top) == 0, parent, lambda: empty)

    late = x + nought(result)
    for d in range(1, nx):
        part = shift(back[d - 1], -d, nx)[:, None]
        child_out = lax.dynamic_update_slice(child_out, part, (0, (late + d) % nx, 0, 0))
    child_out = child_out.reshape(child_front.shape)
    result = exchange(result.reshape(nr * nx, slots, 8, NB), ("row", "col"))
    result = result.reshape(nr, nx, slots, 8, NB).transpose(2, 1, 0, 3, 4).reshape(parent_front.shape)
    return child_out, result


def solution(mesh):
    placed = (P("cube", "row", "col"), P("cube", None, None), P(), P(("cube", "row"), "col"), P())
    return jax.shard_map(
        per_device,
        mesh=mesh,
        in_specs=placed,
        out_specs=(P("cube", "row", "col"), P(("cube", "row"), "col")),
        check_vma=False,
    )
```

```python
import functools

import jax
import jax.numpy as jnp
from jax import lax
from jax.experimental import pallas as pl
from jax.experimental.pallas import tpu as pltpu
from jax.sharding import PartitionSpec as P

NB = 256
K = 4
KP = 2
PB = 64

f32, bf16 = jnp.float32, jnp.bfloat16


def dims(a, b):
    return (((a,), (b,)), ((), ()))


NN, NT, TN = dims(1, 0), dims(1, 1), dims(0, 0)


def split(x):
    high = x.astype(bf16)
    return high, (x - high.astype(f32)).astype(bf16)


def dot3(x, y, d):
    xh, xl = x
    yh, yl = y
    part = lambda p, q: lax.dot_general(p, q, d, preferred_element_type=f32)
    return part(xh, yh) + (part(xh, yl) + part(xl, yh))


def small_factor(t):
    count = PB // 8
    tiles = [t[8 * i : 8 * i + 8] for i in range(count)]
    full = (8, 128)
    sub = lax.broadcasted_iota(jnp.int32, full, 0)
    for s in range(count):
        c0 = PB + 8 * s
        cols = [
            [jnp.broadcast_to(tiles[q][:, c0 + k : c0 + k + 1], full) for k in range(8)]
            for q in range(s, count)
        ]
        a = [
            [jnp.broadcast_to(cols[0][k][i : i + 1], full) if i >= k else None for k in range(8)]
            for i in range(8)
        ]
        rows = [jnp.broadcast_to(tiles[s][k : k + 1], full) for k in range(8)]
        mults = [[] for _ in range(s, count)]
        scale = None
        for k in range(8):
            r = 1.0 / a[k][k]
            root = lax.rsqrt(a[k][k])
            scale = root if k == 0 else jnp.where(sub == k, root, scale)
            m = [a[i][k] * r if i > k else None for i in range(8)]
            for q in range(count - s):
                mult = cols[q][k] * r
                if q == 0:
                    mult = jnp.where(sub > k, mult, 0.0)
                mults[q].append(mult)
            for i in range(k + 1, 8):
                rows[i] = rows[i] - m[i] * rows[k]
                for q in range(count - s):
                    cols[q][i] = cols[q][i] - mults[q][k] * a[i][k]
                for j in range(k + 1, i + 1):
                    a[i][j] = a[i][j] - m[i] * a[j][k]
        for q in range(count - s):
            acc = tiles[s + q]
            for k in range(8):
                acc = acc - mults[q][k] * rows[k]
            tiles[s + q] = acc
        tiles[s] = tiles[s] * scale
    return jnp.concatenate(tiles, axis=0)


def factor(block, work, out):
    row = lax.broadcasted_iota(jnp.int32, (NB, NB), 0)
    lane = lax.broadcasted_iota(jnp.int32, (NB, NB), 1)
    low = jnp.where(row >= lane, block, 0.0)
    work[:, :NB] = low + jnp.where(row > lane, block, 0.0).T
    work[:, NB:] = jnp.where(row == lane, 1.0, 0.0)
    lane_of = lax.broadcasted_iota(jnp.int32, (PB, 128), 1)
    row_of = lax.broadcasted_iota(jnp.int32, (PB, 128), 0)
    wide_lane = lax.broadcasted_iota(jnp.int32, (PB, NB), 1)

    def body(p, _):
        base = pl.multiple_of(p * PB, PB)
        slab = work[pl.ds(base, PB), :]
        turned = pltpu.roll(slab[:, :NB], jnp.where(p == 0, PB, NB + PB - base), 1)[:, :128]
        unit = jnp.where(lane_of == row_of, 1.0, 0.0)
        t = jnp.where((lane_of >= PB) & (lane_of < 2 * PB), turned, unit)
        j = small_factor(t)[:, :PB]
        u = dot3(split(j), split(slab), NN)
        out[pl.ds(base, PB), :] = u
        uh, ul = split(u)
        keep = wide_lane >= base + PB
        zero = jnp.zeros((PB, NB), bf16)
        left = (jnp.where(keep, uh[:, :NB], zero), jnp.where(keep, ul[:, :NB], zero))
        work[...] -= dot3(left, (uh, ul), TN)
        return 0

    lax.fori_loop(0, NB // PB, body, 0)
    g = jnp.where(lane >= row, out[:, :NB], 0.0).T
    return g, out[:, NB:]


FACTOR_SCRATCH = [pltpu.VMEM((NB, 2 * NB), f32), pltpu.VMEM((NB, 2 * NB), f32)]


def kept(flag, value):
    return jnp.where(flag != 0, value, 0.0)


def call(kernel, out_shape, **kwargs):
    kwargs.setdefault("compiler_params", pltpu.CompilerParams(vmem_limit_bytes=56 << 20))
    return pl.pallas_call(
        kernel,
        out_shape=out_shape,
        cost_estimate=pl.CostEstimate(flops=1, bytes_accessed=1, transcendentals=0),
        **kwargs,
    )


VMEM = pl.BlockSpec(memory_space=pltpu.VMEM)
SMEM = pl.BlockSpec(memory_space=pltpu.SMEM)
ANY = pl.BlockSpec(memory_space=pl.ANY)


def block_shape(*lead):
    return jax.ShapeDtypeStruct(lead + (NB, NB), f32)


def whole(ref, index):
    return ref[:, index].reshape(NB, NB)


def pair(i, j):
    return i * (i - 1) // 2 + j


def first_kernel(pattern, piece, g, h, l, work, out):
    g0, h0 = factor(whole(piece, 0), work, out)
    g[0], h[0] = g0, h0
    l10 = kept(pattern[1, 0], dot3(split(whole(piece, 1)), split(h0), NT))
    l[0] = l10
    s10 = split(l10)
    g[1], h[1] = factor(whole(piece, 2) - dot3(s10, s10, NT), work, out)


def later_kernel(k, first, pattern, piece, *refs):
    count = k - 1
    h_refs, l_refs = refs[:count], refs[count : 2 * count]
    g, h, l, work, out = refs[2 * count :]
    hs, ls = listed(h_refs), listed(l_refs)
    row = [whole(piece, first + j) for j in range(k + 1)]
    for j in range(k):
        l[j] = kept(pattern[k, j], dot3(split(row[j]), split(hs[j][...]), NT))
        value = split(l[j])
        for i in range(j + 1, k):
            row[i] = row[i] - dot3(value, split(ls[pair(i, j)][...]), NT)
        row[k] = row[k] - dot3(value, value, NT)
    g[0], h[0] = factor(row[k], work, out)


def listed(refs):
    return [ref.at[i] for ref in refs for i in range(ref.shape[0])]


def solve_rows(columns, mask, h, l):
    solved = []
    columns = list(columns)
    for k in range(len(columns)):
        value = mask(k, dot3(split(columns[k]), h(k), NT))
        solved.append(value)
        value = split(value)
        for j in range(k + 1, len(columns)):
            columns[j] = columns[j] - dot3(value, l(j, k), NT)
    return solved


def row_mask(info, first, groups, height):
    def mask(k, value):
        parts = [
            kept(info[first + i, 1 + k], value[i * height : (i + 1) * height]) for i in range(groups)
        ]
        return jnp.concatenate(parts, axis=0) if groups > 1 else parts[0]

    return mask


def crossing(pattern, first, lower, hh, hl, lh, ll):
    columns = [jnp.concatenate([whole(lower, j * K + k) for j in range(2)], axis=0) for k in range(K)]

    def mask(k, value):
        parts = [kept(pattern[K + first + j, k], value[j * NB : (j + 1) * NB]) for j in range(2)]
        return jnp.concatenate(parts, axis=0)

    h = lambda k: (hh[k], hl[k])
    l = lambda j, k: (lh[pair(j, k)], ll[pair(j, k)])
    return split(jnp.concatenate(solve_rows(columns, mask, h, l), axis=1))


def lead_kernel(info, place, pattern, lower, h01, h2, h3, l1, l2, l3, e0, e1, e2, e3, *refs):
    hh, hl, lh, ll, ch, cl, top, rows = refs
    for k, block in enumerate(listed([h01, h2, h3])):
        hh[k], hl[k] = split(block[...])
    for k, block in enumerate(listed([l1, l2, l3])):
        lh[k], ll[k] = split(block[...])
    across = crossing(pattern, 0, lower, hh, hl, lh, ll)
    ch[...], cl[...] = across
    for d, early in enumerate([e0, e1, e2, e3]):
        rows[place[d]] = early[...]
    height = rows.shape[1]
    solved = solve_rows(
        [rows[k, :, :NB] for k in range(K)],
        row_mask(info, info[0, 2 + K], 1, height),
        lambda k: (hh[k], hl[k]),
        lambda j, k: (lh[pair(j, k)], ll[pair(j, k)]),
    )
    update = dot3(split(jnp.concatenate(solved, axis=1)), across, NT)
    for v in range(K):
        start = NB + v % 2 * 128
        schur = rows[v // 2, :, start : start + 128] - update[:, v * 128 : v * 128 + 128]
        top[v, :, 0] = schur.reshape(height // 8, 8, 128)
        top[v, :, 1] = rows[v // 2, :, start + NB : start + NB + 128].reshape(height // 8, 8, 128)


def crossing_kernel(pattern, lower, hh, hl, lh, ll, ch, cl):
    ch[...], cl[...] = crossing(pattern, 2, lower, hh, hl, lh, ll)


def rows_kernel(info, place, front, p1, p2, p3, g01, g2, g3, hh, hl, lh, ll, ch, cl, dh, dl, *refs):
    child, b1, b2, b3, extend, fin, fout, eout, insem, outsem, extsem = refs[-11:]
    step, steps = pl.program_id(0), pl.num_programs(0)
    groups, height = fin.shape[2], fin.shape[3]
    octets = height // 8
    slot = lax.rem(step, 2)

    def load(at, slot):
        for s in range(groups):
            here = at * groups + s
            for d, source in enumerate([front.at[here, place[0]], p1.at[here], p2.at[here], p3.at[here]]):
                pltpu.make_async_copy(source, fin.at[slot, place[d], s], insem.at[slot]).start()

    def store(at, slot):
        for s in range(groups):
            here = at * groups + s
            for d, target in enumerate([child.at[here, place[0]], b1.at[here], b2.at[here], b3.at[here]]):
                pltpu.make_async_copy(fout.at[slot, place[d], s], target, outsem.at[slot]).start()

    def wait(buffer, slot, sem):
        pltpu.make_async_copy(buffer.at[slot], buffer.at[slot], sem.at[slot]).wait()

    @pl.when(step == 0)
    def _():
        load(0, 0)

    @pl.when(step + 1 < steps)
    def _():
        load(step + 1, 1 - slot)

    wait(fin, slot, insem)

    @pl.when(step >= 2)
    def _():
        wait(fout, slot, outsem)
        wait(eout, slot, extsem)

    first = step * groups
    columns = [fin[slot, k, :, :, :NB].reshape(groups * height, NB) for k in range(K)]
    solved = solve_rows(
        columns,
        row_mask(info, first, groups, height),
        lambda k: (hh[k], hl[k]),
        lambda j, k: (lh[pair(j, k)], ll[pair(j, k)]),
    )
    final = split(jnp.concatenate(solved, axis=1))
    halves = [dot3(final, (ch[...], cl[...]), NT), dot3(final, (dh[...], dl[...]), NT)]
    for k, g in enumerate(listed([g01, g2, g3])):
        fout[slot, k, :, :, :NB] = solved[k].reshape(groups, height, NB)
        schur = fin[slot, k, :, :, NB:].reshape(groups * height, NB) - halves[k // 2][:, k % 2 * NB : (k % 2 + 1) * NB]
        fout[slot, k, :, :, NB:] = schur.reshape(groups, height, NB)
        eout[slot, :, :, :, k * NB : (k + 1) * NB] = schur.reshape(groups, octets, 8, NB)
        for i in range(groups):

            @pl.when(info[first + i, 0] == k)
            def _():
                mine = pl.ds(pl.multiple_of(place[0] * height, height), height)
                fout[slot, k, i, :, :NB] = g[mine, :]

    store(step, slot)

    def send(i):
        at = info[first + i, 1 + K]
        holder = pl.multiple_of(lax.div(at, groups) * octets, octets)
        target = extend.at[pl.ds(holder, octets), lax.rem(at, groups)]
        return pltpu.make_async_copy(eout.at[slot, i], target, extsem.at[slot])

    for i in range(groups):
        send(i).start()

    @pl.when(step == steps - 1)
    def _():
        for other in range(2):
            wait(fout, other, outsem)
            wait(eout, other, extsem)


def parent_kernel(pattern, top, g, hh, hl, lh, ll, work, out):
    def block(i, j):
        halves = [
            jnp.swapaxes(top[2 * j + v, :, :, i], 0, 1).reshape(NB, 128) for v in range(2)
        ]
        return jnp.concatenate(halves, axis=1)

    g0, h0 = factor(block(0, 0), work, out)
    g[0] = g0
    h0 = split(h0)
    hh[0], hl[0] = h0
    first = []
    for i in range(1, 4):
        value = split(kept(pattern[i, 0], dot3(split(block(i, 0)), h0, NT)))
        lh[i - 1], ll[i - 1] = value
        first.append(value)
    g1, h1 = factor(block(1, 1) - dot3(first[0], first[0], NT), work, out)
    g[1] = g1
    h1 = split(h1)
    hh[1], hl[1] = h1
    for i in range(2, 4):
        rest = block(i, 1) - dot3(first[i - 1], first[0], NT)
        lh[i + 1], ll[i + 1] = split(kept(pattern[i, 1], dot3(split(rest), h1, NT)))


def parent_steps(columns, mask, hh, hl, lh, ll):
    one = mask(0, dot3(split(columns[0]), (hh[0], hl[0]), NT))
    first = split(one)
    two = mask(1, dot3(split(columns[1] - dot3(first, (lh[0], ll[0]), NT)), (hh[1], hl[1]), NT))
    second = split(two)
    results = [one, two]
    for j in range(2, 4):
        left = dot3(first, (lh[j - 1], ll[j - 1]), NT) + dot3(second, (lh[j + 1], ll[j + 1]), NT)
        results.append(columns[j] - left)
    return results


def parent_rows_kernel(info, place, target, extend, own, g, hh, hl, lh, ll, out, acc):
    slots, members = acc.shape[0], acc.shape[1]
    count = own.shape[0] // members
    for s in range(slots):
        for i in range(members):
            for j in range(count):
                acc[s, i, :, j * NB : (j + 1) * NB] = own[i * count + j, 1 + s]

    def add(q, _):
        for s in range(slots):
            where = target[q, s]

            @pl.when(where >= 0)
            def _():
                acc[s, where] += extend[q, s]

        return 0

    lax.fori_loop(0, extend.shape[0], add, 0)
    columns = [acc[:, :, :, j * NB : (j + 1) * NB].reshape(slots * members * 8, NB) for j in range(4)]
    results = parent_steps(columns, row_mask(info, 0, slots * members, 8), hh, hl, lh, ll)
    for j in range(4):
        shaped = results[j].reshape(slots, members, 8, NB)
        for s in range(slots):
            out[:, j, s] = shaped[s]
    for k in range(KP):

        @pl.when(info[k, 0] == k)
        def _():
            mine = pl.ds(pl.multiple_of(place[K] * 8, 8), 8)
            out[k, k, 0] = g[k, mine, :]


def exchange(array, axes):
    return lax.all_to_all(array, axes, split_axis=0, concat_axis=0, tiled=True)


def gather_pieces(pieces, axes, count):
    return exchange(jnp.broadcast_to(pieces[None], (count,) + pieces.shape), axes)


def shift(array, d, n):
    return lax.ppermute(array, "col", [(i, (i + d) % n) for i in range(n)])


def nought(array):
    one = array[(0,) * array.ndim]
    return (one != one).astype(jnp.int32)


def once(arrays, others):
    count = len(arrays)
    return pl.pallas_call(
        lambda *refs: None,
        out_shape=[jax.ShapeDtypeStruct(array.shape, array.dtype) for array in arrays],
        in_specs=[ANY] * (count + len(others)),
        out_specs=[ANY] * count,
        input_output_aliases={i: i for i in range(count)},
    )(*arrays, *others)


def per_device(child_front, child_pattern, block_map, parent_front, parent_pattern):
    nr, nx, nc = lax.axis_size("row"), lax.axis_size("col"), lax.axis_size("cube")
    r, x, c = lax.axis_index("row"), lax.axis_index("col"), lax.axis_index("cube")
    local = child_front.shape[1] // NB
    slots = parent_front.shape[0] // NB
    height = NB // nx
    octets = height // 8
    holders = nc * nr
    front = child_front[0]
    pattern = child_pattern[0]

    place = jnp.stack([(x - d) % nx for d in range(nx)] + [x * octets + r]).astype(jnp.int32)
    square = block_shape
    half = lambda *shape: jax.ShapeDtypeStruct(shape, bf16)

    tables = block_map.reshape(nc, local, nr).transpose(0, 2, 1)
    live = tables >= 0
    cubes = jnp.where(live, tables % holders // nr, -1)
    places = jnp.where(live, tables // holders, -1)
    members = jnp.where(live, tables % nr, -1)
    mine = tables[c, r]
    spot = jnp.where(mine >= 0, cubes[c, r] * slots + places[c, r], -1)
    spot = jnp.where(spot >= 0, spot, local * (local - 1) // 2 - jnp.sum(jnp.maximum(spot, 0)))
    lead = jnp.sum(jnp.where(spot == 0, jnp.arange(local), 0))
    block_row = jnp.arange(local) * nr + r
    kept_rows = jnp.where(
        block_row[:, None] > jnp.arange(K)[None], jnp.take(pattern, block_row, axis=0, mode="clip"), 0
    )
    row_info = jnp.concatenate(
        [block_row[:, None], kept_rows, spot[:, None], jnp.full((local, 1), lead)], axis=1
    ).astype(jnp.int32)

    quarters = front.reshape(local, nx, height, -1)
    ahead = lax.dynamic_index_in_dim(quarters, lead, axis=0, keepdims=False)
    ahead = jnp.concatenate([ahead, parent_front[:NB].reshape(nx, height, NB)], axis=2)

    parent_row = (jnp.arange(slots)[:, None] * holders + c * nr + jnp.arange(nr)[None, :]).reshape(-1)
    flags = jnp.take(parent_pattern, parent_row, axis=0, mode="clip")
    flags = jnp.where(parent_row[:, None] > jnp.arange(KP)[None], flags, 0)
    parent_info = jnp.concatenate([parent_row[:, None], flags], axis=1).astype(jnp.int32)
    here = (cubes == c)[:, :, None, :] & (places[:, :, None, :] == jnp.arange(slots)[None, None, :, None])
    target = jnp.max(jnp.where(here, members[:, :, None, :], -1), axis=-1).reshape(holders, slots)
    target = target.astype(jnp.int32)

    corner = front[:NB, :NB].reshape(nr * nx, 1, 8, NB)
    own = parent_front.reshape(slots, nx, octets, 8, NB).transpose(2, 1, 0, 3, 4).reshape(nr * nx, slots, 8, NB)
    own = exchange(jnp.concatenate([corner, own], axis=1), ("row", "col"))
    pieces = own[:, 0]
    lines = [pieces[i * nx : i * nx + i + 1] for i in range(K)] + [pieces[K * nx : 2 * K * nx]]
    lines = jnp.concatenate(lines, axis=0)
    early = [lax.dynamic_index_in_dim(ahead, (x + d) % nx, axis=0, keepdims=False) for d in range(nx)]
    sent = [lax.dynamic_index_in_dim(quarters, (x + d) % nx, axis=1, keepdims=False) for d in range(1, nx)]
    tables = [row_info, place, pattern[: 2 * K], parent_pattern[:4], parent_info, target]
    lines, row_info, place, lead_pattern, top_pattern, parent_info, target, *made = once(
        [lines, *tables, *early, *sent], []
    )
    early, sent = made[:nx], made[nx:]
    lines = jnp.stack([lines] + [shift(lines, d, nx) for d in range(1, nx)])
    lines = jnp.take(lines, (x - jnp.arange(nx)) % nx, axis=0, mode="clip")
    lines = lines.transpose(1, 0, 2, 3).reshape(-1, nx * 8, NB)
    square_sent = jnp.broadcast_to(lines[None, :10], (nr, 10) + lines.shape[1:])
    square_parts = exchange(square_sent, ("row",))
    lower = lax.all_gather(lines[10:], "row")
    early = list(once(early, [square_sent]))
    early = early[:1] + [shift(early[d], d, nx) for d in range(1, nx)]
    sent = once(sent, early[1:])
    parts = [shift(part, d + 1, nx) for d, part in enumerate(sent)]

    def panels():
        g01, h01, l1 = call(
            first_kernel,
            [square(2), square(2), square(1)],
            in_specs=[SMEM, VMEM],
            out_specs=[VMEM] * 3,
            scratch_shapes=FACTOR_SCRATCH,
        )(lead_pattern, square_parts)
        g2, h2, l2 = call(
            functools.partial(later_kernel, 2, 3),
            [square(1), square(1), square(2)],
            in_specs=[SMEM] + [VMEM] * 3,
            out_specs=[VMEM] * 3,
            scratch_shapes=FACTOR_SCRATCH,
        )(lead_pattern, square_parts, h01, l1)
        g3, h3, l3 = call(
            functools.partial(later_kernel, 3, 6),
            [square(1), square(1), square(3)],
            in_specs=[SMEM] + [VMEM] * 5,
            out_specs=[VMEM] * 3,
            scratch_shapes=FACTOR_SCRATCH,
        )(lead_pattern, square_parts, h01, h2, l1, l2)
        return g01, g2, g3, h01, h2, h3, l1, l2, l3

    empty = jax.tree.map(lambda leaf: jnp.zeros(leaf.shape, leaf.dtype), jax.eval_shape(panels))
    g01, g2, g3, h01, h2, h3, l1, l2, l3 = lax.cond(nought(square_parts) == 0, panels, lambda: empty)

    some_lower = lambda n: pl.BlockSpec((nr, 2 * K, nx * 8, NB), lambda i, n=n: (0, n, 0, 0))
    *weights, top = call(
        lead_kernel,
        [half(K, NB, NB)] * 2
        + [half(6, NB, NB)] * 2
        + [half(2 * NB, K * NB)] * 2
        + [jax.ShapeDtypeStruct((nc, octets, 2, 8, 128), f32)],
        grid=(1,),
        in_specs=[SMEM] * 3 + [some_lower(0)] + [VMEM] * 10,
        out_specs=[VMEM] * 7,
        scratch_shapes=[pltpu.VMEM((nx, height, 3 * NB), f32)],
    )(row_info, place, lead_pattern, lower, h01, h2, h3, l1, l2, l3, *early)
    (top,) = once([top], parts)
    weights += call(
        crossing_kernel,
        [half(2 * NB, K * NB)] * 2,
        grid=(1,),
        in_specs=[SMEM, some_lower(1)] + [VMEM] * 4,
        out_specs=[VMEM] * 2,
    )(lead_pattern, lower, *weights[:4])
    top = exchange(top.reshape(holders, 2, 8, 128), ("cube", "row"))
    top_row = jnp.max(jnp.where((cubes == 0) & (places == 0), members, -1), axis=-1).reshape(holders)
    chosen = top_row[None, :] == jnp.arange(4)[:, None]
    top = top[:4, 1] + jnp.sum(jnp.where(chosen[:, :, None, None], top[None, :, 0], 0.0), axis=1)

    (top,) = once([top], weights[-2:])
    top_sent = jnp.broadcast_to(top[None], (nc * nr * nx,) + top.shape)
    top = exchange(top_sent, ("cube", "row", "col")).reshape(nc, nr, nx, 4, 8, 128)

    full = lambda a: pl.BlockSpec(a.shape, lambda i, n=a.ndim: (0,) * n)
    buffer = pltpu.VMEM((2, nx, slots, height, 2 * NB), f32)
    wide = jax.ShapeDtypeStruct((nc * octets, slots, 8, nx * NB), f32)
    child_out, *back, extend = call(
        rows_kernel,
        [jax.ShapeDtypeStruct(quarters.shape, f32), *[jax.ShapeDtypeStruct(parts[0].shape, f32)] * 3, wide],
        grid=(local // slots,),
        in_specs=[SMEM] * 2 + [ANY] * 4 + [full(a) for a in (g01, g2, g3, *weights)] + [ANY],
        out_specs=[ANY] * 5,
        scratch_shapes=[buffer, buffer, pltpu.VMEM((2, slots, octets, 8, nx * NB), f32)]
        + [pltpu.SemaphoreType.DMA((2,))] * 3,
    )(row_info, place, quarters, *parts, g01, g2, g3, *weights, top_sent)
    def parent():
        arrived = exchange(extend, ("cube", "row"))

        g_parent, *parent_weights = call(
            parent_kernel,
            [square(2)] + [half(2, NB, NB)] * 2 + [half(5, NB, NB)] * 2,
            in_specs=[SMEM, VMEM],
            out_specs=[VMEM] * 5,
            scratch_shapes=FACTOR_SCRATCH,
        )(top_pattern, top)

        result = call(
            parent_rows_kernel,
            jax.ShapeDtypeStruct((nr, nx, slots, 8, NB), f32),
            in_specs=[SMEM] * 3 + [VMEM] * 7,
            out_specs=VMEM,
            scratch_shapes=[pltpu.VMEM((slots, nr, 8, nx * NB), f32)],
        )(
            parent_info,
            place,
            target,
            arrived,
            own,
            g_parent,
            *parent_weights,
        )
        return result

    empty = jax.tree.map(lambda leaf: jnp.zeros(leaf.shape, leaf.dtype), jax.eval_shape(parent))
    result = lax.cond(nought(top) == 0, parent, lambda: empty)

    late = x + nought(result)
    for d in range(1, nx):
        part = shift(back[d - 1], -d, nx)[:, None]
        child_out = lax.dynamic_update_slice(child_out, part, (0, (late + d) % nx, 0, 0))
    child_out = child_out.reshape(child_front.shape)
    result = exchange(result.reshape(nr * nx, slots, 8, NB), ("row", "col"))
    result = result.reshape(nr, nx, slots, 8, NB).transpose(2, 1, 0, 3, 4).reshape(parent_front.shape)
    return child_out, result


def solution(mesh):
    placed = (P("cube", "row", "col"), P("cube", None, None), P(), P(("cube", "row"), "col"), P())
    return jax.shard_map(
        per_device,
        mesh=mesh,
        in_specs=placed,
        out_specs=(P("cube", "row", "col"), P(("cube", "row"), "col")),
        check_vma=False,
    )
```

```python
import functools

import jax
import jax.numpy as jnp
from jax import lax
from jax.experimental import pallas as pl
from jax.experimental.pallas import tpu as pltpu
from jax.sharding import PartitionSpec as P

NB = 256
K = 4
KP = 2
PB = 64

f32, bf16 = jnp.float32, jnp.bfloat16


def dims(a, b):
    return (((a,), (b,)), ((), ()))


NN, NT, TN = dims(1, 0), dims(1, 1), dims(0, 0)


def split(x):
    high = x.astype(bf16)
    return high, (x - high.astype(f32)).astype(bf16)


def dot3(x, y, d):
    xh, xl = x
    yh, yl = y
    part = lambda p, q: lax.dot_general(p, q, d, preferred_element_type=f32)
    return part(xh, yh) + (part(xh, yl) + part(xl, yh))


def small_factor(t):
    count = PB // 8
    tiles = [t[8 * i : 8 * i + 8] for i in range(count)]
    full = (8, 128)
    sub = lax.broadcasted_iota(jnp.int32, full, 0)
    for s in range(count):
        c0 = PB + 8 * s
        cols = [
            [jnp.broadcast_to(tiles[q][:, c0 + k : c0 + k + 1], full) for k in range(8)]
            for q in range(s, count)
        ]
        a = [
            [jnp.broadcast_to(cols[0][k][i : i + 1], full) if i >= k else None for k in range(8)]
            for i in range(8)
        ]
        rows = [jnp.broadcast_to(tiles[s][k : k + 1], full) for k in range(8)]
        mults = [[] for _ in range(s, count)]
        scale = None
        for k in range(8):
            r = 1.0 / a[k][k]
            root = lax.rsqrt(a[k][k])
            scale = root if k == 0 else jnp.where(sub == k, root, scale)
            m = [a[i][k] * r if i > k else None for i in range(8)]
            for q in range(count - s):
                mult = cols[q][k] * r
                if q == 0:
                    mult = jnp.where(sub > k, mult, 0.0)
                mults[q].append(mult)
            for i in range(k + 1, 8):
                rows[i] = rows[i] - m[i] * rows[k]
                for q in range(count - s):
                    cols[q][i] = cols[q][i] - mults[q][k] * a[i][k]
                for j in range(k + 1, i + 1):
                    a[i][j] = a[i][j] - m[i] * a[j][k]
        for q in range(count - s):
            acc = tiles[s + q]
            for k in range(8):
                acc = acc - mults[q][k] * rows[k]
            tiles[s + q] = acc
        tiles[s] = tiles[s] * scale
    return jnp.concatenate(tiles, axis=0)


def factor(block, work, out):
    row = lax.broadcasted_iota(jnp.int32, (NB, NB), 0)
    lane = lax.broadcasted_iota(jnp.int32, (NB, NB), 1)
    low = jnp.where(row >= lane, block, 0.0)
    work[:, :NB] = low + jnp.where(row > lane, block, 0.0).T
    work[:, NB:] = jnp.where(row == lane, 1.0, 0.0)
    lane_of = lax.broadcasted_iota(jnp.int32, (PB, 128), 1)
    row_of = lax.broadcasted_iota(jnp.int32, (PB, 128), 0)
    wide_lane = lax.broadcasted_iota(jnp.int32, (PB, NB), 1)

    def body(p, _):
        base = pl.multiple_of(p * PB, PB)
        slab = work[pl.ds(base, PB), :]
        turned = pltpu.roll(slab[:, :NB], jnp.where(p == 0, PB, NB + PB - base), 1)[:, :128]
        unit = jnp.where(lane_of == row_of, 1.0, 0.0)
        t = jnp.where((lane_of >= PB) & (lane_of < 2 * PB), turned, unit)
        j = small_factor(t)[:, :PB]
        u = dot3(split(j), split(slab), NN)
        out[pl.ds(base, PB), :] = u
        uh, ul = split(u)
        keep = wide_lane >= base + PB
        zero = jnp.zeros((PB, NB), bf16)
        left = (jnp.where(keep, uh[:, :NB], zero), jnp.where(keep, ul[:, :NB], zero))
        work[...] -= dot3(left, (uh, ul), TN)
        return 0

    lax.fori_loop(0, NB // PB, body, 0)
    g = jnp.where(lane >= row, out[:, :NB], 0.0).T
    return g, out[:, NB:]


FACTOR_SCRATCH = [pltpu.VMEM((NB, 2 * NB), f32), pltpu.VMEM((NB, 2 * NB), f32)]


def kept(flag, value):
    return jnp.where(flag != 0, value, 0.0)


def call(kernel, out_shape, **kwargs):
    kwargs.setdefault("compiler_params", pltpu.CompilerParams(vmem_limit_bytes=56 << 20))
    return pl.pallas_call(
        kernel,
        out_shape=out_shape,
        cost_estimate=pl.CostEstimate(flops=1, bytes_accessed=1, transcendentals=0),
        **kwargs,
    )


VMEM = pl.BlockSpec(memory_space=pltpu.VMEM)
SMEM = pl.BlockSpec(memory_space=pltpu.SMEM)
ANY = pl.BlockSpec(memory_space=pl.ANY)


def block_shape(*lead):
    return jax.ShapeDtypeStruct(lead + (NB, NB), f32)


def whole(ref, index):
    return ref[:, index].reshape(NB, NB)


def pair(i, j):
    return i * (i - 1) // 2 + j


def first_kernel(pattern, piece, g, h, l, work, out):
    g0, h0 = factor(whole(piece, 0), work, out)
    g[0], h[0] = g0, h0
    l10 = kept(pattern[1, 0], dot3(split(whole(piece, 1)), split(h0), NT))
    l[0] = l10
    s10 = split(l10)
    g[1], h[1] = factor(whole(piece, 2) - dot3(s10, s10, NT), work, out)


def later_kernel(k, first, pattern, piece, *refs):
    count = k - 1
    h_refs, l_refs = refs[:count], refs[count : 2 * count]
    g, h, l, work, out = refs[2 * count :]
    hs, ls = listed(h_refs), listed(l_refs)
    row = [whole(piece, first + j) for j in range(k + 1)]
    for j in range(k):
        l[j] = kept(pattern[k, j], dot3(split(row[j]), split(hs[j][...]), NT))
        value = split(l[j])
        for i in range(j + 1, k):
            row[i] = row[i] - dot3(value, split(ls[pair(i, j)][...]), NT)
        row[k] = row[k] - dot3(value, value, NT)
    g[0], h[0] = factor(row[k], work, out)


def listed(refs):
    return [ref.at[i] for ref in refs for i in range(ref.shape[0])]


def solve_rows(columns, mask, h, l):
    solved = []
    columns = list(columns)
    for k in range(len(columns)):
        value = mask(k, dot3(split(columns[k]), h(k), NT))
        solved.append(value)
        value = split(value)
        for j in range(k + 1, len(columns)):
            columns[j] = columns[j] - dot3(value, l(j, k), NT)
    return solved


def row_mask(info, first, groups, height):
    def mask(k, value):
        parts = [
            kept(info[first + i, 1 + k], value[i * height : (i + 1) * height]) for i in range(groups)
        ]
        return jnp.concatenate(parts, axis=0) if groups > 1 else parts[0]

    return mask


def panels_kernel(pattern, piece, g01, h01, l1, g2, h2, l2, g3, h3, l3, work, out):
    first_kernel(pattern, piece, g01, h01, l1, work, out)
    later_kernel(2, 3, pattern, piece, h01, l1, g2, h2, l2, work, out)
    later_kernel(3, 6, pattern, piece, h01, h2, l1, l2, g3, h3, l3, work, out)


def crossing(pattern, first, lower, hh, hl, lh, ll):
    columns = [jnp.concatenate([whole(lower, j * K + k) for j in range(2)], axis=0) for k in range(K)]

    def mask(k, value):
        parts = [kept(pattern[K + first + j, k], value[j * NB : (j + 1) * NB]) for j in range(2)]
        return jnp.concatenate(parts, axis=0)

    h = lambda k: (hh[k], hl[k])
    l = lambda j, k: (lh[pair(j, k)], ll[pair(j, k)])
    return split(jnp.concatenate(solve_rows(columns, mask, h, l), axis=1))


def lead_kernel(info, place, pattern, lower, h01, h2, h3, l1, l2, l3, e0, e1, e2, e3, *refs):
    hh, hl, lh, ll, ch, cl, top, rows = refs
    for k, block in enumerate(listed([h01, h2, h3])):
        hh[k], hl[k] = split(block[...])
    for k, block in enumerate(listed([l1, l2, l3])):
        lh[k], ll[k] = split(block[...])
    across = crossing(pattern, 0, lower, hh, hl, lh, ll)
    ch[...], cl[...] = across
    for d, early in enumerate([e0, e1, e2, e3]):
        rows[place[d]] = early[...]
    height = rows.shape[1]
    solved = solve_rows(
        [rows[k, :, :NB] for k in range(K)],
        row_mask(info, info[0, 2 + K], 1, height),
        lambda k: (hh[k], hl[k]),
        lambda j, k: (lh[pair(j, k)], ll[pair(j, k)]),
    )
    update = dot3(split(jnp.concatenate(solved, axis=1)), across, NT)
    for v in range(K):
        start = NB + v % 2 * 128
        schur = rows[v // 2, :, start : start + 128] - update[:, v * 128 : v * 128 + 128]
        top[v, :, 0] = schur.reshape(height // 8, 8, 128)
        top[v, :, 1] = rows[v // 2, :, start + NB : start + NB + 128].reshape(height // 8, 8, 128)


def crossing_kernel(pattern, lower, hh, hl, lh, ll, ch, cl):
    ch[...], cl[...] = crossing(pattern, 2, lower, hh, hl, lh, ll)


def rows_kernel(info, place, front, p1, p2, p3, g01, g2, g3, hh, hl, lh, ll, ch, cl, dh, dl, *refs):
    child, b1, b2, b3, extend, fin, fout, eout, insem, outsem, extsem = refs[-11:]
    step, steps = pl.program_id(0), pl.num_programs(0)
    groups, height = fin.shape[2], fin.shape[3]
    octets = height // 8
    slot = lax.rem(step, 2)

    def load(at, slot):
        for s in range(groups):
            here = at * groups + s
            for d, source in enumerate([front.at[here, place[0]], p1.at[here], p2.at[here], p3.at[here]]):
                pltpu.make_async_copy(source, fin.at[slot, place[d], s], insem.at[slot]).start()

    def store(at, slot):
        for s in range(groups):
            here = at * groups + s
            for d, target in enumerate([child.at[here, place[0]], b1.at[here], b2.at[here], b3.at[here]]):
                pltpu.make_async_copy(fout.at[slot, place[d], s], target, outsem.at[slot]).start()

    def wait(buffer, slot, sem):
        pltpu.make_async_copy(buffer.at[slot], buffer.at[slot], sem.at[slot]).wait()

    @pl.when(step == 0)
    def _():
        load(0, 0)

    @pl.when(step + 1 < steps)
    def _():
        load(step + 1, 1 - slot)

    wait(fin, slot, insem)

    @pl.when(step >= 2)
    def _():
        wait(fout, slot, outsem)
        wait(eout, slot, extsem)

    first = step * groups
    columns = [fin[slot, k, :, :, :NB].reshape(groups * height, NB) for k in range(K)]
    solved = solve_rows(
        columns,
        row_mask(info, first, groups, height),
        lambda k: (hh[k], hl[k]),
        lambda j, k: (lh[pair(j, k)], ll[pair(j, k)]),
    )
    final = split(jnp.concatenate(solved, axis=1))
    halves = [dot3(final, (ch[...], cl[...]), NT), dot3(final, (dh[...], dl[...]), NT)]
    for k, g in enumerate(listed([g01, g2, g3])):
        fout[slot, k, :, :, :NB] = solved[k].reshape(groups, height, NB)
        schur = fin[slot, k, :, :, NB:].reshape(groups * height, NB) - halves[k // 2][:, k % 2 * NB : (k % 2 + 1) * NB]
        fout[slot, k, :, :, NB:] = schur.reshape(groups, height, NB)
        eout[slot, :, :, :, k * NB : (k + 1) * NB] = schur.reshape(groups, octets, 8, NB)
        for i in range(groups):

            @pl.when(info[first + i, 0] == k)
            def _():
                mine = pl.ds(pl.multiple_of(place[0] * height, height), height)
                fout[slot, k, i, :, :NB] = g[mine, :]

    store(step, slot)

    def send(i):
        at = info[first + i, 1 + K]
        holder = pl.multiple_of(lax.div(at, groups) * octets, octets)
        target = extend.at[pl.ds(holder, octets), lax.rem(at, groups)]
        return pltpu.make_async_copy(eout.at[slot, i], target, extsem.at[slot])

    for i in range(groups):
        send(i).start()

    @pl.when(step == steps - 1)
    def _():
        for other in range(2):
            wait(fout, other, outsem)
            wait(eout, other, extsem)


def parent_kernel(pattern, top, g, hh, hl, lh, ll, work, out):
    def block(i, j):
        halves = [
            jnp.swapaxes(top[2 * j + v, :, :, i], 0, 1).reshape(NB, 128) for v in range(2)
        ]
        return jnp.concatenate(halves, axis=1)

    g0, h0 = factor(block(0, 0), work, out)
    g[0] = g0
    h0 = split(h0)
    hh[0], hl[0] = h0
    first = []
    for i in range(1, 4):
        value = split(kept(pattern[i, 0], dot3(split(block(i, 0)), h0, NT)))
        lh[i - 1], ll[i - 1] = value
        first.append(value)
    g1, h1 = factor(block(1, 1) - dot3(first[0], first[0], NT), work, out)
    g[1] = g1
    h1 = split(h1)
    hh[1], hl[1] = h1
    for i in range(2, 4):
        rest = block(i, 1) - dot3(first[i - 1], first[0], NT)
        lh[i + 1], ll[i + 1] = split(kept(pattern[i, 1], dot3(split(rest), h1, NT)))


def parent_steps(columns, mask, hh, hl, lh, ll):
    one = mask(0, dot3(split(columns[0]), (hh[0], hl[0]), NT))
    first = split(one)
    two = mask(1, dot3(split(columns[1] - dot3(first, (lh[0], ll[0]), NT)), (hh[1], hl[1]), NT))
    second = split(two)
    results = [one, two]
    for j in range(2, 4):
        left = dot3(first, (lh[j - 1], ll[j - 1]), NT) + dot3(second, (lh[j + 1], ll[j + 1]), NT)
        results.append(columns[j] - left)
    return results


def parent_rows_kernel(info, place, target, extend, own, g, hh, hl, lh, ll, out, acc):
    slots, members = acc.shape[0], acc.shape[1]
    count = own.shape[0] // members
    for s in range(slots):
        for i in range(members):
            for j in range(count):
                acc[s, i, :, j * NB : (j + 1) * NB] = own[i * count + j, 1 + s]

    def add(q, _):
        for s in range(slots):
            where = target[q, s]

            @pl.when(where >= 0)
            def _():
                acc[s, where] += extend[q, s]

        return 0

    lax.fori_loop(0, extend.shape[0], add, 0)
    columns = [acc[:, :, :, j * NB : (j + 1) * NB].reshape(slots * members * 8, NB) for j in range(4)]
    results = parent_steps(columns, row_mask(info, 0, slots * members, 8), hh, hl, lh, ll)
    for j in range(4):
        shaped = results[j].reshape(slots, members, 8, NB)
        for s in range(slots):
            out[:, j, s] = shaped[s]
    for k in range(KP):

        @pl.when(info[k, 0] == k)
        def _():
            mine = pl.ds(pl.multiple_of(place[K] * 8, 8), 8)
            out[k, k, 0] = g[k, mine, :]


def exchange(array, axes):
    return lax.all_to_all(array, axes, split_axis=0, concat_axis=0, tiled=True)


def gather_pieces(pieces, axes, count):
    return exchange(jnp.broadcast_to(pieces[None], (count,) + pieces.shape), axes)


def shift(array, d, n):
    return lax.ppermute(array, "col", [(i, (i + d) % n) for i in range(n)])


def nought(array):
    one = array[(0,) * array.ndim]
    return (one != one).astype(jnp.int32)


def once(arrays, others):
    count = len(arrays)
    return pl.pallas_call(
        lambda *refs: None,
        out_shape=[jax.ShapeDtypeStruct(array.shape, array.dtype) for array in arrays],
        in_specs=[ANY] * (count + len(others)),
        out_specs=[ANY] * count,
        input_output_aliases={i: i for i in range(count)},
    )(*arrays, *others)


def per_device(child_front, child_pattern, block_map, parent_front, parent_pattern):
    nr, nx, nc = lax.axis_size("row"), lax.axis_size("col"), lax.axis_size("cube")
    r, x, c = lax.axis_index("row"), lax.axis_index("col"), lax.axis_index("cube")
    local = child_front.shape[1] // NB
    slots = parent_front.shape[0] // NB
    height = NB // nx
    octets = height // 8
    holders = nc * nr
    front = child_front[0]
    pattern = child_pattern[0]

    place = jnp.stack([(x - d) % nx for d in range(nx)] + [x * octets + r]).astype(jnp.int32)
    square = block_shape
    half = lambda *shape: jax.ShapeDtypeStruct(shape, bf16)

    tables = block_map.reshape(nc, local, nr).transpose(0, 2, 1)
    live = tables >= 0
    cubes = jnp.where(live, tables % holders // nr, -1)
    places = jnp.where(live, tables // holders, -1)
    members = jnp.where(live, tables % nr, -1)
    mine = tables[c, r]
    spot = jnp.where(mine >= 0, cubes[c, r] * slots + places[c, r], -1)
    spot = jnp.where(spot >= 0, spot, local * (local - 1) // 2 - jnp.sum(jnp.maximum(spot, 0)))
    lead = jnp.sum(jnp.where(spot == 0, jnp.arange(local), 0))
    block_row = jnp.arange(local) * nr + r
    kept_rows = jnp.where(
        block_row[:, None] > jnp.arange(K)[None], jnp.take(pattern, block_row, axis=0, mode="clip"), 0
    )
    row_info = jnp.concatenate(
        [block_row[:, None], kept_rows, spot[:, None], jnp.full((local, 1), lead)], axis=1
    ).astype(jnp.int32)

    quarters = front.reshape(local, nx, height, -1)
    ahead = lax.dynamic_index_in_dim(quarters, lead, axis=0, keepdims=False)
    ahead = jnp.concatenate([ahead, parent_front[:NB].reshape(nx, height, NB)], axis=2)

    parent_row = (jnp.arange(slots)[:, None] * holders + c * nr + jnp.arange(nr)[None, :]).reshape(-1)
    flags = jnp.take(parent_pattern, parent_row, axis=0, mode="clip")
    flags = jnp.where(parent_row[:, None] > jnp.arange(KP)[None], flags, 0)
    parent_info = jnp.concatenate([parent_row[:, None], flags], axis=1).astype(jnp.int32)
    here = (cubes == c)[:, :, None, :] & (places[:, :, None, :] == jnp.arange(slots)[None, None, :, None])
    target = jnp.max(jnp.where(here, members[:, :, None, :], -1), axis=-1).reshape(holders, slots)
    target = target.astype(jnp.int32)

    corner = front[:NB, :NB].reshape(nr * nx, 1, 8, NB)
    own = parent_front.reshape(slots, nx, octets, 8, NB).transpose(2, 1, 0, 3, 4).reshape(nr * nx, slots, 8, NB)
    own = exchange(jnp.concatenate([corner, own], axis=1), ("row", "col"))
    pieces = own[:, 0]
    lines = [pieces[i * nx : i * nx + i + 1] for i in range(K)] + [pieces[K * nx : 2 * K * nx]]
    lines = jnp.concatenate(lines, axis=0)
    early = [lax.dynamic_index_in_dim(ahead, (x + d) % nx, axis=0, keepdims=False) for d in range(nx)]
    sent = [lax.dynamic_index_in_dim(quarters, (x + d) % nx, axis=1, keepdims=False) for d in range(1, nx)]
    tables = [row_info, place, pattern[: 2 * K], parent_pattern[:4], parent_info, target]
    lines, row_info, place, lead_pattern, top_pattern, parent_info, target, *made = once(
        [lines, *tables, *early, *sent], []
    )
    early, sent = made[:nx], made[nx:]
    lines = jnp.stack([lines] + [shift(lines, d, nx) for d in range(1, nx)])
    lines = jnp.take(lines, (x - jnp.arange(nx)) % nx, axis=0, mode="clip")
    lines = lines.transpose(1, 0, 2, 3).reshape(-1, nx * 8, NB)
    square_sent = jnp.broadcast_to(lines[None, :10], (nr, 10) + lines.shape[1:])
    square_parts = exchange(square_sent, ("row",))
    lower = lax.all_gather(lines[10:], "row")
    early = list(once(early, [square_sent]))
    early = early[:1] + [shift(early[d], d, nx) for d in range(1, nx)]
    sent = once(sent, early[1:])
    parts = [shift(part, d + 1, nx) for d, part in enumerate(sent)]

    def panels():
        g01, h01, l1, g2, h2, l2, g3, h3, l3 = call(
            panels_kernel,
            [square(2), square(2), square(1), square(1), square(1), square(2), square(1), square(1), square(3)],
            in_specs=[SMEM, VMEM],
            out_specs=[VMEM] * 9,
            scratch_shapes=FACTOR_SCRATCH,
        )(lead_pattern, square_parts)
        return g01, g2, g3, h01, h2, h3, l1, l2, l3

    empty = jax.tree.map(lambda leaf: jnp.zeros(leaf.shape, leaf.dtype), jax.eval_shape(panels))
    g01, g2, g3, h01, h2, h3, l1, l2, l3 = lax.cond(nought(square_parts) == 0, panels, lambda: empty)

    some_lower = lambda n: pl.BlockSpec((nr, 2 * K, nx * 8, NB), lambda i, n=n: (0, n, 0, 0))
    *weights, top = call(
        lead_kernel,
        [half(K, NB, NB)] * 2
        + [half(6, NB, NB)] * 2
        + [half(2 * NB, K * NB)] * 2
        + [jax.ShapeDtypeStruct((nc, octets, 2, 8, 128), f32)],
        grid=(1,),
        in_specs=[SMEM] * 3 + [some_lower(0)] + [VMEM] * 10,
        out_specs=[VMEM] * 7,
        scratch_shapes=[pltpu.VMEM((nx, height, 3 * NB), f32)],
    )(row_info, place, lead_pattern, lower, h01, h2, h3, l1, l2, l3, *early)
    (top,) = once([top], [parts[0], parts[2]])
    weights += call(
        crossing_kernel,
        [half(2 * NB, K * NB)] * 2,
        grid=(1,),
        in_specs=[SMEM, some_lower(1)] + [VMEM] * 4,
        out_specs=[VMEM] * 2,
    )(lead_pattern, lower, *weights[:4])
    top = exchange(top.reshape(holders, 2, 8, 128), ("cube", "row"))
    top_row = jnp.max(jnp.where((cubes == 0) & (places == 0), members, -1), axis=-1).reshape(holders)
    chosen = top_row[None, :] == jnp.arange(4)[:, None]
    top = top[:4, 1] + jnp.sum(jnp.where(chosen[:, :, None, None], top[None, :, 0], 0.0), axis=1)

    (top,) = once([top], [*weights[-2:], parts[1]])
    top_sent = jnp.broadcast_to(top[None], (nc * nr * nx,) + top.shape)
    top = exchange(top_sent, ("cube", "row", "col")).reshape(nc, nr, nx, 4, 8, 128)

    full = lambda a: pl.BlockSpec(a.shape, lambda i, n=a.ndim: (0,) * n)
    buffer = pltpu.VMEM((2, nx, slots, height, 2 * NB), f32)
    wide = jax.ShapeDtypeStruct((nc * octets, slots, 8, nx * NB), f32)
    child_out, *back, extend = call(
        rows_kernel,
        [jax.ShapeDtypeStruct(quarters.shape, f32), *[jax.ShapeDtypeStruct(parts[0].shape, f32)] * 3, wide],
        grid=(local // slots,),
        in_specs=[SMEM] * 2 + [ANY] * 4 + [full(a) for a in (g01, g2, g3, *weights)] + [ANY],
        out_specs=[ANY] * 5,
        scratch_shapes=[buffer, buffer, pltpu.VMEM((2, slots, octets, 8, nx * NB), f32)]
        + [pltpu.SemaphoreType.DMA((2,))] * 3,
    )(row_info, place, quarters, *parts, g01, g2, g3, *weights, top_sent)
    def parent():
        arrived = exchange(extend, ("cube", "row"))

        g_parent, *parent_weights = call(
            parent_kernel,
            [square(2)] + [half(2, NB, NB)] * 2 + [half(5, NB, NB)] * 2,
            in_specs=[SMEM, VMEM],
            out_specs=[VMEM] * 5,
            scratch_shapes=FACTOR_SCRATCH,
        )(top_pattern, top)

        result = call(
            parent_rows_kernel,
            jax.ShapeDtypeStruct((nr, nx, slots, 8, NB), f32),
            in_specs=[SMEM] * 3 + [VMEM] * 7,
            out_specs=VMEM,
            scratch_shapes=[pltpu.VMEM((slots, nr, 8, nx * NB), f32)],
        )(
            parent_info,
            place,
            target,
            arrived,
            own,
            g_parent,
            *parent_weights,
        )
        return result

    empty = jax.tree.map(lambda leaf: jnp.zeros(leaf.shape, leaf.dtype), jax.eval_shape(parent))
    result = lax.cond(nought(top) == 0, parent, lambda: empty)

    late = x + nought(result)
    for d in range(1, nx):
        part = shift(back[d - 1], -d, nx)[:, None]
        child_out = lax.dynamic_update_slice(child_out, part, (0, (late + d) % nx, 0, 0))
    child_out = child_out.reshape(child_front.shape)
    result = exchange(result.reshape(nr * nx, slots, 8, NB), ("row", "col"))
    result = result.reshape(nr, nx, slots, 8, NB).transpose(2, 1, 0, 3, 4).reshape(parent_front.shape)
    return child_out, result


def solution(mesh):
    placed = (P("cube", "row", "col"), P("cube", None, None), P(), P(("cube", "row"), "col"), P())
    return jax.shard_map(
        per_device,
        mesh=mesh,
        in_specs=placed,
        out_specs=(P("cube", "row", "col"), P(("cube", "row"), "col")),
        check_vma=False,
    )
```

```python
import functools

import jax
import jax.numpy as jnp
from jax import lax
from jax.experimental import pallas as pl
from jax.experimental.pallas import tpu as pltpu
from jax.sharding import PartitionSpec as P

NB = 256
K = 4
KP = 2
PB = 64

f32, bf16 = jnp.float32, jnp.bfloat16


def dims(a, b):
    return (((a,), (b,)), ((), ()))


NN, NT, TN = dims(1, 0), dims(1, 1), dims(0, 0)


def split(x):
    high = x.astype(bf16)
    return high, (x - high.astype(f32)).astype(bf16)


def dot3(x, y, d):
    xh, xl = x
    yh, yl = y
    part = lambda p, q: lax.dot_general(p, q, d, preferred_element_type=f32)
    return part(xh, yh) + (part(xh, yl) + part(xl, yh))


def small_factor(t):
    count = PB // 8
    tiles = [t[8 * i : 8 * i + 8] for i in range(count)]
    full = (8, 128)
    sub = lax.broadcasted_iota(jnp.int32, full, 0)
    for s in range(count):
        c0 = PB + 8 * s
        cols = [
            [jnp.broadcast_to(tiles[q][:, c0 + k : c0 + k + 1], full) for k in range(8)]
            for q in range(s, count)
        ]
        a = [
            [jnp.broadcast_to(cols[0][k][i : i + 1], full) if i >= k else None for k in range(8)]
            for i in range(8)
        ]
        rows = [jnp.broadcast_to(tiles[s][k : k + 1], full) for k in range(8)]
        mults = [[] for _ in range(s, count)]
        scale = None
        for k in range(8):
            r = 1.0 / a[k][k]
            root = lax.rsqrt(a[k][k])
            scale = root if k == 0 else jnp.where(sub == k, root, scale)
            m = [a[i][k] * r if i > k else None for i in range(8)]
            for q in range(count - s):
                mult = cols[q][k] * r
                if q == 0:
                    mult = jnp.where(sub > k, mult, 0.0)
                mults[q].append(mult)
            for i in range(k + 1, 8):
                rows[i] = rows[i] - m[i] * rows[k]
                for q in range(count - s):
                    cols[q][i] = cols[q][i] - mults[q][k] * a[i][k]
                for j in range(k + 1, i + 1):
                    a[i][j] = a[i][j] - m[i] * a[j][k]
        for q in range(count - s):
            acc = tiles[s + q]
            for k in range(8):
                acc = acc - mults[q][k] * rows[k]
            tiles[s + q] = acc
        tiles[s] = tiles[s] * scale
    return jnp.concatenate(tiles, axis=0)


def factor(block, work, out):
    row = lax.broadcasted_iota(jnp.int32, (NB, NB), 0)
    lane = lax.broadcasted_iota(jnp.int32, (NB, NB), 1)
    low = jnp.where(row >= lane, block, 0.0)
    work[:, :NB] = low + jnp.where(row > lane, block, 0.0).T
    work[:, NB:] = jnp.where(row == lane, 1.0, 0.0)
    lane_of = lax.broadcasted_iota(jnp.int32, (PB, 128), 1)
    row_of = lax.broadcasted_iota(jnp.int32, (PB, 128), 0)
    wide_lane = lax.broadcasted_iota(jnp.int32, (PB, NB), 1)

    def body(p, _):
        base = pl.multiple_of(p * PB, PB)
        slab = work[pl.ds(base, PB), :]
        turned = pltpu.roll(slab[:, :NB], jnp.where(p == 0, PB, NB + PB - base), 1)[:, :128]
        unit = jnp.where(lane_of == row_of, 1.0, 0.0)
        t = jnp.where((lane_of >= PB) & (lane_of < 2 * PB), turned, unit)
        j = small_factor(t)[:, :PB]
        u = dot3(split(j), split(slab), NN)
        out[pl.ds(base, PB), :] = u
        uh, ul = split(u)
        keep = wide_lane >= base + PB
        zero = jnp.zeros((PB, NB), bf16)
        left = (jnp.where(keep, uh[:, :NB], zero), jnp.where(keep, ul[:, :NB], zero))
        work[...] -= dot3(left, (uh, ul), TN)
        return 0

    lax.fori_loop(0, NB // PB, body, 0)
    g = jnp.where(lane >= row, out[:, :NB], 0.0).T
    return g, out[:, NB:]


FACTOR_SCRATCH = [pltpu.VMEM((NB, 2 * NB), f32), pltpu.VMEM((NB, 2 * NB), f32)]


def kept(flag, value):
    return jnp.where(flag != 0, value, 0.0)


def call(kernel, out_shape, **kwargs):
    kwargs.setdefault("compiler_params", pltpu.CompilerParams(vmem_limit_bytes=56 << 20))
    return pl.pallas_call(
        kernel,
        out_shape=out_shape,
        cost_estimate=pl.CostEstimate(flops=1, bytes_accessed=1, transcendentals=0),
        **kwargs,
    )


VMEM = pl.BlockSpec(memory_space=pltpu.VMEM)
SMEM = pl.BlockSpec(memory_space=pltpu.SMEM)
ANY = pl.BlockSpec(memory_space=pl.ANY)


def block_shape(*lead):
    return jax.ShapeDtypeStruct(lead + (NB, NB), f32)


def whole(ref, index):
    return ref[:, index].reshape(NB, NB)


def pair(i, j):
    return i * (i - 1) // 2 + j


def first_kernel(pattern, piece, g, h, l, work, out):
    g0, h0 = factor(whole(piece, 0), work, out)
    g[0], h[0] = g0, h0
    l10 = kept(pattern[1, 0], dot3(split(whole(piece, 1)), split(h0), NT))
    l[0] = l10
    s10 = split(l10)
    g[1], h[1] = factor(whole(piece, 2) - dot3(s10, s10, NT), work, out)


def later_kernel(k, first, pattern, piece, *refs):
    count = k - 1
    h_refs, l_refs = refs[:count], refs[count : 2 * count]
    g, h, l, work, out = refs[2 * count :]
    hs, ls = listed(h_refs), listed(l_refs)
    row = [whole(piece, first + j) for j in range(k + 1)]
    for j in range(k):
        l[j] = kept(pattern[k, j], dot3(split(row[j]), split(hs[j][...]), NT))
        value = split(l[j])
        for i in range(j + 1, k):
            row[i] = row[i] - dot3(value, split(ls[pair(i, j)][...]), NT)
        row[k] = row[k] - dot3(value, value, NT)
    g[0], h[0] = factor(row[k], work, out)


def listed(refs):
    return [ref.at[i] for ref in refs for i in range(ref.shape[0])]


def solve_rows(columns, mask, h, l):
    solved = []
    columns = list(columns)
    for k in range(len(columns)):
        value = mask(k, dot3(split(columns[k]), h(k), NT))
        solved.append(value)
        value = split(value)
        for j in range(k + 1, len(columns)):
            columns[j] = columns[j] - dot3(value, l(j, k), NT)
    return solved


def row_mask(info, first, groups, height):
    def mask(k, value):
        parts = [
            kept(info[first + i, 1 + k], value[i * height : (i + 1) * height]) for i in range(groups)
        ]
        return jnp.concatenate(parts, axis=0) if groups > 1 else parts[0]

    return mask


def panels_kernel(pattern, piece, g01, h01, l1, g2, h2, l2, g3, h3, l3, work, out):
    first_kernel(pattern, piece, g01, h01, l1, work, out)
    later_kernel(2, 3, pattern, piece, h01, l1, g2, h2, l2, work, out)
    later_kernel(3, 6, pattern, piece, h01, h2, l1, l2, g3, h3, l3, work, out)


def crossing(pattern, first, lower, hh, hl, lh, ll):
    columns = [jnp.concatenate([whole(lower, j * K + k) for j in range(2)], axis=0) for k in range(K)]

    def mask(k, value):
        parts = [kept(pattern[K + first + j, k], value[j * NB : (j + 1) * NB]) for j in range(2)]
        return jnp.concatenate(parts, axis=0)

    h = lambda k: (hh[k], hl[k])
    l = lambda j, k: (lh[pair(j, k)], ll[pair(j, k)])
    return split(jnp.concatenate(solve_rows(columns, mask, h, l), axis=1))


def lead_kernel(info, place, pattern, lower, h01, h2, h3, l1, l2, l3, e0, e1, e2, e3, *refs):
    hh, hl, lh, ll, ch, cl, top, rows = refs
    for k, block in enumerate(listed([h01, h2, h3])):
        hh[k], hl[k] = split(block[...])
    for k, block in enumerate(listed([l1, l2, l3])):
        lh[k], ll[k] = split(block[...])
    across = crossing(pattern, 0, lower, hh, hl, lh, ll)
    ch[...], cl[...] = across
    for d, early in enumerate([e0, e1, e2, e3]):
        rows[place[d]] = early[...]
    height = rows.shape[1]
    solved = solve_rows(
        [rows[k, :, :NB] for k in range(K)],
        row_mask(info, info[0, 2 + K], 1, height),
        lambda k: (hh[k], hl[k]),
        lambda j, k: (lh[pair(j, k)], ll[pair(j, k)]),
    )
    update = dot3(split(jnp.concatenate(solved, axis=1)), across, NT)
    for v in range(K):
        start = NB + v % 2 * 128
        schur = rows[v // 2, :, start : start + 128] - update[:, v * 128 : v * 128 + 128]
        top[v, :, 0] = schur.reshape(height // 8, 8, 128)
        top[v, :, 1] = rows[v // 2, :, start + NB : start + NB + 128].reshape(height // 8, 8, 128)


def crossing_kernel(pattern, lower, hh, hl, lh, ll, ch, cl):
    ch[...], cl[...] = crossing(pattern, 2, lower, hh, hl, lh, ll)


def rows_kernel(info, place, front, p1, p2, p3, g01, g2, g3, hh, hl, lh, ll, ch, cl, dh, dl, *refs):
    child, b1, b2, b3, extend, fin, fout, eout, insem, outsem, extsem = refs[-11:]
    step, steps = pl.program_id(0), pl.num_programs(0)
    groups, height = fin.shape[2], fin.shape[3]
    octets = height // 8
    slot = lax.rem(step, 2)

    def load(at, slot):
        for s in range(groups):
            here = at * groups + s
            for d, source in enumerate([front.at[here, place[0]], p1.at[here], p2.at[here], p3.at[here]]):
                pltpu.make_async_copy(source, fin.at[slot, place[d], s], insem.at[slot]).start()

    def store(at, slot):
        for s in range(groups):
            here = at * groups + s
            for d, target in enumerate([child.at[here, place[0]], b1.at[here], b2.at[here], b3.at[here]]):
                pltpu.make_async_copy(fout.at[slot, place[d], s], target, outsem.at[slot]).start()

    def wait(buffer, slot, sem):
        pltpu.make_async_copy(buffer.at[slot], buffer.at[slot], sem.at[slot]).wait()

    @pl.when(step == 0)
    def _():
        load(0, 0)

    @pl.when(step + 1 < steps)
    def _():
        load(step + 1, 1 - slot)

    wait(fin, slot, insem)

    @pl.when(step >= 2)
    def _():
        wait(fout, slot, outsem)
        wait(eout, slot, extsem)

    first = step * groups
    columns = [fin[slot, k, :, :, :NB].reshape(groups * height, NB) for k in range(K)]
    solved = solve_rows(
        columns,
        row_mask(info, first, groups, height),
        lambda k: (hh[k], hl[k]),
        lambda j, k: (lh[pair(j, k)], ll[pair(j, k)]),
    )
    final = split(jnp.concatenate(solved, axis=1))
    halves = [dot3(final, (ch[...], cl[...]), NT), dot3(final, (dh[...], dl[...]), NT)]
    for k, g in enumerate(listed([g01, g2, g3])):
        fout[slot, k, :, :, :NB] = solved[k].reshape(groups, height, NB)
        schur = fin[slot, k, :, :, NB:].reshape(groups * height, NB) - halves[k // 2][:, k % 2 * NB : (k % 2 + 1) * NB]
        fout[slot, k, :, :, NB:] = schur.reshape(groups, height, NB)
        eout[slot, :, :, :, k * NB : (k + 1) * NB] = schur.reshape(groups, octets, 8, NB)
        for i in range(groups):

            @pl.when(info[first + i, 0] == k)
            def _():
                mine = pl.ds(pl.multiple_of(place[0] * height, height), height)
                fout[slot, k, i, :, :NB] = g[mine, :]

    store(step, slot)

    def send(i):
        at = info[first + i, 1 + K]
        holder = pl.multiple_of(lax.div(at, groups) * octets, octets)
        target = extend.at[pl.ds(holder, octets), lax.rem(at, groups)]
        return pltpu.make_async_copy(eout.at[slot, i], target, extsem.at[slot])

    for i in range(groups):
        send(i).start()

    @pl.when(step == steps - 1)
    def _():
        for other in range(2):
            wait(fout, other, outsem)
            wait(eout, other, extsem)


def parent_kernel(pattern, top, g, hh, hl, lh, ll, work, out):
    def block(i, j):
        halves = [
            jnp.swapaxes(top[2 * j + v, :, :, i], 0, 1).reshape(NB, 128) for v in range(2)
        ]
        return jnp.concatenate(halves, axis=1)

    g0, h0 = factor(block(0, 0), work, out)
    g[0] = g0
    h0 = split(h0)
    hh[0], hl[0] = h0
    first = []
    for i in range(1, 4):
        value = split(kept(pattern[i, 0], dot3(split(block(i, 0)), h0, NT)))
        lh[i - 1], ll[i - 1] = value
        first.append(value)
    g1, h1 = factor(block(1, 1) - dot3(first[0], first[0], NT), work, out)
    g[1] = g1
    h1 = split(h1)
    hh[1], hl[1] = h1
    for i in range(2, 4):
        rest = block(i, 1) - dot3(first[i - 1], first[0], NT)
        lh[i + 1], ll[i + 1] = split(kept(pattern[i, 1], dot3(split(rest), h1, NT)))


def parent_steps(columns, mask, hh, hl, lh, ll):
    one = mask(0, dot3(split(columns[0]), (hh[0], hl[0]), NT))
    first = split(one)
    two = mask(1, dot3(split(columns[1] - dot3(first, (lh[0], ll[0]), NT)), (hh[1], hl[1]), NT))
    second = split(two)
    results = [one, two]
    for j in range(2, 4):
        left = dot3(first, (lh[j - 1], ll[j - 1]), NT) + dot3(second, (lh[j + 1], ll[j + 1]), NT)
        results.append(columns[j] - left)
    return results


def parent_rows_kernel(info, place, target, extend, own, g, hh, hl, lh, ll, out, acc):
    slots, members = acc.shape[0], acc.shape[1]
    count = own.shape[0] // members
    for s in range(slots):
        for i in range(members):
            for j in range(count):
                acc[s, i, :, j * NB : (j + 1) * NB] = own[i * count + j, 1 + s]

    def add(q, _):
        for s in range(slots):
            where = target[q, s]

            @pl.when(where >= 0)
            def _():
                acc[s, where] += extend[q, s]

        return 0

    lax.fori_loop(0, extend.shape[0], add, 0)
    columns = [acc[:, :, :, j * NB : (j + 1) * NB].reshape(slots * members * 8, NB) for j in range(4)]
    results = parent_steps(columns, row_mask(info, 0, slots * members, 8), hh, hl, lh, ll)
    for j in range(4):
        shaped = results[j].reshape(slots, members, 8, NB)
        for s in range(slots):
            out[:, j, s] = shaped[s]
    for k in range(KP):

        @pl.when(info[k, 0] == k)
        def _():
            mine = pl.ds(pl.multiple_of(place[K] * 8, 8), 8)
            out[k, k, 0] = g[k, mine, :]


def exchange(array, axes):
    return lax.all_to_all(array, axes, split_axis=0, concat_axis=0, tiled=True)


def gather_pieces(pieces, axes, count):
    return exchange(jnp.broadcast_to(pieces[None], (count,) + pieces.shape), axes)


def shift(array, d, n):
    return lax.ppermute(array, "col", [(i, (i + d) % n) for i in range(n)])


def nought(array):
    one = array[(0,) * array.ndim]
    return (one != one).astype(jnp.int32)


def once(arrays, others):
    count = len(arrays)
    return pl.pallas_call(
        lambda *refs: None,
        out_shape=[jax.ShapeDtypeStruct(array.shape, array.dtype) for array in arrays],
        in_specs=[ANY] * (count + len(others)),
        out_specs=[ANY] * count,
        input_output_aliases={i: i for i in range(count)},
    )(*arrays, *others)


def per_device(child_front, child_pattern, block_map, parent_front, parent_pattern):
    nr, nx, nc = lax.axis_size("row"), lax.axis_size("col"), lax.axis_size("cube")
    r, x, c = lax.axis_index("row"), lax.axis_index("col"), lax.axis_index("cube")
    local = child_front.shape[1] // NB
    slots = parent_front.shape[0] // NB
    height = NB // nx
    octets = height // 8
    holders = nc * nr
    front = child_front[0]
    pattern = child_pattern[0]

    place = jnp.stack([(x - d) % nx for d in range(nx)] + [x * octets + r]).astype(jnp.int32)
    square = block_shape
    half = lambda *shape: jax.ShapeDtypeStruct(shape, bf16)

    tables = block_map.reshape(nc, local, nr).transpose(0, 2, 1)
    live = tables >= 0
    cubes = jnp.where(live, tables % holders // nr, -1)
    places = jnp.where(live, tables // holders, -1)
    members = jnp.where(live, tables % nr, -1)
    mine = tables[c, r]
    spot = jnp.where(mine >= 0, cubes[c, r] * slots + places[c, r], -1)
    spot = jnp.where(spot >= 0, spot, local * (local - 1) // 2 - jnp.sum(jnp.maximum(spot, 0)))
    lead = jnp.sum(jnp.where(spot == 0, jnp.arange(local), 0))
    block_row = jnp.arange(local) * nr + r
    kept_rows = jnp.where(
        block_row[:, None] > jnp.arange(K)[None], jnp.take(pattern, block_row, axis=0, mode="clip"), 0
    )
    row_info = jnp.concatenate(
        [block_row[:, None], kept_rows, spot[:, None], jnp.full((local, 1), lead)], axis=1
    ).astype(jnp.int32)

    quarters = front.reshape(local, nx, height, -1)
    ahead = lax.dynamic_index_in_dim(quarters, lead, axis=0, keepdims=False)
    ahead = jnp.concatenate([ahead, parent_front[:NB].reshape(nx, height, NB)], axis=2)

    parent_row = (jnp.arange(slots)[:, None] * holders + c * nr + jnp.arange(nr)[None, :]).reshape(-1)
    flags = jnp.take(parent_pattern, parent_row, axis=0, mode="clip")
    flags = jnp.where(parent_row[:, None] > jnp.arange(KP)[None], flags, 0)
    parent_info = jnp.concatenate([parent_row[:, None], flags], axis=1).astype(jnp.int32)
    here = (cubes == c)[:, :, None, :] & (places[:, :, None, :] == jnp.arange(slots)[None, None, :, None])
    target = jnp.max(jnp.where(here, members[:, :, None, :], -1), axis=-1).reshape(holders, slots)
    target = target.astype(jnp.int32)

    corner = front[:NB, :NB].reshape(nr * nx, 1, 8, NB)
    own = parent_front.reshape(slots, nx, octets, 8, NB).transpose(2, 1, 0, 3, 4).reshape(nr * nx, slots, 8, NB)
    own = exchange(jnp.concatenate([corner, own], axis=1), ("row", "col"))
    pieces = own[:, 0]
    lines = [pieces[i * nx : i * nx + i + 1] for i in range(K)] + [pieces[K * nx : 2 * K * nx]]
    lines = jnp.concatenate(lines, axis=0)
    early = [lax.dynamic_index_in_dim(ahead, (x + d) % nx, axis=0, keepdims=False) for d in range(nx)]
    sent = [lax.dynamic_index_in_dim(quarters, (x + d) % nx, axis=1, keepdims=False) for d in range(1, nx)]
    tables = [row_info, place, pattern[: 2 * K], parent_pattern[:4], parent_info, target]
    lines, row_info, place, lead_pattern, top_pattern, parent_info, target, *made = once(
        [lines, *tables, *early, *sent], []
    )
    early, sent = made[:nx], made[nx:]
    lines = jnp.stack([lines] + [shift(lines, d, nx) for d in range(1, nx)])
    lines = jnp.take(lines, (x - jnp.arange(nx)) % nx, axis=0, mode="clip")
    lines = lines.transpose(1, 0, 2, 3).reshape(-1, nx * 8, NB)
    square_sent = jnp.broadcast_to(lines[None, :10], (nr, 10) + lines.shape[1:])
    square_parts = exchange(square_sent, ("row",))
    lower = lax.all_gather(lines[10:], "row")
    early = list(once(early, [square_sent]))
    early = early[:1] + [shift(early[d], d, nx) for d in range(1, nx)]
    sent = once(sent, early[1:])
    parts = [shift(part, d + 1, nx) for d, part in enumerate(sent)]

    def panels():
        g01, h01, l1, g2, h2, l2, g3, h3, l3 = call(
            panels_kernel,
            [square(2), square(2), square(1), square(1), square(1), square(2), square(1), square(1), square(3)],
            in_specs=[SMEM, VMEM],
            out_specs=[VMEM] * 9,
            scratch_shapes=FACTOR_SCRATCH,
        )(lead_pattern, square_parts)
        return g01, g2, g3, h01, h2, h3, l1, l2, l3

    empty = jax.tree.map(lambda leaf: jnp.zeros(leaf.shape, leaf.dtype), jax.eval_shape(panels))
    g01, g2, g3, h01, h2, h3, l1, l2, l3 = lax.cond(nought(square_parts) == 0, panels, lambda: empty)

    some_lower = lambda n: pl.BlockSpec((nr, 2 * K, nx * 8, NB), lambda i, n=n: (0, n, 0, 0))
    *weights, top = call(
        lead_kernel,
        [half(K, NB, NB)] * 2
        + [half(6, NB, NB)] * 2
        + [half(2 * NB, K * NB)] * 2
        + [jax.ShapeDtypeStruct((nc, octets, 2, 8, 128), f32)],
        grid=(1,),
        in_specs=[SMEM] * 3 + [some_lower(0)] + [VMEM] * 10,
        out_specs=[VMEM] * 7,
        scratch_shapes=[pltpu.VMEM((nx, height, 3 * NB), f32)],
    )(row_info, place, lead_pattern, lower, h01, h2, h3, l1, l2, l3, *early)
    weights += call(
        crossing_kernel,
        [half(2 * NB, K * NB)] * 2,
        grid=(1,),
        in_specs=[SMEM, some_lower(1)] + [VMEM] * 4,
        out_specs=[VMEM] * 2,
    )(lead_pattern, lower, *weights[:4])
    top = exchange(top.reshape(holders, 2, 8, 128), ("cube", "row"))
    top_row = jnp.max(jnp.where((cubes == 0) & (places == 0), members, -1), axis=-1).reshape(holders)
    chosen = top_row[None, :] == jnp.arange(4)[:, None]
    top = top[:4, 1] + jnp.sum(jnp.where(chosen[:, :, None, None], top[None, :, 0], 0.0), axis=1)

    (top,) = once([top], [*weights[-2:], *parts])
    top_sent = jnp.broadcast_to(top[None], (nc * nr * nx,) + top.shape)
    top = exchange(top_sent, ("cube", "row", "col")).reshape(nc, nr, nx, 4, 8, 128)

    full = lambda a: pl.BlockSpec(a.shape, lambda i, n=a.ndim: (0,) * n)
    buffer = pltpu.VMEM((2, nx, slots, height, 2 * NB), f32)
    wide = jax.ShapeDtypeStruct((nc * octets, slots, 8, nx * NB), f32)
    child_out, *back, extend = call(
        rows_kernel,
        [jax.ShapeDtypeStruct(quarters.shape, f32), *[jax.ShapeDtypeStruct(parts[0].shape, f32)] * 3, wide],
        grid=(local // slots,),
        in_specs=[SMEM] * 2 + [ANY] * 4 + [full(a) for a in (g01, g2, g3, *weights)] + [ANY],
        out_specs=[ANY] * 5,
        scratch_shapes=[buffer, buffer, pltpu.VMEM((2, slots, octets, 8, nx * NB), f32)]
        + [pltpu.SemaphoreType.DMA((2,))] * 3,
    )(row_info, place, quarters, *parts, g01, g2, g3, *weights, top_sent)
    def parent():
        arrived = exchange(extend, ("cube", "row"))

        g_parent, *parent_weights = call(
            parent_kernel,
            [square(2)] + [half(2, NB, NB)] * 2 + [half(5, NB, NB)] * 2,
            in_specs=[SMEM, VMEM],
            out_specs=[VMEM] * 5,
            scratch_shapes=FACTOR_SCRATCH,
        )(top_pattern, top)

        result = call(
            parent_rows_kernel,
            jax.ShapeDtypeStruct((nr, nx, slots, 8, NB), f32),
            in_specs=[SMEM] * 3 + [VMEM] * 7,
            out_specs=VMEM,
            scratch_shapes=[pltpu.VMEM((slots, nr, 8, nx * NB), f32)],
        )(
            parent_info,
            place,
            target,
            arrived,
            own,
            g_parent,
            *parent_weights,
        )
        return result

    empty = jax.tree.map(lambda leaf: jnp.zeros(leaf.shape, leaf.dtype), jax.eval_shape(parent))
    result = lax.cond(nought(top) == 0, parent, lambda: empty)

    late = x + nought(result)
    for d in range(1, nx):
        part = shift(back[d - 1], -d, nx)[:, None]
        child_out = lax.dynamic_update_slice(child_out, part, (0, (late + d) % nx, 0, 0))
    child_out = child_out.reshape(child_front.shape)
    result = exchange(result.reshape(nr * nx, slots, 8, NB), ("row", "col"))
    result = result.reshape(nr, nx, slots, 8, NB).transpose(2, 1, 0, 3, 4).reshape(parent_front.shape)
    return child_out, result


def solution(mesh):
    placed = (P("cube", "row", "col"), P("cube", None, None), P(), P(("cube", "row"), "col"), P())
    return jax.shard_map(
        per_device,
        mesh=mesh,
        in_specs=placed,
        out_specs=(P("cube", "row", "col"), P(("cube", "row"), "col")),
        check_vma=False,
    )
```
